32 devices in a mesh: dp: 8 (over z, y), tensor: 4 (over x, core).
Axes of the slice: x: 2, y: 2, z: 4, core: 2. Of those that a mesh axis runs over, the one named last changes fastest.
Arguments:
- block_input: bfloat16 [8192, 1024], P('dp'), may hold values from -6 to 6
- output_grad: bfloat16 [8192, 1024], P('dp'), may hold values from -6 to 6
- seq_lengths: int32 [4], replicated, may hold values from 1024 to 4096, as said below
- ln1_gain: float32 [1024], replicated, may hold values from 0.5 to 1.5
- ln1_bias: float32 [1024], replicated, may hold values from -3 to 3
- w_qkv: bfloat16 [3, 1024, 1024], P(None, None, 'tensor'), may hold values from -2 to 2
- b_qv: float32 [2, 1024], P(None, 'tensor'), may hold values from -3 to 3
- w_out: bfloat16 [1024, 1024], P('tensor'), may hold values from -4 to 4
- b_out: float32 [1024], replicated, may hold values from -3 to 3
- ln2_gain: float32 [1024], replicated, may hold values from 0.5 to 1.5
- ln2_bias: float32 [1024], replicated, may hold values from -3 to 3
- w_fc: bfloat16 [1024, 4096], P(None, 'tensor'), may hold values from -0.1875 to 0.1875
- b_fc: float32 [4096], P('tensor'), may hold values from -3 to 3
- w_proj: bfloat16 [4096, 1024], P('tensor'), may hold values from -0.09375 to 0.09375
- b_proj: float32 [1024], replicated, may hold values from -3 to 3
Outputs:
- block_output: bfloat16 [8192, 1024], P('dp')
- input_grad: bfloat16 [8192, 1024], P('dp')
- grad_ln1_gain: float32 [1024], replicated
- grad_ln1_bias: float32 [1024], replicated
- grad_w_qkv: float32 [3, 1024, 1024], P(None, None, 'tensor')
- grad_b_qv: float32 [2, 1024], P(None, 'tensor')
- grad_w_out: float32 [1024, 1024], P('tensor')
- grad_b_out: float32 [1024], replicated
- grad_ln2_gain: float32 [1024], replicated
- grad_ln2_bias: float32 [1024], replicated
- grad_w_fc: float32 [1024, 4096], P(None, 'tensor')
- grad_b_fc: float32 [4096], P('tensor')
- grad_w_proj: float32 [4096, 1024], P('tensor')
- grad_b_proj: float32 [1024], replicated
The draws below stay inside these ranges and needn't reach their ends.
Inputs may be any that keep to these rules, and one draw needn't show every extreme that they name: `seq_lengths`: the 4 sequences lie one after another and fill all 8192 tokens; each has 1024 to 4096 tokens and one has exactly 4096.
All inputs are finite; a program needn't handle non-finite values.
Results may differ from the reference program's by a relative error of at most 0.012.
Values may be sent and summed in bfloat16 or wider, within the bound.
No kernel may reach another device: no remote copies, remote signals or barrier semaphores. Data moves between devices by JAX's collectives and lax.ppermute only.
A program may use at most 256 MiB of HBM per device.

```python
import math
import jax
import jax.numpy as jnp
from jax import lax

D = 1024
HEADS = 16
HEAD_DIM = 64
FF = 4096
MAXLEN = 4096
MINLEN = 1024
QBLOCK = 512
WINDOW = 4608
TOKENS = 8192
SEQS = 4


def draw_block_input(key, part):
    drawn = jnp.clip(jax.random.normal(key, (TOKENS, D), jnp.float32), -6.0, 6.0)
    return drawn.astype(jnp.bfloat16)


def draw_w_qkv(key, part):
    drawn = jnp.clip(jax.random.normal(key, (3, D, D), jnp.float32), -6.0, 6.0)
    return (drawn * (1.0 / math.sqrt(D))).astype(jnp.bfloat16)


def draw_seq_lengths(key, part):
    free_count = SEQS - 1
    key_list = jax.random.split(key, SEQS + 1)

    def pick_length(remain, pair):
        position, subkey = pair
        still_left = free_count - 1 - position
        lowest = jnp.maximum(MINLEN, remain - still_left * MAXLEN)
        highest = jnp.minimum(MAXLEN, remain - still_left * MINLEN)
        picked = jax.random.randint(subkey, (), lowest, highest + 1)
        return (remain - picked, picked)
    remain_end, free_lengths = lax.scan(pick_length, jnp.int32(TOKENS - MAXLEN), (jnp.arange(free_count, dtype=jnp.int32), key_list[:free_count]))
    long_slot = jax.random.randint(key_list[SEQS], (), 0, SEQS)
    slot_ids = jnp.arange(SEQS, dtype=jnp.int32)
    source = jnp.clip(jnp.where(slot_ids < long_slot, slot_ids, slot_ids - 1), 0, free_count - 1)
    return jnp.where(slot_ids == long_slot, MAXLEN, free_lengths[source]).astype(jnp.int32)


def block_levels(rng, shape, shards, smallest, high):
    def one(dim, shards_of):
        draws = jax.random.uniform(jax.random.fold_in(jax.random.fold_in(rng, 6), dim), (shards_of,), jnp.float32, smallest / len(shards), high / len(shards))
        return jnp.repeat(jnp.exp(draws), shape[dim] // shards_of).reshape((-1,) + (1,) * (len(shape) - dim - 1))

    gain = one(*shards[0])
    for cut in shards[1:]:
        gain = gain * one(*cut)
    return gain


def normal_values(own_key, shape, scale, reach, pieces=(), held_as=jnp.bfloat16):
    array = jax.random.normal(own_key, shape, jnp.float32) * scale
    if len(pieces) > 0:
        array = block_levels(own_key, shape, pieces, -0.22, 0.18) * array
    return jnp.clip(array, min=-reach, max=reach).astype(held_as)


def setup_inputs(seed: int = 0) -> dict:
    keys = jax.random.split(jax.random.key(seed), 16)
    return {
        "block_input": draw_block_input(jax.random.fold_in(keys[15], 71), 0),
        "output_grad": normal_values(keys[1], (TOKENS, D), 1.0, 6.0, ((0, 8),)),
        "seq_lengths": draw_seq_lengths(jax.random.fold_in(keys[15], 71), 0),
        "ln1_gain": jnp.clip(1.0 + 0.1 * jax.random.normal(keys[3], (D,), jnp.float32), 0.5, 1.5),
        "ln1_bias": normal_values(keys[4], (D,), 0.5, 3.0, (), jnp.float32),
        "w_qkv": draw_w_qkv(jax.random.fold_in(keys[15], 71), 0),
        "b_qv": normal_values(keys[6], (2, D), 0.5, 3.0, ((1, 4),), jnp.float32),
        "w_out": normal_values(keys[7], (D, D), 2 ** -0.5, 4.0, ((0, 4),)),
        "b_out": normal_values(keys[8], (D,), 0.5, 3.0, (), jnp.float32),
        "ln2_gain": jnp.clip(1.0 + 0.1 * jax.random.normal(keys[9], (D,), jnp.float32), 0.5, 1.5),
        "ln2_bias": normal_values(keys[10], (D,), 0.5, 3.0, (), jnp.float32),
        "w_fc": normal_values(keys[11], (D, FF), D ** -0.5, 0.1875, ((1, 4),)),
        "b_fc": normal_values(keys[12], (FF,), 0.5, 3.0, ((0, 4),), jnp.float32),
        "w_proj": normal_values(keys[13], (FF, D), FF ** -0.5, 0.09375, ((0, 4),)),
        "b_proj": normal_values(keys[14], (D,), 0.5, 3.0, (), jnp.float32),
    }


@jax.custom_vjp
def low(v):
    return lax.optimization_barrier(v.astype(jnp.bfloat16)).astype(jnp.float32)

@jax.custom_vjp
def low_back(v):
    return v

def low_keep(v):
    return (low(v), None)

def low_pass(kept, grad):
    return (grad,)

def back_keep(v):
    return (v, None)

def back_low(kept, grad):
    return (low(grad),)
low.defvjp(low_keep, low_pass)
low_back.defvjp(back_keep, back_low)

def norm_rows(values, weight_row, shift_row):
    centred = values - lax.optimization_barrier(jnp.mean(values, axis=-1, keepdims=True))
    spread = lax.optimization_barrier(jnp.mean(centred * centred, axis=-1, keepdims=True))
    return centred * lax.rsqrt(spread + 1e-05) * weight_row + shift_row

def reference(block_input, output_grad, seq_lengths, ln1_gain, ln1_bias, w_qkv, b_qv, w_out, b_out, ln2_gain, ln2_bias, w_fc, b_fc, w_proj, b_proj):
    highest = lax.Precision.HIGHEST
    seq_ends = jnp.cumsum(seq_lengths).astype(jnp.int32)
    positions = jnp.arange(TOKENS, dtype=jnp.int32)
    segment = lax.optimization_barrier(jnp.sum((positions[:, None] >= seq_ends[None, :]).astype(jnp.int32), axis=1))
    key_place = jnp.arange(TOKENS + MAXLEN, dtype=jnp.int32) - MAXLEN
    key_group = jnp.concatenate([jnp.full((MAXLEN,), -1, jnp.int32), segment])

    def attention(queries, key_rows, value_rows):
        query3 = queries.reshape(TOKENS, HEADS, HEAD_DIM)
        front = jnp.zeros((MAXLEN, HEADS, HEAD_DIM), jnp.float32)
        keys3 = jnp.concatenate([front, key_rows.reshape(TOKENS, HEADS, HEAD_DIM)], 0)
        values3 = jnp.concatenate([front, value_rows.reshape(TOKENS, HEADS, HEAD_DIM)], 0)

        def one_block(block_id):
            query_start = (block_id * QBLOCK).astype(jnp.int32)
            query_block = lax.dynamic_slice_in_dim(query3, query_start, QBLOCK, 0)
            key_window = lax.dynamic_slice_in_dim(keys3, query_start, WINDOW, 0)
            value_window = lax.dynamic_slice_in_dim(values3, query_start, WINDOW, 0)
            query_place = lax.dynamic_slice_in_dim(positions, query_start, QBLOCK, 0)
            query_group = lax.dynamic_slice_in_dim(segment, query_start, QBLOCK, 0)
            window_place = lax.dynamic_slice_in_dim(key_place, query_start, WINDOW, 0)
            window_group = lax.dynamic_slice_in_dim(key_group, query_start, WINDOW, 0)
            allowed = (window_group[None, :] == query_group[:, None]) & (window_place[None, :] <= query_place[:, None]) & (window_place[None, :] >= 0)
            scores = low_back(jnp.einsum('qhd,khd->hqk', query_block, key_window, precision=highest) * 0.125)
            scores = jnp.where(allowed[None], scores, -1e+30)
            highest_score = lax.optimization_barrier(jnp.max(scores, axis=-1, keepdims=True))
            exp_scores = jnp.exp(scores - highest_score)
            probs = low(exp_scores / lax.optimization_barrier(jnp.sum(exp_scores, axis=-1, keepdims=True)))
            return jnp.einsum('hqk,khd->qhd', probs, value_window, precision=highest)
        mixed = lax.map(jax.checkpoint(one_block), jnp.arange(TOKENS // QBLOCK, dtype=jnp.int32))
        return mixed.reshape(TOKENS, D)

    def forward(x_float, gain_one, shift_one, qkv_w, qv_bias, out_w, out_bias, gain_two, shift_two, fc_w, fc_bias, proj_w, proj_bias):
        first_norm = low(norm_rows(x_float, gain_one, shift_one))
        queries = jnp.dot(first_norm, qkv_w[0], precision=highest) + qv_bias[0]
        key_rows = jnp.dot(first_norm, qkv_w[1], precision=highest)
        value_rows = jnp.dot(first_norm, qkv_w[2], precision=highest) + qv_bias[1]
        queries = low(low_back(queries))
        key_rows = low(low_back(key_rows))
        value_rows = low(low_back(value_rows))
        heads_out = low(low_back(attention(queries, key_rows, value_rows)))
        branch = low_back(jnp.dot(heads_out, out_w, precision=highest) + out_bias)
        middle = x_float + branch
        second_norm = low(norm_rows(middle, gain_two, shift_two))
        hidden = low_back(jnp.dot(second_norm, fc_w, precision=highest) + fc_bias)
        active = low(jax.nn.gelu(hidden, approximate=True))
        feed = low_back(jnp.dot(active, proj_w, precision=highest) + proj_bias)
        return middle + feed
    floats = (block_input.astype(jnp.float32), ln1_gain.astype(jnp.float32), ln1_bias.astype(jnp.float32), w_qkv.astype(jnp.float32), b_qv.astype(jnp.float32), w_out.astype(jnp.float32), b_out.astype(jnp.float32), ln2_gain.astype(jnp.float32), ln2_bias.astype(jnp.float32), w_fc.astype(jnp.float32), b_fc.astype(jnp.float32), w_proj.astype(jnp.float32), b_proj.astype(jnp.float32))
    result, backward = jax.vjp(forward, *floats)
    grads = backward(output_grad.astype(jnp.float32))
    return (result.astype(jnp.bfloat16), grads[0].astype(jnp.bfloat16), grads[1], grads[2], grads[3], grads[4], grads[5], grads[6], grads[7], grads[8], grads[9], grads[10], grads[11], grads[12])
```

```python
import functools

import jax
import jax.numpy as jnp
from jax import lax
from jax.experimental import pallas as pl
from jax.experimental.pallas import tpu as pltpu
from jax.sharding import PartitionSpec as P

HEAD_DIM = 64
NEG = -1e30
TN = (((0,), (0,)), ((), ()))
NN = (((1,), (0,)), ((), ()))
NT = (((1,), (1,)), ((), ()))
LOW = jnp.bfloat16
F32 = jnp.float32


def dotf(a,b,dims): return lax.dot_general(a,b,dims,preferred_element_type=jnp.float32)

def seq_start(place, ends):
    start = jnp.zeros_like(place)
    for e in ends: start = jnp.where(place >= e, e, start)
    return start

def read_ends(seq_ref):
    ends=[]; total=jnp.int32(0)
    for s in range(seq_ref.shape[0]-1):
        total=total+seq_ref[s]; ends.append(total)
    return ends

def key_spot(kstart, meta_ref, J,S,T):
    b=kstart//T
    gg=lax.rem(b,S); kj=b//S
    e=lax.rem(meta_ref[1]-gg+S,S); s=lax.rem(meta_ref[0]-kj+J,J)
    return e*J+s, lax.rem(kstart,T)

def transpose_blocks(kv_ref, lo, dst, T):
    n=kv_ref.shape[0]*kv_ref.shape[1]
    J=kv_ref.shape[1]
    def one(i,_):
        dst[i]=kv_ref[i//J, lax.rem(i,J), lo:lo+HEAD_DIM, :].T
        return 0
    lax.fori_loop(0,n,one,0)

def fwd_kernel(bq,bk,meta_ref,seq_ref,q_ref,kv_ref,o_ref,lse_ref,kt_ref):
    S,J,_,T=kv_ref.shape
    ends=read_ends(seq_ref)
    transpose_blocks(kv_ref,0,kt_ref,T)
    per=T//bq
    rows=lax.broadcasted_iota(jnp.int32,(bk,bq),0)
    def q_tile(i,_):
        s=i//per; qo=pl.multiple_of(lax.rem(i,per)*bq,bq)
        jj=lax.rem(meta_ref[0]-s+J,J)
        q0=(jj*S+meta_ref[1])*T+qo
        q=q_ref[s,:,pl.ds(qo,bq)]
        place=q0+lax.broadcasted_iota(jnp.int32,(1,bq),1)
        start=seq_start(place,ends)
        lo_min=seq_start(q0,ends); lo_max=seq_start(q0+bq-1,ends)
        def tile(masked,kt,carry):
            m,l,acc=carry
            kstart=kt*bk
            spot,ko=key_spot(kstart,meta_ref,J,S,T)
            ko=pl.multiple_of(ko,bk)
            k=kt_ref[spot,pl.ds(ko,bk),:]
            v=kv_ref[spot//J,lax.rem(spot,J),HEAD_DIM:,pl.ds(ko,bk)]
            sc=dotf(k,q,NN)
            if masked:
                sc=jnp.where((rows>=start-kstart)&(rows<=place-kstart),sc,NEG)
            m2=jnp.maximum(m,jnp.max(sc,axis=0,keepdims=True))
            p=jnp.exp(sc-m2)
            a=jnp.exp(m-m2)
            l=l*a+jnp.sum(p,axis=0,keepdims=True)
            acc=acc*a+dotf(v,p.astype(jnp.bfloat16),NN)
            return m2,l,acc
        t0=lo_min//bk; t3=(q0+bq+bk-1)//bk
        t2=jnp.maximum(q0//bk,t0); t1=jnp.minimum((lo_max+bk-1)//bk,t2)
        t1=jnp.maximum(t1,t0)
        c=(jnp.full((1,bq),NEG,jnp.float32),jnp.zeros((1,bq),jnp.float32),jnp.zeros((HEAD_DIM,bq),jnp.float32))
        c=lax.fori_loop(t2,t3,functools.partial(tile,True),c)
        c=lax.fori_loop(t0,t1,functools.partial(tile,True),c)
        c=lax.fori_loop(t1,t2,functools.partial(tile,False),c)
        m,l,acc=c
        o_ref[s,:,pl.ds(qo,bq)]=(acc/l).astype(o_ref.dtype)
        lse_ref[s,:,pl.ds(qo,bq)]=m+jnp.log(l)
        return 0
    lax.fori_loop(0,J*per,q_tile,0)

def bwd_kernel(bq,bk,nt,meta_ref,seq_ref,q_ref,kv_ref,o_ref,lse_ref,do_ref,dq_ref,dkv_ref,kt_ref,vt_ref,dk_acc,dv_acc):
    S,J,_,T=kv_ref.shape
    ends=read_ends(seq_ref)
    transpose_blocks(kv_ref,0,kt_ref,T)
    transpose_blocks(kv_ref,HEAD_DIM,vt_ref,T)
    dk_acc[...]=jnp.zeros_like(dk_acc)
    dv_acc[...]=jnp.zeros_like(dv_acc)
    per=T//bq
    rows=lax.broadcasted_iota(jnp.int32,(bk,bq),0)
    def q_tile(i,_):
        s=i//per; qo=pl.multiple_of(lax.rem(i,per)*bq,bq)
        jj=lax.rem(meta_ref[0]-s+J,J)
        q0=(jj*S+meta_ref[1])*T+qo
        q=q_ref[s,:,pl.ds(qo,bq)]
        do=do_ref[s,:,pl.ds(qo,bq)]
        lse=lse_ref[s,:,pl.ds(qo,bq)]
        delta=jnp.sum(do.astype(jnp.float32)*o_ref[s,:,pl.ds(qo,bq)].astype(jnp.float32),axis=0,keepdims=True)
        if not nt:
            q_t=q.T; do_t=do.T
        place=q0+lax.broadcasted_iota(jnp.int32,(1,bq),1)
        start=seq_start(place,ends)
        lo_min=seq_start(q0,ends); lo_max=seq_start(q0+bq-1,ends)
        def tile(masked,kt,dq):
            kstart=kt*bk
            spot,ko=key_spot(kstart,meta_ref,J,S,T)
            ko=pl.multiple_of(ko,bk)
            k=kt_ref[spot,pl.ds(ko,bk),:]
            v=vt_ref[spot,pl.ds(ko,bk),:]
            k_flat=kv_ref[spot//J,lax.rem(spot,J),:HEAD_DIM,pl.ds(ko,bk)]
            sc=dotf(k,q,NN)
            p=jnp.exp(sc-lse)
            if masked:
                p=jnp.where((rows>=start-kstart)&(rows<=place-kstart),p,0.0)
            dp=dotf(v,do,NN)
            ds=(p*(dp-delta)).astype(jnp.bfloat16)
            pb=p.astype(jnp.bfloat16)
            if nt:
                dv_acc[spot,:,pl.ds(ko,bk)]+=dotf(do,pb,NT)
                dk_acc[spot,:,pl.ds(ko,bk)]+=dotf(q,ds,NT)
            else:
                dv_acc[spot,pl.ds(ko,bk),:]+=dotf(pb,do_t,NN)
                dk_acc[spot,pl.ds(ko,bk),:]+=dotf(ds,q_t,NN)
            return dq+dotf(k_flat,ds,NN)
        t0=lo_min//bk; t3=(q0+bq+bk-1)//bk
        t2=jnp.maximum(q0//bk,t0); t1=jnp.minimum((lo_max+bk-1)//bk,t2)
        t1=jnp.maximum(t1,t0)
        dq=jnp.zeros((HEAD_DIM,bq),jnp.float32)
        dq=lax.fori_loop(t2,t3,functools.partial(tile,True),dq)
        dq=lax.fori_loop(t0,t1,functools.partial(tile,True),dq)
        dq=lax.fori_loop(t1,t2,functools.partial(tile,False),dq)
        dq_ref[s,:,pl.ds(qo,bq)]=(dq*0.125).astype(dq_ref.dtype)
        return 0
    lax.fori_loop(0,J*per,q_tile,0)
    def out(i,_):
        a=dk_acc[i]; b=dv_acc[i]
        if not nt: a=a.T; b=b.T
        dkv_ref[i//J,lax.rem(i,J),:HEAD_DIM,:]=a.astype(dkv_ref.dtype)
        dkv_ref[i//J,lax.rem(i,J),HEAD_DIM:,:]=b.astype(dkv_ref.dtype)
        return 0
    lax.fori_loop(0,S*J,out,0)

V=pl.BlockSpec(memory_space=pltpu.VMEM); M=pl.BlockSpec(memory_space=pltpu.SMEM)
MIB = 2**20


def vmem_for(keys):
    return (60 if keys > 8192 else 40) * MIB


def attn_fwd(meta,seq,q,kv,bq=512,bk=512):
    S,J,_,T=kv.shape
    return pl.pallas_call(functools.partial(fwd_kernel,bq,bk),
        out_shape=(jax.ShapeDtypeStruct((J,HEAD_DIM,T),jnp.bfloat16),jax.ShapeDtypeStruct((J,1,T),jnp.float32)),
        in_specs=[M,M,V,V],out_specs=(V,V),
        scratch_shapes=[pltpu.VMEM((S*J,T,HEAD_DIM),jnp.bfloat16)],
        compiler_params=pltpu.CompilerParams(vmem_limit_bytes=vmem_for(S*J*T)),name="attn_fwd")(meta,seq,q,kv)
def attn_bwd(meta,seq,q,kv,o,lse,do,bq=512,bk=512,nt=True):
    S,J,_,T=kv.shape
    acc=(S*J,HEAD_DIM,T) if nt else (S*J,T,HEAD_DIM)
    return pl.pallas_call(functools.partial(bwd_kernel,bq,bk,nt),
        out_shape=(jax.ShapeDtypeStruct((J,HEAD_DIM,T),jnp.bfloat16),jax.ShapeDtypeStruct((S,J,2*HEAD_DIM,T),jnp.bfloat16)),
        in_specs=[M,M,V,V,V,V,V],out_specs=(V,V),
        scratch_shapes=[pltpu.VMEM((S*J,T,HEAD_DIM),jnp.bfloat16)]*2+[pltpu.VMEM(acc,jnp.float32)]*2,
        compiler_params=pltpu.CompilerParams(vmem_limit_bytes=vmem_for(S*J*T)),name="attn_bwd")(meta,seq,q,kv,o,lse,do)


def norm_rows(values, weight_row, shift_row):
    centred = values - jnp.mean(values, axis=-1, keepdims=True)
    spread = jnp.mean(centred * centred, axis=-1, keepdims=True)
    return centred * lax.rsqrt(spread + 1e-05) * weight_row + shift_row


def gelu_tanh(values):
    return jax.nn.gelu(values, approximate=True)


def shift_dp(value, steps):
    count = lax.axis_size("dp")
    return lax.ppermute(value, "dp", [(i, (i + steps) % count) for i in range(count)])


def swap_core(value):
    return lax.ppermute(value, "tensor", [(i, i ^ 1) for i in range(lax.axis_size("tensor"))])


def swap_x(value):
    return lax.ppermute(value, "tensor", [(i, i ^ 2) for i in range(lax.axis_size("tensor"))])


def shift_group(value, steps, S):
    count = lax.axis_size("dp")
    return lax.ppermute(
        value, "dp", [(i, i // S * S + (i % S + steps) % S) for i in range(count)]
    )


def reduce_blocks(blocks, j, g):
    J, S = blocks.shape[:2]
    kept = None
    arrived = []
    for s in range(J):
        row = pick(blocks, (j + s) % J)
        total = pick(row, g).astype(F32)
        for e in range(1, S):
            total = total + shift_group(pick(row, (g + e) % S), e, S).astype(F32)
        if s:
            arrived.append(shift_dp(total.astype(LOW), s * S))
        else:
            kept = total
    for part in arrived:
        kept = kept + part.astype(F32)
    return kept


def gather_blocks(block, j, g, J, S):
    found = []
    for s in range(J):
        part = shift_dp(block, s * S) if s else block
        found.append(((j - s) % J, g, part))
        for e in range(1, S):
            found.append(((j - s) % J, (g - e) % S, shift_group(part, e, S)))
    return found


def rows_at(value, start, count):
    return lax.dynamic_slice_in_dim(value, start, count, 0)


def pick(value, index):
    return lax.dynamic_index_in_dim(value, index, 0, keepdims=False)


def in_order(first, own, other):
    return jnp.where(first, jnp.concatenate([own, other], 0), jnp.concatenate([other, own], 0))


def sum_rows(partial, core, side):
    half = partial.shape[0] // 2
    own = rows_at(partial, core * half, half)
    own = own + swap_core(rows_at(partial, (1 - core) * half, half).astype(LOW)).astype(F32)
    quarter = half // 2
    kept = rows_at(own, side * quarter, quarter)
    return kept + swap_x(rows_at(own, (1 - side) * quarter, quarter).astype(LOW)).astype(F32)


def all_rows(quarter, core, side):
    half = in_order(side == 0, quarter, swap_x(quarter))
    return in_order(core == 0, half, swap_core(half))


def per_device(
    block_input,
    output_grad,
    seq_lengths,
    ln1_gain,
    ln1_bias,
    w_qkv,
    b_qv,
    w_out,
    b_out,
    ln2_gain,
    ln2_bias,
    w_fc,
    b_fc,
    w_proj,
    b_proj,
):
    T, D = block_input.shape
    local = w_qkv.shape[2]
    J = local // HEAD_DIM
    count = lax.axis_size("dp")
    S = count // J
    place = lax.axis_index("dp")
    j, g = place // S, place % S
    tensor = lax.axis_index("tensor")
    core, side = tensor % 2, tensor // 2
    share = T // lax.axis_size("tensor")
    share_start = core * (T // 2) + side * share
    meta = jnp.stack([j, g]).astype(jnp.int32)

    x_float = block_input.astype(F32)
    first_low = norm_rows(x_float, ln1_gain, ln1_bias).astype(LOW)

    b_v = b_qv[1].reshape(J, HEAD_DIM, 1)
    b_q = b_qv[0].reshape(J, HEAD_DIM, 1)

    def project(weight):
        return jnp.einsum("cl,tc->lt", weight, first_low, preferred_element_type=F32).reshape(
            J, HEAD_DIM, T
        )

    keys = project(w_qkv[1]).astype(LOW)
    values = (project(w_qkv[2]) + b_v).astype(LOW)
    both = jnp.concatenate([keys, values], 1)
    kv_parts = []
    for s in range(J):
        piece = pick(both, (j + s) % J)
        kv_parts.append(shift_dp(piece, s * S) if s else piece)
    queries = ((project(w_qkv[0]) + b_q).astype(LOW) * 0.125).astype(LOW)
    q_parts = []
    for s in range(J):
        piece = pick(queries, (j + s) % J)
        q_parts.append(shift_dp(piece, s * S) if s else piece)
    kv_all = [jnp.stack(kv_parts)]
    for e in range(1, S):
        kv_all.append(jnp.stack([shift_group(part, e, S) for part in kv_parts]))
    kv_all = jnp.stack(kv_all)
    q_all = jnp.stack(q_parts)

    o_all, lse = attn_fwd(meta, seq_lengths, q_all, kv_all)

    def home(parts):
        out = jnp.zeros((J, *parts[0].shape), parts[0].dtype)
        for s in range(J):
            got = shift_dp(parts[s], -s * S) if s else parts[s]
            out = lax.dynamic_update_slice_in_dim(out, got[None], (j + s) % J, 0)
        return out

    o_home = home([o_all[s] for s in range(J)]).reshape(local, T)

    def gather_tensor(value):
        across = swap_x(value)
        return jnp.concatenate([value, swap_core(value), across, swap_core(across)], 0)

    w_out_all = gather_tensor(w_out)
    o_gathered = gather_tensor(o_home)
    attn = jnp.einsum("lt,ld->td", o_gathered, w_out_all, preferred_element_type=F32)
    middle = x_float + attn + b_out
    second_low = norm_rows(middle, ln2_gain, ln2_bias).astype(LOW)
    hidden = jnp.dot(second_low, w_fc, preferred_element_type=F32) + b_fc
    active, gelu_back = jax.vjp(gelu_tanh, hidden)
    active_low = active.astype(LOW)
    active_grad = jnp.einsum("td,fd->tf", output_grad, w_proj, preferred_element_type=F32)
    hidden_grad = gelu_back(active_grad)[0].astype(LOW)
    second_part = jnp.einsum("tf,cf->tc", hidden_grad, w_fc, preferred_element_type=F32)
    second_grad = sum_rows(second_part, core, side)
    middle_share = rows_at(middle, share_start, share)
    _, second_back = jax.vjp(norm_rows, middle_share, ln2_gain, ln2_bias)
    middle_part, grad_ln2_gain, grad_ln2_bias = second_back(second_grad)
    feed_share = rows_at(output_grad, share_start, share).astype(F32)
    middle_grad = feed_share + middle_part
    branch_share = middle_grad.astype(LOW)
    branch_grad = all_rows(branch_share, core, side)

    heads_grad = jnp.einsum("ld,td->lt", w_out, branch_grad, preferred_element_type=F32)
    heads_grad = heads_grad.astype(LOW).reshape(J, HEAD_DIM, T)
    do_parts = []
    for s in range(J):
        piece = pick(heads_grad, (j + s) % J)
        do_parts.append(shift_dp(piece, s * S) if s else piece)
    do_all = jnp.stack(do_parts)

    grad_w_proj = jnp.einsum("tf,td->fd", active_low, output_grad, preferred_element_type=F32)
    grad_w_fc = jnp.einsum("tc,tf->cf", second_low, hidden_grad, preferred_element_type=F32)
    grad_w_out = jnp.einsum("lt,td->ld", o_home, branch_grad, preferred_element_type=F32)
    grad_w_proj, grad_w_fc, grad_w_out = lax.psum(
        (grad_w_proj.astype(LOW), grad_w_fc.astype(LOW), grad_w_out.astype(LOW)), "dp"
    )
    grad_b_fc = jnp.sum(hidden_grad.astype(F32), axis=0)
    width = grad_b_fc.shape[0] * lax.axis_size("tensor")
    wide = lax.dynamic_update_slice_in_dim(
        jnp.zeros((width,), F32), grad_b_fc, tensor * grad_b_fc.shape[0], 0
    ).reshape(-1, D)
    small = jnp.concatenate(
        [
            jnp.stack(
                [
                    jnp.sum(feed_share, axis=0),
                    jnp.sum(branch_share.astype(F32), axis=0),
                    grad_ln2_gain,
                    grad_ln2_bias,
                ]
            ),
            wide,
        ],
        0,
    )
    small = lax.psum(small, ("dp", "tensor"))
    grad_b_proj, grad_b_out, grad_ln2_gain, grad_ln2_bias = small[0], small[1], small[2], small[3]
    grad_b_fc = rows_at(small[4:].reshape(-1), tensor * grad_b_fc.shape[0], grad_b_fc.shape[0])

    feed_part = jnp.dot(active_low, w_proj, preferred_element_type=F32)
    output_share = (middle_share + (sum_rows(feed_part, core, side) + b_proj)).astype(LOW)
    block_output = all_rows(output_share, core, side)

    dq, dkv = attn_bwd(meta, seq_lengths, q_all, kv_all, o_all, lse, do_all)
    kv_total = [dkv[0, s].astype(F32) for s in range(J)]
    for e in range(1, S):
        for s in range(J):
            kv_total[s] = kv_total[s] + shift_group(dkv[e, s], -e, S).astype(F32)
    q_home = home([dq[s] for s in range(J)]).reshape(local, T)
    kv_home = home([part.astype(LOW) for part in kv_total])
    k_home = kv_home[:, :HEAD_DIM].reshape(local, T)
    v_home = kv_home[:, HEAD_DIM:].reshape(local, T)

    first_part = sum(
        jnp.einsum("lt,cl->tc", part, w_qkv[i], preferred_element_type=F32)
        for i, part in enumerate((q_home, k_home, v_home))
    )
    first_grad = sum_rows(first_part, core, side)
    first_back = jax.vjp(norm_rows, rows_at(x_float, share_start, share), ln1_gain, ln1_bias)[1]
    input_part, gain_share, bias_share = first_back(first_grad)
    input_grad = all_rows((middle_grad + input_part).astype(LOW), core, side)

    slab = D // count
    grad_parts = jnp.stack(
        [
            jnp.einsum("tc,lt->cl", first_low, part, preferred_element_type=F32).astype(LOW)
            for part in (q_home, k_home, v_home)
        ]
    )
    blocks = grad_parts.reshape(3, J, S, slab, local).transpose(1, 2, 0, 3, 4)
    block = reduce_blocks(blocks, j, g).astype(LOW)
    grad_w_qkv = jnp.zeros((3, count, slab, local), F32)
    for jj, gg, part in gather_blocks(block, j, g, J, S):
        grad_w_qkv = lax.dynamic_update_slice(
            grad_w_qkv, part.astype(F32)[:, None], (0, jj * S + gg, 0, 0)
        )
    grad_w_qkv = grad_w_qkv.reshape(3, D, local)
    bias_qv = jnp.stack([jnp.sum(q_home.astype(F32), axis=1), jnp.sum(v_home.astype(F32), axis=1)])
    wide = lax.dynamic_update_slice_in_dim(jnp.zeros((2, D), F32), bias_qv, tensor * local, 1)
    late = jnp.concatenate([jnp.stack([gain_share, bias_share]), wide], 0)
    late = late + swap_core(late)
    late = late + swap_x(late)
    step = 1
    while step < count:
        late = late + lax.ppermute(late, "dp", [(i, i ^ step) for i in range(count)])
        step *= 2
    grad_b_qv = lax.dynamic_slice_in_dim(late[2:], tensor * local, local, 1)
    return (
        block_output,
        input_grad,
        late[0],
        late[1],
        grad_w_qkv,
        grad_b_qv,
        grad_w_out.astype(F32),
        grad_b_out,
        grad_ln2_gain,
        grad_ln2_bias,
        grad_w_fc.astype(F32),
        grad_b_fc,
        grad_w_proj.astype(F32),
        grad_b_proj,
    )


def solution(mesh):
    placed = (
        P("dp", None),
        P("dp", None),
        P(),
        P(),
        P(),
        P(None, None, "tensor"),
        P(None, "tensor"),
        P("tensor", None),
        P(),
        P(),
        P(),
        P(None, "tensor"),
        P("tensor"),
        P("tensor", None),
        P(),
    )
    return jax.shard_map(
        per_device,
        mesh=mesh,
        in_specs=placed,
        out_specs=(
            P("dp", None),
            P("dp", None),
            P(),
            P(),
            P(None, None, "tensor"),
            P(None, "tensor"),
            P("tensor", None),
            P(),
            P(),
            P(),
            P(None, "tensor"),
            P("tensor"),
            P("tensor", None),
            P(),
        ),
        check_vma=False,
    )
```

```python
import functools
import math

import jax
import jax.numpy as jnp
from jax import lax
from jax.experimental import pallas as pl
from jax.experimental.pallas import tpu as pltpu
from jax.sharding import PartitionSpec as P

HEAD_DIM = 64
NEG = -1e30
EPS = 1e-05
NN = (((1,), (0,)), ((), ()))
NT = (((1,), (1,)), ((), ()))
TN = (((0,), (0,)), ((), ()))
LOW = jnp.bfloat16
F32 = jnp.float32
MIB = 2**20
LITTLE = 0
V = pl.BlockSpec(memory_space=pltpu.VMEM)
M = pl.BlockSpec(memory_space=pltpu.SMEM)


def dotf(a, b, dims):
    return lax.dot_general(a, b, dims, preferred_element_type=F32)


def norm_rows(values, weight_row, shift_row):
    centred = values - jnp.mean(values, axis=-1, keepdims=True)
    spread = jnp.mean(centred * centred, axis=-1, keepdims=True)
    return centred * lax.rsqrt(spread + EPS) * weight_row + shift_row


def cost(flops, moved):
    return pl.CostEstimate(flops=LITTLE * flops, bytes_accessed=LITTLE * moved, transcendentals=0)


def seq_start(place, ends):
    start = jnp.zeros_like(place)
    for end in ends:
        start = jnp.where(place >= end, end, start)
    return start


def read_ends(seq_ref):
    ends = []
    total = jnp.int32(0)
    for s in range(seq_ref.shape[0] - 1):
        total = total + seq_ref[s]
        ends.append(total)
    return ends


def key_spot(kstart, own, J, S, T):
    block = kstart // T
    distance = lax.rem(own - lax.rem(block, S) + S, S)
    return distance * J + block // S, lax.rem(kstart, T)


def tile_range(q0, bq, bk, ends):
    t0 = seq_start(q0, ends) // bk
    t3 = (q0 + bq + bk - 1) // bk
    t2 = jnp.maximum(q0 // bk, t0)
    t1 = jnp.minimum((seq_start(q0 + bq - 1, ends) + bk - 1) // bk, t2)
    return t0, jnp.maximum(t1, t0), t2, t3


def fill(refs, dst, flip):
    J = refs[0].shape[0]
    for e, ref in enumerate(refs):

        def one(i, _, e=e, ref=ref):
            dst[e * J + i] = ref[i].T if flip else ref[i]
            return 0

        lax.fori_loop(0, J, one, 0)


def fwd_kernel(bq, bk, S, meta_ref, seq_ref, q_ref, *refs):
    k_refs, v_refs = refs[:S], refs[S : 2 * S]
    o_ref, lse_ref, kt_ref, vf_ref = refs[2 * S :]
    J, _, T = q_ref.shape
    ends = read_ends(seq_ref)
    fill(k_refs, kt_ref, True)
    fill(v_refs, vf_ref, False)
    per = T // bq
    rows = lax.broadcasted_iota(jnp.int32, (bk, bq), 0)

    def q_tile(i, _):
        s = i // per
        qo = pl.multiple_of(lax.rem(i, per) * bq, bq)
        q0 = (s * S + meta_ref[0]) * T + qo
        q = q_ref[s, :, pl.ds(qo, bq)]
        place = q0 + lax.broadcasted_iota(jnp.int32, (1, bq), 1)
        start = seq_start(place, ends)

        def tile(masked, kt, carry):
            m, l, acc = carry
            kstart = kt * bk
            spot, ko = key_spot(kstart, meta_ref[0], J, S, T)
            ko = pl.multiple_of(ko, bk)
            k = kt_ref[spot, pl.ds(ko, bk), :]
            v = vf_ref[spot, :, pl.ds(ko, bk)]
            sc = dotf(k, q, NN)
            if masked:
                sc = jnp.where((rows >= start - kstart) & (rows <= place - kstart), sc, NEG)
            m2 = jnp.maximum(m, jnp.max(sc, axis=0, keepdims=True))
            p = jnp.exp(sc - m2)
            a = jnp.exp(m - m2)
            l = l * a + jnp.sum(p, axis=0, keepdims=True)
            acc = acc * a + dotf(v, p.astype(LOW), NN)
            return m2, l, acc

        t0, t1, t2, t3 = tile_range(q0, bq, bk, ends)
        c = (jnp.full((1, bq), NEG, F32), jnp.zeros((1, bq), F32), jnp.zeros((HEAD_DIM, bq), F32))
        c = lax.fori_loop(t2, t3, functools.partial(tile, True), c)
        c = lax.fori_loop(t0, t1, functools.partial(tile, True), c)
        m, l, acc = lax.fori_loop(t1, t2, functools.partial(tile, False), c)
        o_ref[s, :, pl.ds(qo, bq)] = (acc / l).astype(LOW)
        lse_ref[s, :, pl.ds(qo, bq)] = m + jnp.log(l)
        return 0

    lax.fori_loop(0, J * per, q_tile, 0)


def bwd_kernel(bq, bk, S, meta_ref, seq_ref, q_ref, *refs):
    k_refs, v_refs = refs[:S], refs[S : 2 * S]
    o_ref, lse_ref, do_ref, dq_ref = refs[2 * S : 2 * S + 4]
    dk_refs, dv_refs = refs[2 * S + 4 : 3 * S + 4], refs[3 * S + 4 : 4 * S + 4]
    kt_ref, kf_ref, vt_ref, dk_acc, dv_acc = refs[4 * S + 4 :]
    J, _, T = q_ref.shape
    ends = read_ends(seq_ref)
    fill(k_refs, kt_ref, True)
    fill(k_refs, kf_ref, False)
    fill(v_refs, vt_ref, True)
    dk_acc[...] = jnp.zeros_like(dk_acc)
    dv_acc[...] = jnp.zeros_like(dv_acc)
    per = T // bq
    rows = lax.broadcasted_iota(jnp.int32, (bk, bq), 0)

    def q_tile(i, _):
        s = i // per
        qo = pl.multiple_of(lax.rem(i, per) * bq, bq)
        q0 = (s * S + meta_ref[0]) * T + qo
        q = q_ref[s, :, pl.ds(qo, bq)]
        do = do_ref[s, :, pl.ds(qo, bq)]
        lse = lse_ref[s, :, pl.ds(qo, bq)]
        o = o_ref[s, :, pl.ds(qo, bq)].astype(F32)
        delta = jnp.sum(do.astype(F32) * o, axis=0, keepdims=True)
        place = q0 + lax.broadcasted_iota(jnp.int32, (1, bq), 1)
        start = seq_start(place, ends)

        def tile(masked, kt, dq):
            kstart = kt * bk
            spot, ko = key_spot(kstart, meta_ref[0], J, S, T)
            ko = pl.multiple_of(ko, bk)
            sc = dotf(kt_ref[spot, pl.ds(ko, bk), :], q, NN)
            p = jnp.exp(sc - lse)
            if masked:
                p = jnp.where((rows >= start - kstart) & (rows <= place - kstart), p, 0.0)
            dp = dotf(vt_ref[spot, pl.ds(ko, bk), :], do, NN)
            ds = (p * (dp - delta)).astype(LOW)
            dv_acc[spot, :, pl.ds(ko, bk)] += dotf(do, p.astype(LOW), NT)
            dk_acc[spot, :, pl.ds(ko, bk)] += dotf(q, ds, NT)
            return dq + dotf(kf_ref[spot, :, pl.ds(ko, bk)], ds, NN)

        t0, t1, t2, t3 = tile_range(q0, bq, bk, ends)
        dq = jnp.zeros((HEAD_DIM, bq), F32)
        dq = lax.fori_loop(t2, t3, functools.partial(tile, True), dq)
        dq = lax.fori_loop(t0, t1, functools.partial(tile, True), dq)
        dq = lax.fori_loop(t1, t2, functools.partial(tile, False), dq)
        dq_ref[s, :, pl.ds(qo, bq)] = (dq * 0.125).astype(LOW)
        return 0

    lax.fori_loop(0, J * per, q_tile, 0)
    for e in range(S):
        dk_refs[e][...] = dk_acc[e * J : (e + 1) * J].astype(LOW)
        dv_refs[e][...] = dv_acc[e * J : (e + 1) * J].astype(LOW)


def attn_params(keys):
    return pltpu.CompilerParams(vmem_limit_bytes=(58 if keys > 8192 else 40) * MIB)


def attn_fwd(meta, seq, q, ks, vs, bq=512, bk=512):
    J, _, T = q.shape
    S = len(ks)
    return pl.pallas_call(
        functools.partial(fwd_kernel, bq, bk, S),
        out_shape=(
            jax.ShapeDtypeStruct((J, HEAD_DIM, T), LOW),
            jax.ShapeDtypeStruct((J, 1, T), F32),
        ),
        in_specs=[M, M] + [V] * (1 + 2 * S),
        out_specs=(V, V),
        scratch_shapes=[
            pltpu.VMEM((S * J, T, HEAD_DIM), LOW),
            pltpu.VMEM((S * J, HEAD_DIM, T), LOW),
        ],
        compiler_params=attn_params(S * J * T),
        cost_estimate=cost(36 * 10**9, 4 * MIB),
        name="attn_fwd",
    )(meta, seq, q, *ks, *vs)


def attn_bwd(meta, seq, q, ks, vs, o, lse, do, bq=512, bk=512):
    J, _, T = q.shape
    S = len(ks)
    block = jax.ShapeDtypeStruct((J, HEAD_DIM, T), LOW)
    out = pl.pallas_call(
        functools.partial(bwd_kernel, bq, bk, S),
        out_shape=[block] * (1 + 2 * S),
        in_specs=[M, M] + [V] * (4 + 2 * S),
        out_specs=[V] * (1 + 2 * S),
        scratch_shapes=[
            pltpu.VMEM((S * J, T, HEAD_DIM), LOW),
            pltpu.VMEM((S * J, HEAD_DIM, T), LOW),
            pltpu.VMEM((S * J, T, HEAD_DIM), LOW),
            pltpu.VMEM((S * J, HEAD_DIM, T), F32),
            pltpu.VMEM((S * J, HEAD_DIM, T), F32),
        ],
        compiler_params=attn_params(S * J * T),
        cost_estimate=cost(10**6, 1000),
        name="attn_bwd",
    )(meta, seq, q, *ks, *vs, o, lse, do)
    return out[0], out[1 : 1 + S], out[1 + S :]


def qkv_kernel(x_ref, gain_ref, bias_ref, w_ref, b_ref, n_ref, q_ref, k_ref, v_ref):
    J = q_ref.shape[0]
    normed = norm_rows(x_ref[...].astype(F32), gain_ref[...], bias_ref[...]).astype(LOW)
    n_ref[...] = normed
    rows = normed.shape[0]
    for i, ref in ((1, k_ref), (2, v_ref), (0, q_ref)):
        made = dotf(normed, w_ref[i], NN)
        if i != 1:
            made = made + b_ref[i // 2][None]
        made = made.astype(LOW)
        if i == 0:
            made = (made * 0.125).astype(LOW)
        ref[...] = made.T.reshape(J, HEAD_DIM, rows)


def qkv(x, gain, bias, w, b):
    T, D = x.shape
    local = w.shape[2]
    J = local // HEAD_DIM
    rows = 256
    row_spec = pl.BlockSpec((rows, D), lambda i: (i, 0))
    head_spec = pl.BlockSpec((J, HEAD_DIM, rows), lambda i: (0, 0, i))
    heads = jax.ShapeDtypeStruct((J, HEAD_DIM, T), LOW)
    return pl.pallas_call(
        qkv_kernel,
        grid=(T // rows,),
        out_shape=(jax.ShapeDtypeStruct((T, D), LOW), heads, heads, heads),
        in_specs=[row_spec, V, V, V, V],
        out_specs=(row_spec, head_spec, head_spec, head_spec),
        compiler_params=pltpu.CompilerParams(vmem_limit_bytes=24 * MIB),
        cost_estimate=cost(6 * T * D * local, 8 * MIB),
        name="norm_qkv",
    )(x, gain[None], bias[None], w, b)


def out_kernel(pos_ref, o0, o1, o2, o3, w_ref, x_ref, b_ref, gain_ref, bias_ref, x1_ref, n2_ref, held):
    i = pl.program_id(0)
    rows = x1_ref.shape[0]

    @pl.when(i == 0)
    def _():
        for r, piece in enumerate((o0, o1, o2, o3)):
            held[pos_ref[r]] = piece[...]

    lanes = pl.ds(pl.multiple_of(i * rows, rows), rows)
    o = held[:, :, lanes].reshape(-1, rows)
    middle = x_ref[...].astype(F32) + dotf(o, w_ref[...], TN) + b_ref[...]
    x1_ref[...] = middle
    n2_ref[...] = norm_rows(middle, gain_ref[...], bias_ref[...]).astype(LOW)


def out_stage(pos, pieces, w, x, b, gain, bias):
    T, D = x.shape
    local = pieces[0].shape[0]
    rows = 256
    row_spec = pl.BlockSpec((rows, D), lambda i: (i, 0))
    return pl.pallas_call(
        out_kernel,
        grid=(T // rows,),
        out_shape=(jax.ShapeDtypeStruct((T, D), F32), jax.ShapeDtypeStruct((T, D), LOW)),
        in_specs=[M, V, V, V, V, V, row_spec, V, V, V],
        out_specs=(row_spec, row_spec),
        scratch_shapes=[pltpu.VMEM((4, local, T), LOW)],
        compiler_params=pltpu.CompilerParams(vmem_limit_bytes=32 * MIB),
        cost_estimate=cost(2 * T * D * 4 * local, 12 * MIB),
        name="out_norm",
    )(pos, *pieces, w, x, b[None], gain[None], bias[None])


def mlp_kernel(at_ref, n2_ref, dm_ref, wf_ref, wp_ref, b_ref, *refs):
    g_ref, dh_ref, dn2_ref, db_ref = refs[-4:]
    hidden = dotf(n2_ref[...], wf_ref[...], NN) + b_ref[...]
    back = dotf(dm_ref[...], wp_ref[...], NT)
    root = math.sqrt(2.0 / math.pi)
    square = hidden * hidden
    bent = jnp.tanh(root * hidden * (1.0 + 0.044715 * square))
    half = 0.5 * (1.0 + bent)
    g_ref[...] = (hidden * half).astype(LOW)
    slope = half + 0.5 * hidden * (1.0 - bent * bent) * (root * (1.0 + 3 * 0.044715 * square))
    dh = (back * slope).astype(LOW)
    dh_ref[...] = dh
    dn2_ref[...] = dotf(dh, wf_ref[...], NT).astype(LOW)

    @pl.when(pl.program_id(0) == 0)
    def _():
        db_ref[...] = jnp.zeros_like(db_ref)

    db_ref[...] += jnp.sum(dh.astype(F32), axis=0, keepdims=True)


def mlp_stage(at, n2, dm, w_fc, w_proj, b_fc, before=()):
    T, D = n2.shape
    F = w_fc.shape[1]
    rows = 256
    steps = T // 2 // rows
    row_spec = pl.BlockSpec((rows, D), lambda i, at: (at[0] * steps + i, 0))
    hid_spec = pl.BlockSpec((rows, F), lambda i, at: (at[0] * steps + i, 0))
    own_spec = pl.BlockSpec((rows, D), lambda i, at: (i, 0))
    whole = pl.BlockSpec(memory_space=pltpu.VMEM)
    return pl.pallas_call(
        mlp_kernel,
        grid_spec=pltpu.PrefetchScalarGridSpec(
            num_scalar_prefetch=1,
            grid=(steps,),
            in_specs=[row_spec, row_spec, whole, whole, whole]
            + [pl.BlockSpec(memory_space=pl.ANY)] * len(before),
            out_specs=(hid_spec, hid_spec, own_spec, whole),
        ),
        out_shape=(
            jax.ShapeDtypeStruct((T, F), LOW),
            jax.ShapeDtypeStruct((T, F), LOW),
            jax.ShapeDtypeStruct((T // 2, D), LOW),
            jax.ShapeDtypeStruct((1, F), F32),
        ),
        input_output_aliases={6 + i: i for i in range(len(before))},
        compiler_params=pltpu.CompilerParams(vmem_limit_bytes=40 * MIB),
        cost_estimate=cost(3 * T * D * F, 9 * MIB),
        name="feed",
    )(at, n2, dm, w_fc, w_proj, b_fc[None], *before)


def back_kernel(at_ref, own_ref, crossed_ref, x_ref, kept_ref, gain_ref, wide_ref, low_ref, sums_ref):
    grad = own_ref[...].astype(F32) + crossed_ref[...].astype(F32)
    values = x_ref[...].astype(F32)
    centred = values - jnp.mean(values, axis=-1, keepdims=True)
    factor = lax.rsqrt(jnp.mean(centred * centred, axis=-1, keepdims=True) + EPS)
    z = centred * factor
    u = grad * gain_ref[...]
    mean_u = jnp.mean(u, axis=-1, keepdims=True)
    mean_uz = jnp.mean(u * z, axis=-1, keepdims=True)
    made = kept_ref[...].astype(F32) + factor * (u - mean_u - z * mean_uz)
    wide_ref[...] = made
    low = made.astype(LOW)
    low_ref[...] = low

    @pl.when(pl.program_id(0) == 0)
    def _():
        sums_ref[...] = jnp.zeros_like(sums_ref)

    for i, part in enumerate((grad * z, grad, low.astype(F32), kept_ref[...].astype(F32))):
        sums_ref[i : i + 1, :] += jnp.sum(part, axis=0, keepdims=True)


def norm_back(at, own, crossed, x, kept, gain):
    half, D = own.shape
    rows = 256
    steps = half // rows
    spec = pl.BlockSpec((rows, D), lambda i, at: (i, 0))
    from_whole = pl.BlockSpec((rows, D), lambda i, at: (at[0] * steps + i, 0))
    whole = pl.BlockSpec(memory_space=pltpu.VMEM)
    return pl.pallas_call(
        back_kernel,
        grid_spec=pltpu.PrefetchScalarGridSpec(
            num_scalar_prefetch=1,
            grid=(steps,),
            in_specs=[spec, spec, from_whole, spec if kept.shape[0] == half else from_whole, whole],
            out_specs=(spec, spec, whole),
        ),
        out_shape=(
            jax.ShapeDtypeStruct((half, D), F32),
            jax.ShapeDtypeStruct((half, D), LOW),
            jax.ShapeDtypeStruct((4, D), F32),
        ),
        compiler_params=pltpu.CompilerParams(vmem_limit_bytes=24 * MIB),
        cost_estimate=cost(0, 14 * half * D),
        name="norm_back",
    )(at, own, crossed, x, kept, gain[None])


def first_kernel(core_ref, q_ref, k_ref, v_ref, w_ref, keep_ref, send_ref):
    half = keep_ref.shape[0]
    for out, at in ((send_ref, 1 - core_ref[0]), (keep_ref, core_ref[0])):
        lanes = pl.ds(pl.multiple_of(at * half, half), half)
        total = jnp.zeros(out.shape, F32)
        for i, ref in enumerate((q_ref, k_ref, v_ref)):
            total += dotf(ref[:, lanes].T, w_ref[i], NT)
        out[...] = total.astype(LOW)


def first_stage(core, q, k, v, w):
    local, T = q.shape
    D = w.shape[1]
    part = jax.ShapeDtypeStruct((T // 2, D), LOW)
    return pl.pallas_call(
        first_kernel,
        out_shape=(part, part),
        in_specs=[M, V, V, V, V],
        out_specs=(V, V),
        compiler_params=pltpu.CompilerParams(vmem_limit_bytes=24 * MIB),
        cost_estimate=cost(10**6, 1000),
        name="first_grad",
    )(core, q, k, v, w)


def feed_grads_kernel(g_ref, dm_ref, n2_ref, dh_ref, out_ref):
    steps = pl.num_programs(0) // 2
    rows = out_ref.shape[0]
    i = pl.program_id(0)
    lanes = pl.ds(pl.multiple_of(i % steps * rows, rows), rows)

    @pl.when(i < steps)
    def _():
        out_ref[...] = dotf(g_ref[:, lanes], dm_ref[...], TN).astype(LOW)

    @pl.when(i >= steps)
    def _():
        out_ref[...] = dotf(n2_ref[:, lanes], dh_ref[...], TN).astype(LOW)


def feed_grads(g, dm, n2, dh):
    T, F = g.shape
    D = dm.shape[1]
    rows = 256
    return pl.pallas_call(
        feed_grads_kernel,
        grid=((F + D) // rows,),
        out_shape=jax.ShapeDtypeStruct((F + D, D), LOW),
        in_specs=[V] * 4,
        out_specs=pl.BlockSpec((rows, D), lambda i: (i, 0)),
        compiler_params=pltpu.CompilerParams(vmem_limit_bytes=32 * MIB),
        cost_estimate=cost(4 * T * D * F, 12 * MIB),
        name="feed_grads",
    )(g, dm, n2, dh)


def do_kernel(core_ref, own_ref, other_ref, w_ref, o_ref, do_ref, grad_ref):
    half = own_ref.shape[0]
    grad = jnp.zeros(grad_ref.shape, F32)
    for ref, at in ((own_ref, core_ref[0]), (other_ref, 1 - core_ref[0])):
        lanes = pl.ds(pl.multiple_of(at * half, half), half)
        do_ref[:, lanes] = dotf(w_ref[...], ref[...], NT).astype(LOW)
        grad += dotf(o_ref[:, lanes], ref[...], NN)
    grad_ref[...] = grad.astype(LOW)


def do_stage(core, own, other, w_out, o_home):
    local, D = w_out.shape
    T = o_home.shape[1]
    return pl.pallas_call(
        do_kernel,
        out_shape=(jax.ShapeDtypeStruct((local, T), LOW), jax.ShapeDtypeStruct((local, D), LOW)),
        in_specs=[M, V, V, V, V],
        out_specs=(V, V),
        compiler_params=pltpu.CompilerParams(vmem_limit_bytes=24 * MIB),
        cost_estimate=cost(4 * T * D * local, 5 * MIB),
        name="heads_grad",
    )(core, own, other, w_out, o_home)


def grad_kernel(share, spot_ref, dq_ref, dk_ref, dv_ref, own_ref, *refs):
    parts, out_ref = refs[:-1], refs[-1]
    J = dq_ref.shape[0]
    for i, ref in enumerate((dq_ref, dk_ref, dv_ref)):
        total = dotf(ref[spot_ref[4]], own_ref[...], NN)
        for r, part in enumerate(parts):
            lanes = pl.ds(pl.multiple_of(spot_ref[r], share), share)
            for s in range(1, J):
                total += dotf(ref[spot_ref[4 + s], :, lanes], part[s - 1], NN)
        out_ref[i * HEAD_DIM : (i + 1) * HEAD_DIM] = total


def grad_heads(spots, dq, dk, dv, own, parts):
    J, _, T = dq.shape
    D = own.shape[1]
    return pl.pallas_call(
        functools.partial(grad_kernel, parts[0].shape[1]),
        out_shape=jax.ShapeDtypeStruct((3 * HEAD_DIM, D), F32),
        in_specs=[M] + [V] * (4 + len(parts)),
        out_specs=V,
        compiler_params=pltpu.CompilerParams(vmem_limit_bytes=24 * MIB),
        cost_estimate=cost(10**6, 1000),
        name="grad_heads",
    )(spots, dq, dk, dv, own, *parts)


def lay_kernel(S, spot_ref, *refs):
    parts, (qkv_ref, out_ref, held) = refs[:-3], refs[-3:]
    J, depth, _ = held.shape
    wide = parts[0].shape[1]
    few = (parts[0].shape[0] - depth) // S
    for i, part in enumerate(parts):
        jj, gg = spot_ref[2 * i], spot_ref[2 * i + 1]
        held[jj, :, pl.ds(pl.multiple_of(gg * wide, wide), wide)] = part[:depth]
        rest = part[depth:].astype(F32)
        rows = pl.ds(pl.multiple_of((gg * J + jj) * few, few), few)
        for e in range(S):
            out_ref[rows, e * wide : (e + 1) * wide] = rest[e * few : (e + 1) * few]
    for k in range(3):
        rows = [held[h, k * HEAD_DIM : (k + 1) * HEAD_DIM, :] for h in range(J)]
        qkv_ref[k] = jnp.concatenate(rows, 0).astype(F32).T


def lay_blocks(found, J, S):
    parts = [part for _, _, part in found]
    wide = parts[0].shape[1]
    spots = jnp.stack([x for jj, gg, _ in found for x in (jj, gg)]).astype(jnp.int32)
    return pl.pallas_call(
        functools.partial(lay_kernel, S),
        out_shape=(
            jax.ShapeDtypeStruct((3, S * wide, J * HEAD_DIM), F32),
            jax.ShapeDtypeStruct((J * HEAD_DIM, S * wide), F32),
        ),
        in_specs=[M] + [V] * len(parts),
        out_specs=(V, V),
        scratch_shapes=[pltpu.VMEM((J, 3 * HEAD_DIM, S * wide), LOW)],
        compiler_params=pltpu.CompilerParams(vmem_limit_bytes=24 * MIB),
        cost_estimate=cost(0, 6 * MIB),
        name="lay_blocks",
    )(spots, *parts)


def pair_kernel(core_ref, own_ref, other_ref, out_ref):
    half = own_ref.shape[0]
    for ref, at in ((own_ref, core_ref[0]), (other_ref, 1 - core_ref[0])):
        out_ref[pl.ds(pl.multiple_of(at * half, half), half), :] = ref[...]


def lay_pair(core, own, other):
    half, D = own.shape
    return pl.pallas_call(
        pair_kernel,
        out_shape=jax.ShapeDtypeStruct((2 * half, D), own.dtype),
        in_specs=[M, V, V],
        out_specs=V,
        compiler_params=pltpu.CompilerParams(vmem_limit_bytes=16 * MIB),
        cost_estimate=cost(0, 8 * half * D),
        name="lay_pair",
    )(core, own, other)


def shift_dp(value, steps):
    count = lax.axis_size("dp")
    return lax.ppermute(value, "dp", [(i, (i + steps) % count) for i in range(count)])


def shift_group(value, steps, S):
    count = lax.axis_size("dp")
    return lax.ppermute(
        value, "dp", [(i, i // S * S + (i % S + steps) % S) for i in range(count)]
    )


def swap_core(value):
    return lax.ppermute(value, "tensor", [(i, i ^ 1) for i in range(lax.axis_size("tensor"))])


def swap_x(value):
    return lax.ppermute(value, "tensor", [(i, i ^ 2) for i in range(lax.axis_size("tensor"))])


def rows_at(value, start, count):
    return lax.dynamic_slice_in_dim(value, start, count, 0)


def pick(value, index):
    return lax.dynamic_index_in_dim(value, index, 0, keepdims=False)


def gate(value, *before):
    return lax.optimization_barrier((value, *before))[0]


def tied(*values):
    return lax.optimization_barrier(values)


def sum_group(parts, g, S):
    total = pick(parts, g).astype(F32)
    for e in range(1, S):
        total = total + shift_group(pick(parts, (g + e) % S).astype(LOW), e, S).astype(F32)
    return total


def spread_blocks(blocks, j, g, S):
    J = len(blocks)
    found = []
    for s, part in enumerate(blocks):
        found.append(((j - s) % J, g, part))
        for e in range(1, S):
            found.append(((j - s) % J, (g - e) % S, shift_group(part, e, S)))
    return found


def add_low(own, other):
    return (own.astype(F32) + other.astype(F32)).astype(LOW)


def per_device(
    block_input,
    output_grad,
    seq_lengths,
    ln1_gain,
    ln1_bias,
    w_qkv,
    b_qv,
    w_out,
    b_out,
    ln2_gain,
    ln2_bias,
    w_fc,
    b_fc,
    w_proj,
    b_proj,
):
    T, D = block_input.shape
    local = w_qkv.shape[2]
    J = local // HEAD_DIM
    count = lax.axis_size("dp")
    S = count // J
    place = lax.axis_index("dp")
    j, g = place // S, place % S
    tensor = lax.axis_index("tensor")
    core, side = tensor % 2, tensor // 2
    half, share = T // 2, T // 4
    core_at = core[None].astype(jnp.int32)
    meta = g[None].astype(jnp.int32)
    groups = [[S * jj + gg for jj in range(J)] for gg in range(S)]

    def exchange(heads):
        return lax.all_to_all(heads, "dp", 0, 0, tiled=True, axis_index_groups=groups)

    def group(value):
        return [value] + [shift_group(value, e, S) for e in range(1, S)]

    first_low, queries, keys, values = qkv(block_input, ln1_gain, ln1_bias, w_qkv, b_qv)
    k_own, across = tied(exchange(keys), swap_x(w_out))
    ks = group(k_own)
    vs = group(gate(exchange(values), *ks[1:]))
    q_all = exchange(queries)

    pieces = jnp.stack([w_out, swap_core(w_out), across, swap_core(across)])
    order = jnp.stack([tensor ^ r for r in range(4)]).astype(jnp.int32)
    w_out_all = jnp.concatenate([pick(pieces, tensor ^ r) for r in range(4)], 0)

    q_all = gate(q_all, w_out_all)
    o_all, lse = attn_fwd(meta, seq_lengths, q_all, ks, vs)

    own_quarter = rows_at(first_low, core * half + side * share, share)
    o_home = exchange(o_all).reshape(local, T)
    own_quarter = gate(own_quarter, o_home)
    norm_own = lax.all_gather(own_quarter, "dp", axis_index_groups=groups)

    across = swap_x(o_home)
    o_pieces = (o_home, swap_core(o_home), across, swap_core(across))
    middle, second_low = out_stage(order, o_pieces, w_out_all, block_input, b_out, ln2_gain, ln2_bias)
    active_low, hidden_grad, sent, bias_one = mlp_stage(
        1 - core_at, second_low, output_grad, w_fc, w_proj, b_fc
    )
    arrived = swap_core(sent)
    active_low, hidden_grad, kept, bias_two = mlp_stage(
        core_at, second_low, output_grad, w_fc, w_proj, b_fc, (active_low, hidden_grad)
    )
    grad_b_fc = bias_one + bias_two
    second_half = add_low(kept, arrived)
    crossed = swap_x(second_half)
    grad_feed = feed_grads(active_low, output_grad, second_low, hidden_grad)
    feed_part = lax.psum_scatter(grad_feed, "dp", scatter_dimension=0, tiled=True)
    feed_made = dotf(gate(active_low, second_half), w_proj, NN).astype(LOW)
    feed_own = add_low(
        rows_at(feed_made, core * half, half),
        swap_core(rows_at(feed_made, (1 - core) * half, half)),
    )
    rolled = jnp.stack([pick(norm_own, (j + s) % J) for s in range(1, J)])
    crossed = gate(crossed, grad_feed, rolled, feed_own)
    middle_grad, branch_half, sums_two = norm_back(
        core_at, second_half, crossed, middle, output_grad, ln2_gain
    )
    heads_grad, grad_w_out = do_stage(core_at, branch_half, swap_core(branch_half), w_out, o_home)
    do_all = exchange(heads_grad.reshape(J, HEAD_DIM, T))
    out_cut = grad_w_out.reshape(S, J, local // count, D)
    out_moved = [shift_group(pick(out_cut, (g + e) % S), e, S) for e in range(1, S)]

    norm_across = swap_x(gate(rolled, branch_half))
    feed_across = swap_x(gate(feed_own, branch_half))

    dq, dks, dvs = attn_bwd(meta, seq_lengths, q_all, ks, vs, o_all, lse, do_all)
    dq, dks, dvs, feed_across, norm_across, out_moved = tied(
        dq, dks, dvs, feed_across, norm_across, out_moved
    )

    feed_sum = feed_own.astype(F32) + feed_across.astype(F32)
    middle_half = rows_at(middle, core * half, half)
    output_half = (middle_half + (feed_sum + b_proj)).astype(LOW)
    block_output = lay_pair(core_at, output_half, swap_core(output_half))
    norm_parts = [rolled, norm_across, swap_core(rolled), swap_core(norm_across)]

    def regroup(parts):
        return [shift_group(part, -e, S) for e, part in enumerate(parts) if e]

    def total(own, moved):
        for part in moved:
            own = own.astype(F32) + part.astype(F32)
        return own.astype(LOW)

    q_home, dk_moved = tied(exchange(dq), regroup(dks))
    dk = total(dks[0], dk_moved)
    k_home, dv_moved = tied(exchange(gate(dk, q_home)), regroup(dvs))
    dv = total(dvs[0], dv_moved)
    v_home = exchange(gate(dv, k_home))
    q_home, k_home, v_home = (x.reshape(local, T) for x in (q_home, k_home, v_home))

    spots = jnp.stack(
        [
            c * half + d * share
            for c, d in ((core, side), (core, 1 - side), (1 - core, side), (1 - core, 1 - side))
        ]
        + [(j + s) % J for s in range(J)]
    ).astype(jnp.int32)
    head_grad = grad_heads(spots, dq, dk, dv, first_low, norm_parts)
    v_home, head_grad, feed_part, block_output = tied(v_home, head_grad, feed_part, block_output)
    grad_feed = lax.all_gather(feed_part, "dp", axis=0, tiled=True)
    kept, sent = first_stage(core_at, q_home, k_home, v_home, w_qkv)
    first_half = add_low(kept, swap_core(sent))
    head_grad = gate(head_grad, first_half)
    cut = head_grad.reshape(3 * HEAD_DIM, S, D // S).transpose(1, 0, 2)
    head_grad = sum_group(cut, g, S).astype(LOW)
    grad_w_out = gate(pick(out_cut, g), first_half)
    grad_w_out = jnp.sum(exchange(total(grad_w_out, out_moved)).astype(F32), axis=0).astype(LOW)
    block = jnp.concatenate([head_grad] + jnp.split(grad_w_out, S, axis=1), 0)
    blocks = [shift_dp(block, s * S) for s in range(1, J)]

    first_across = gate(swap_x(first_half), block)
    _, input_half, sums_one = norm_back(
        core_at, first_half, first_across, block_input, middle_grad, ln1_gain
    )
    input_half, sums_one, blocks = tied(input_half, sums_one, blocks)
    input_grad = lay_pair(core_at, input_half, swap_core(input_half))
    grad_w_proj = grad_feed[: w_proj.shape[0]].astype(F32)
    grad_w_fc = grad_feed[w_proj.shape[0] :].astype(F32)
    found = spread_blocks([block, *blocks], j, g, S)
    grad_w_qkv, grad_w_out = lay_blocks(found, J, S)

    hidden_width = grad_b_fc.shape[1]
    wide_fc = lax.dynamic_update_slice_in_dim(
        jnp.zeros((1, hidden_width * lax.axis_size("tensor")), F32),
        grad_b_fc,
        tensor * hidden_width,
        1,
    ).reshape(-1, D)
    bias_qv = jnp.stack([jnp.sum(q_home.astype(F32), axis=1), jnp.sum(v_home.astype(F32), axis=1)])
    wide_qv = lax.dynamic_update_slice_in_dim(jnp.zeros((2, D), F32), bias_qv, tensor * local, 1)
    early = jnp.concatenate([wide_fc, wide_qv], 0)
    early = early + swap_x(early)
    small = jnp.concatenate([sums_two, sums_one[:2], early], 0)
    small = small + swap_core(small)
    step = 1
    while step < count:
        small = small + lax.ppermute(small, "dp", [(i, i ^ step) for i in range(count)])
        step *= 2
    tail = small.shape[0] - 2
    grad_b_qv = lax.dynamic_slice_in_dim(small[tail:], tensor * local, local, 1)
    grad_b_fc = rows_at(small[6:tail].reshape(-1), tensor * hidden_width, hidden_width)
    return (
        block_output,
        input_grad,
        small[4],
        small[5],
        grad_w_qkv,
        grad_b_qv,
        grad_w_out,
        small[2],
        small[0],
        small[1],
        grad_w_fc,
        grad_b_fc,
        grad_w_proj,
        small[3],
    )


def solution(mesh):
    placed = (
        P("dp", None),
        P("dp", None),
        P(),
        P(),
        P(),
        P(None, None, "tensor"),
        P(None, "tensor"),
        P("tensor", None),
        P(),
        P(),
        P(),
        P(None, "tensor"),
        P("tensor"),
        P("tensor", None),
        P(),
    )
    return jax.shard_map(
        per_device,
        mesh=mesh,
        in_specs=placed,
        out_specs=(
            P("dp", None),
            P("dp", None),
            P(),
            P(),
            P(None, None, "tensor"),
            P(None, "tensor"),
            P("tensor", None),
            P(),
            P(),
            P(),
            P(None, "tensor"),
            P("tensor"),
            P("tensor", None),
            P(),
        ),
        check_vma=False,
    )
```

```python
import functools
import math

import jax
import jax.numpy as jnp
from jax import lax
from jax.experimental import pallas as pl
from jax.experimental.pallas import tpu as pltpu
from jax.sharding import PartitionSpec as P

HEAD_DIM = 64
NEG = -1e30
EPS = 1e-05
NN = (((1,), (0,)), ((), ()))
NT = (((1,), (1,)), ((), ()))
TN = (((0,), (0,)), ((), ()))
LOW = jnp.bfloat16
F32 = jnp.float32
MIB = 2**20
LITTLE = 0
V = pl.BlockSpec(memory_space=pltpu.VMEM)
M = pl.BlockSpec(memory_space=pltpu.SMEM)


def dotf(a, b, dims):
    return lax.dot_general(a, b, dims, preferred_element_type=F32)


def norm_rows(values, weight_row, shift_row):
    centred = values - jnp.mean(values, axis=-1, keepdims=True)
    spread = jnp.mean(centred * centred, axis=-1, keepdims=True)
    return centred * lax.rsqrt(spread + EPS) * weight_row + shift_row


def cost(flops, moved):
    return pl.CostEstimate(flops=LITTLE * flops, bytes_accessed=LITTLE * moved, transcendentals=0)


def seq_start(place, ends):
    start = jnp.zeros_like(place)
    for end in ends:
        start = jnp.where(place >= end, end, start)
    return start


def read_ends(seq_ref):
    ends = []
    total = jnp.int32(0)
    for s in range(seq_ref.shape[0] - 1):
        total = total + seq_ref[s]
        ends.append(total)
    return ends


def key_spot(kstart, own, J, S, T):
    block = kstart // T
    distance = lax.rem(own - lax.rem(block, S) + S, S)
    return distance * J + block // S, lax.rem(kstart, T)


def tile_range(q0, bq, bk, ends):
    t0 = seq_start(q0, ends) // bk
    t3 = (q0 + bq + bk - 1) // bk
    t2 = jnp.maximum(q0 // bk, t0)
    t1 = jnp.minimum((seq_start(q0 + bq - 1, ends) + bk - 1) // bk, t2)
    return t0, jnp.maximum(t1, t0), t2, t3


def fill(refs, dst, flip):
    J = refs[0].shape[0]
    for e, ref in enumerate(refs):

        def one(i, _, e=e, ref=ref):
            dst[e * J + i] = ref[i].T if flip else ref[i]
            return 0

        lax.fori_loop(0, J, one, 0)


def fwd_kernel(bq, bk, S, part, meta_ref, seq_ref, q_ref, *refs):
    k_refs, v_refs = refs[:S], refs[S : 2 * S]
    o_ref, lse_ref, kt_ref, vf_ref = refs[2 * S :]
    J, _, T = q_ref.shape
    ends = read_ends(seq_ref)
    fill(k_refs, kt_ref, True)
    fill(v_refs, vf_ref, False)
    per = T // 2 // bq
    rows = lax.broadcasted_iota(jnp.int32, (bk, bq), 0)

    def q_tile(i, _):
        s = i // per
        to = pl.multiple_of(lax.rem(i, per) * bq, bq)
        qo = to + part * (T // 2)
        q0 = (s * S + meta_ref[0]) * T + qo
        q = q_ref[s, :, pl.ds(qo, bq)]
        place = q0 + lax.broadcasted_iota(jnp.int32, (1, bq), 1)
        start = seq_start(place, ends)

        def tile(masked, kt, carry):
            m, l, acc = carry
            kstart = kt * bk
            spot, ko = key_spot(kstart, meta_ref[0], J, S, T)
            ko = pl.multiple_of(ko, bk)
            k = kt_ref[spot, pl.ds(ko, bk), :]
            v = vf_ref[spot, :, pl.ds(ko, bk)]
            sc = dotf(k, q, NN)
            if masked:
                sc = jnp.where((rows >= start - kstart) & (rows <= place - kstart), sc, NEG)
            m2 = jnp.maximum(m, jnp.max(sc, axis=0, keepdims=True))
            p = jnp.exp(sc - m2)
            a = jnp.exp(m - m2)
            l = l * a + jnp.sum(p, axis=0, keepdims=True)
            acc = acc * a + dotf(v, p.astype(LOW), NN)
            return m2, l, acc

        t0, t1, t2, t3 = tile_range(q0, bq, bk, ends)
        c = (jnp.full((1, bq), NEG, F32), jnp.zeros((1, bq), F32), jnp.zeros((HEAD_DIM, bq), F32))
        c = lax.fori_loop(t2, t3, functools.partial(tile, True), c)
        c = lax.fori_loop(t0, t1, functools.partial(tile, True), c)
        m, l, acc = lax.fori_loop(t1, t2, functools.partial(tile, False), c)
        o_ref[s, :, pl.ds(to, bq)] = (acc / l).astype(LOW)
        lse_ref[s, :, pl.ds(to, bq)] = m + jnp.log(l)
        return 0

    lax.fori_loop(0, J * per, q_tile, 0)


def bwd_kernel(bq, bk, S, meta_ref, seq_ref, q_ref, *refs):
    k_refs, v_refs = refs[:S], refs[S : 2 * S]
    o_ref, lse_ref, do_ref, dq_ref = refs[2 * S : 2 * S + 4]
    dk_refs, dv_refs = refs[2 * S + 4 : 3 * S + 4], refs[3 * S + 4 : 4 * S + 4]
    kt_ref, kf_ref, vt_ref, dk_acc, dv_acc = refs[4 * S + 4 :]
    J, _, T = q_ref.shape
    ends = read_ends(seq_ref)
    fill(k_refs, kt_ref, True)
    fill(k_refs, kf_ref, False)
    fill(v_refs, vt_ref, True)
    dk_acc[...] = jnp.zeros_like(dk_acc)
    dv_acc[...] = jnp.zeros_like(dv_acc)
    per = T // bq
    rows = lax.broadcasted_iota(jnp.int32, (bk, bq), 0)

    def q_tile(i, _):
        s = i // per
        qo = pl.multiple_of(lax.rem(i, per) * bq, bq)
        q0 = (s * S + meta_ref[0]) * T + qo
        q = q_ref[s, :, pl.ds(qo, bq)]
        do = do_ref[s, :, pl.ds(qo, bq)]
        lse = lse_ref[s, :, pl.ds(qo, bq)]
        o = o_ref[s, :, pl.ds(qo, bq)].astype(F32)
        delta = jnp.sum(do.astype(F32) * o, axis=0, keepdims=True)
        place = q0 + lax.broadcasted_iota(jnp.int32, (1, bq), 1)
        start = seq_start(place, ends)

        def tile(masked, kt, dq):
            kstart = kt * bk
            spot, ko = key_spot(kstart, meta_ref[0], J, S, T)
            ko = pl.multiple_of(ko, bk)
            sc = dotf(kt_ref[spot, pl.ds(ko, bk), :], q, NN)
            p = jnp.exp(sc - lse)
            if masked:
                p = jnp.where((rows >= start - kstart) & (rows <= place - kstart), p, 0.0)
            dp = dotf(vt_ref[spot, pl.ds(ko, bk), :], do, NN)
            ds = (p * (dp - delta)).astype(LOW)
            dv_acc[spot, :, pl.ds(ko, bk)] += dotf(do, p.astype(LOW), NT)
            dk_acc[spot, :, pl.ds(ko, bk)] += dotf(q, ds, NT)
            return dq + dotf(kf_ref[spot, :, pl.ds(ko, bk)], ds, NN)

        t0, t1, t2, t3 = tile_range(q0, bq, bk, ends)
        dq = jnp.zeros((HEAD_DIM, bq), F32)
        dq = lax.fori_loop(t2, t3, functools.partial(tile, True), dq)
        dq = lax.fori_loop(t0, t1, functools.partial(tile, True), dq)
        dq = lax.fori_loop(t1, t2, functools.partial(tile, False), dq)
        dq_ref[s, :, pl.ds(qo, bq)] = (dq * 0.125).astype(LOW)
        return 0

    lax.fori_loop(0, J * per, q_tile, 0)
    for e in range(S):
        dk_refs[e][...] = dk_acc[e * J : (e + 1) * J].astype(LOW)
        dv_refs[e][...] = dv_acc[e * J : (e + 1) * J].astype(LOW)


def attn_params(keys):
    return pltpu.CompilerParams(vmem_limit_bytes=(58 if keys > 8192 else 40) * MIB)


def attn_fwd(meta, seq, q, ks, vs, part, bq=512, bk=512):
    J, _, T = q.shape
    S = len(ks)
    return pl.pallas_call(
        functools.partial(fwd_kernel, bq, bk, S, part),
        out_shape=(
            jax.ShapeDtypeStruct((J, HEAD_DIM, T // 2), LOW),
            jax.ShapeDtypeStruct((J, 1, T // 2), F32),
        ),
        in_specs=[M, M] + [V] * (1 + 2 * S),
        out_specs=(V, V),
        scratch_shapes=[
            pltpu.VMEM((S * J, T, HEAD_DIM), LOW),
            pltpu.VMEM((S * J, HEAD_DIM, T), LOW),
        ],
        compiler_params=attn_params(S * J * T),
        cost_estimate=cost(36 * 10**9, 4 * MIB),
        name="attn_fwd",
    )(meta, seq, q, *ks, *vs)


def attn_bwd(meta, seq, q, ks, vs, o, lse, do, bq=512, bk=512):
    J, _, T = q.shape
    S = len(ks)
    block = jax.ShapeDtypeStruct((J, HEAD_DIM, T), LOW)
    out = pl.pallas_call(
        functools.partial(bwd_kernel, bq, bk, S),
        out_shape=[block] * (1 + 2 * S),
        in_specs=[M, M] + [V] * (4 + 2 * S),
        out_specs=[V] * (1 + 2 * S),
        scratch_shapes=[
            pltpu.VMEM((S * J, T, HEAD_DIM), LOW),
            pltpu.VMEM((S * J, HEAD_DIM, T), LOW),
            pltpu.VMEM((S * J, T, HEAD_DIM), LOW),
            pltpu.VMEM((S * J, HEAD_DIM, T), F32),
            pltpu.VMEM((S * J, HEAD_DIM, T), F32),
        ],
        compiler_params=attn_params(S * J * T),
        cost_estimate=cost(10**6, 1000),
        name="attn_bwd",
    )(meta, seq, q, *ks, *vs, o, lse, do)
    return out[0], out[1 : 1 + S], out[1 + S :]


def qkv_kernel(x_ref, gain_ref, bias_ref, w_ref, b_ref, n_ref, q_ref, k_ref, v_ref):
    J = q_ref.shape[0]
    normed = norm_rows(x_ref[...].astype(F32), gain_ref[...], bias_ref[...]).astype(LOW)
    n_ref[...] = normed
    rows = normed.shape[0]
    for i, ref in ((1, k_ref), (2, v_ref), (0, q_ref)):
        made = dotf(normed, w_ref[i], NN)
        if i != 1:
            made = made + b_ref[i // 2][None]
        made = made.astype(LOW)
        if i == 0:
            made = (made * 0.125).astype(LOW)
        ref[...] = made.T.reshape(J, HEAD_DIM, rows)


def qkv(x, gain, bias, w, b):
    T, D = x.shape
    local = w.shape[2]
    J = local // HEAD_DIM
    rows = 256
    row_spec = pl.BlockSpec((rows, D), lambda i: (i, 0))
    head_spec = pl.BlockSpec((J, HEAD_DIM, rows), lambda i: (0, 0, i))
    heads = jax.ShapeDtypeStruct((J, HEAD_DIM, T), LOW)
    return pl.pallas_call(
        qkv_kernel,
        grid=(T // rows,),
        out_shape=(jax.ShapeDtypeStruct((T, D), LOW), heads, heads, heads),
        in_specs=[row_spec, V, V, V, V],
        out_specs=(row_spec, head_spec, head_spec, head_spec),
        compiler_params=pltpu.CompilerParams(vmem_limit_bytes=24 * MIB),
        cost_estimate=cost(6 * T * D * local, 8 * MIB),
        name="norm_qkv",
    )(x, gain[None], bias[None], w, b)


def out_kernel(pos_ref, *refs):
    pieces = refs[:8]
    w_ref, x_ref, b_ref, gain_ref, bias_ref, x1_ref, n2_ref, held = refs[8:]
    i = pl.program_id(0)
    rows = x1_ref.shape[0]

    @pl.when(i == 0)
    def _():
        for r, piece in enumerate(pieces):
            half = piece.shape[1]
            held[pos_ref[r % 4], :, r // 4 * half : (r // 4 + 1) * half] = piece[...]

    lanes = pl.ds(pl.multiple_of(i * rows, rows), rows)
    o = held[:, :, lanes].reshape(-1, rows)
    middle = x_ref[...].astype(F32) + dotf(o, w_ref[...], TN) + b_ref[...]
    x1_ref[...] = middle
    n2_ref[...] = norm_rows(middle, gain_ref[...], bias_ref[...]).astype(LOW)


def out_stage(pos, pieces, w, x, b, gain, bias):
    T, D = x.shape
    local = pieces[0].shape[0]
    rows = 256
    row_spec = pl.BlockSpec((rows, D), lambda i: (i, 0))
    return pl.pallas_call(
        out_kernel,
        grid=(T // rows,),
        out_shape=(jax.ShapeDtypeStruct((T, D), F32), jax.ShapeDtypeStruct((T, D), LOW)),
        in_specs=[M] + [V] * 9 + [row_spec, V, V, V],
        out_specs=(row_spec, row_spec),
        scratch_shapes=[pltpu.VMEM((4, local, T), LOW)],
        compiler_params=pltpu.CompilerParams(vmem_limit_bytes=32 * MIB),
        cost_estimate=cost(2 * T * D * 4 * local, 12 * MIB),
        name="out_norm",
    )(pos, *pieces, w, x, b[None], gain[None], bias[None])


def mlp_kernel(at_ref, n2_ref, dm_ref, wf_ref, wp_ref, b_ref, *refs):
    g_ref, dh_ref, dn2_ref, db_ref = refs[-4:]
    hidden = dotf(n2_ref[...], wf_ref[...], NN) + b_ref[...]
    back = dotf(dm_ref[...], wp_ref[...], NT)
    root = math.sqrt(2.0 / math.pi)
    square = hidden * hidden
    bent = jnp.tanh(root * hidden * (1.0 + 0.044715 * square))
    half = 0.5 * (1.0 + bent)
    g_ref[...] = (hidden * half).astype(LOW)
    slope = half + 0.5 * hidden * (1.0 - bent * bent) * (root * (1.0 + 3 * 0.044715 * square))
    dh = (back * slope).astype(LOW)
    dh_ref[...] = dh
    dn2_ref[...] = dotf(dh, wf_ref[...], NT).astype(LOW)

    @pl.when(pl.program_id(0) == 0)
    def _():
        db_ref[...] = jnp.zeros_like(db_ref)

    db_ref[...] += jnp.sum(dh.astype(F32), axis=0, keepdims=True)


def mlp_stage(at, n2, dm, w_fc, w_proj, b_fc, before=()):
    T, D = n2.shape
    F = w_fc.shape[1]
    rows = 256
    steps = T // 2 // rows
    row_spec = pl.BlockSpec((rows, D), lambda i, at: (at[0] * steps + i, 0))
    hid_spec = pl.BlockSpec((rows, F), lambda i, at: (at[0] * steps + i, 0))
    own_spec = pl.BlockSpec((rows, D), lambda i, at: (i, 0))
    whole = pl.BlockSpec(memory_space=pltpu.VMEM)
    return pl.pallas_call(
        mlp_kernel,
        grid_spec=pltpu.PrefetchScalarGridSpec(
            num_scalar_prefetch=1,
            grid=(steps,),
            in_specs=[row_spec, row_spec, whole, whole, whole]
            + [pl.BlockSpec(memory_space=pl.ANY)] * len(before),
            out_specs=(hid_spec, hid_spec, own_spec, whole),
        ),
        out_shape=(
            jax.ShapeDtypeStruct((T, F), LOW),
            jax.ShapeDtypeStruct((T, F), LOW),
            jax.ShapeDtypeStruct((T // 2, D), LOW),
            jax.ShapeDtypeStruct((1, F), F32),
        ),
        input_output_aliases={6 + i: i for i in range(len(before))},
        compiler_params=pltpu.CompilerParams(vmem_limit_bytes=40 * MIB),
        cost_estimate=cost(3 * T * D * F, 9 * MIB),
        name="feed",
    )(at, n2, dm, w_fc, w_proj, b_fc[None], *before)


def back_kernel(at_ref, own_ref, crossed_ref, x_ref, kept_ref, gain_ref, wide_ref, low_ref, sums_ref):
    grad = own_ref[...].astype(F32) + crossed_ref[...].astype(F32)
    values = x_ref[...].astype(F32)
    centred = values - jnp.mean(values, axis=-1, keepdims=True)
    factor = lax.rsqrt(jnp.mean(centred * centred, axis=-1, keepdims=True) + EPS)
    z = centred * factor
    u = grad * gain_ref[...]
    mean_u = jnp.mean(u, axis=-1, keepdims=True)
    mean_uz = jnp.mean(u * z, axis=-1, keepdims=True)
    made = kept_ref[...].astype(F32) + factor * (u - mean_u - z * mean_uz)
    wide_ref[...] = made
    low = made.astype(LOW)
    low_ref[...] = low

    @pl.when(pl.program_id(0) == 0)
    def _():
        sums_ref[...] = jnp.zeros_like(sums_ref)

    for i, part in enumerate((grad * z, grad, low.astype(F32), kept_ref[...].astype(F32))):
        sums_ref[i : i + 1, :] += jnp.sum(part, axis=0, keepdims=True)


def norm_back(at, own, crossed, x, kept, gain):
    half, D = own.shape
    rows = 256
    steps = half // rows
    spec = pl.BlockSpec((rows, D), lambda i, at: (i, 0))
    from_whole = pl.BlockSpec((rows, D), lambda i, at: (at[0] * steps + i, 0))
    whole = pl.BlockSpec(memory_space=pltpu.VMEM)
    return pl.pallas_call(
        back_kernel,
        grid_spec=pltpu.PrefetchScalarGridSpec(
            num_scalar_prefetch=1,
            grid=(steps,),
            in_specs=[spec, spec, from_whole, spec if kept.shape[0] == half else from_whole, whole],
            out_specs=(spec, spec, whole),
        ),
        out_shape=(
            jax.ShapeDtypeStruct((half, D), F32),
            jax.ShapeDtypeStruct((half, D), LOW),
            jax.ShapeDtypeStruct((4, D), F32),
        ),
        compiler_params=pltpu.CompilerParams(vmem_limit_bytes=24 * MIB),
        cost_estimate=cost(0, 14 * half * D),
        name="norm_back",
    )(at, own, crossed, x, kept, gain[None])


def first_kernel(core_ref, q_ref, k_ref, v_ref, w_ref, keep_ref, send_ref):
    half = keep_ref.shape[0]
    for out, at in ((send_ref, 1 - core_ref[0]), (keep_ref, core_ref[0])):
        lanes = pl.ds(pl.multiple_of(at * half, half), half)
        total = jnp.zeros(out.shape, F32)
        for i, ref in enumerate((q_ref, k_ref, v_ref)):
            total += dotf(ref[:, lanes].T, w_ref[i], NT)
        out[...] = total.astype(LOW)


def first_stage(core, q, k, v, w):
    local, T = q.shape
    D = w.shape[1]
    part = jax.ShapeDtypeStruct((T // 2, D), LOW)
    return pl.pallas_call(
        first_kernel,
        out_shape=(part, part),
        in_specs=[M, V, V, V, V],
        out_specs=(V, V),
        compiler_params=pltpu.CompilerParams(vmem_limit_bytes=24 * MIB),
        cost_estimate=cost(10**6, 1000),
        name="first_grad",
    )(core, q, k, v, w)


def feed_grads_kernel(g_ref, dm_ref, n2_ref, dh_ref, out_ref):
    steps = pl.num_programs(0) // 2
    rows = out_ref.shape[0]
    i = pl.program_id(0)
    lanes = pl.ds(pl.multiple_of(i % steps * rows, rows), rows)

    @pl.when(i < steps)
    def _():
        out_ref[...] = dotf(g_ref[:, lanes], dm_ref[...], TN).astype(LOW)

    @pl.when(i >= steps)
    def _():
        out_ref[...] = dotf(n2_ref[:, lanes], dh_ref[...], TN).astype(LOW)


def feed_grads(g, dm, n2, dh):
    T, F = g.shape
    D = dm.shape[1]
    rows = 256
    return pl.pallas_call(
        feed_grads_kernel,
        grid=((F + D) // rows,),
        out_shape=jax.ShapeDtypeStruct((F + D, D), LOW),
        in_specs=[V] * 4,
        out_specs=pl.BlockSpec((rows, D), lambda i: (i, 0)),
        compiler_params=pltpu.CompilerParams(vmem_limit_bytes=32 * MIB),
        cost_estimate=cost(4 * T * D * F, 12 * MIB),
        name="feed_grads",
    )(g, dm, n2, dh)


def do_kernel(core_ref, own_ref, other_ref, w_ref, one_ref, two_ref, do_ref, grad_ref):
    half = own_ref.shape[0]
    grad = jnp.zeros(grad_ref.shape, F32)
    for ref, at in ((own_ref, core_ref[0]), (other_ref, 1 - core_ref[0])):
        lanes = pl.ds(pl.multiple_of(at * half, half), half)
        do_ref[:, lanes] = dotf(w_ref[...], ref[...], NT).astype(LOW)
        o = jnp.where(at == 0, one_ref[...], two_ref[...])
        grad += dotf(o, ref[...], NN)
    grad_ref[...] = grad.astype(LOW)


def do_stage(core, own, other, w_out, home_one, home_two):
    local, D = w_out.shape
    T = 2 * home_one.shape[1]
    return pl.pallas_call(
        do_kernel,
        out_shape=(jax.ShapeDtypeStruct((local, T), LOW), jax.ShapeDtypeStruct((local, D), LOW)),
        in_specs=[M, V, V, V, V, V],
        out_specs=(V, V),
        compiler_params=pltpu.CompilerParams(vmem_limit_bytes=24 * MIB),
        cost_estimate=cost(4 * T * D * local, 5 * MIB),
        name="heads_grad",
    )(core, own, other, w_out, home_one, home_two)


def grad_kernel(share, spot_ref, dq_ref, dk_ref, dv_ref, own_ref, *refs):
    parts, out_ref = refs[:-1], refs[-1]
    J = dq_ref.shape[0]
    for i, ref in enumerate((dq_ref, dk_ref, dv_ref)):
        total = dotf(ref[spot_ref[4]], own_ref[...], NN)
        for r, part in enumerate(parts):
            lanes = pl.ds(pl.multiple_of(spot_ref[r], share), share)
            for s in range(1, J):
                total += dotf(ref[spot_ref[4 + s], :, lanes], part[s - 1], NN)
        out_ref[i * HEAD_DIM : (i + 1) * HEAD_DIM] = total


def grad_heads(spots, dq, dk, dv, own, parts):
    J, _, T = dq.shape
    D = own.shape[1]
    return pl.pallas_call(
        functools.partial(grad_kernel, parts[0].shape[1]),
        out_shape=jax.ShapeDtypeStruct((3 * HEAD_DIM, D), F32),
        in_specs=[M] + [V] * (4 + len(parts)),
        out_specs=V,
        compiler_params=pltpu.CompilerParams(vmem_limit_bytes=24 * MIB),
        cost_estimate=cost(10**6, 1000),
        name="grad_heads",
    )(spots, dq, dk, dv, own, *parts)


def lay_kernel(S, spot_ref, *refs):
    parts, (qkv_ref, out_ref, held) = refs[:-3], refs[-3:]
    J, depth, _ = held.shape
    wide = parts[0].shape[1]
    few = (parts[0].shape[0] - depth) // S
    for i, part in enumerate(parts):
        jj, gg = spot_ref[2 * i], spot_ref[2 * i + 1]
        held[jj, :, pl.ds(pl.multiple_of(gg * wide, wide), wide)] = part[:depth]
        rest = part[depth:].astype(F32)
        rows = pl.ds(pl.multiple_of((jj * S + gg) * few, few), few)
        for e in range(S):
            out_ref[rows, e * wide : (e + 1) * wide] = rest[e * few : (e + 1) * few]
    for k in range(3):
        rows = [held[h, k * HEAD_DIM : (k + 1) * HEAD_DIM, :] for h in range(J)]
        qkv_ref[k] = jnp.concatenate(rows, 0).astype(F32).T


def lay_blocks(found, J, S):
    parts = [part for _, _, part in found]
    wide = parts[0].shape[1]
    spots = jnp.stack([x for jj, gg, _ in found for x in (jj, gg)]).astype(jnp.int32)
    return pl.pallas_call(
        functools.partial(lay_kernel, S),
        out_shape=(
            jax.ShapeDtypeStruct((3, S * wide, J * HEAD_DIM), F32),
            jax.ShapeDtypeStruct((J * HEAD_DIM, S * wide), F32),
        ),
        in_specs=[M] + [V] * len(parts),
        out_specs=(V, V),
        scratch_shapes=[pltpu.VMEM((J, 3 * HEAD_DIM, S * wide), LOW)],
        compiler_params=pltpu.CompilerParams(vmem_limit_bytes=24 * MIB),
        cost_estimate=cost(0, 6 * MIB),
        name="lay_blocks",
    )(spots, *parts)


def add_kernel(own_ref, other_ref, out_ref):
    out_ref[...] = (own_ref[...].astype(F32) + other_ref[...].astype(F32)).astype(LOW)


def add_low(own, other):
    return pl.pallas_call(
        add_kernel,
        out_shape=jax.ShapeDtypeStruct(own.shape, LOW),
        in_specs=[V, V],
        out_specs=V,
        compiler_params=pltpu.CompilerParams(vmem_limit_bytes=16 * MIB),
        cost_estimate=cost(0, 6 * own.size),
        name="add_low",
    )(own, other)


def feed_out_kernel(core_ref, g_ref, w_ref, kept_ref, sent_ref):
    half = kept_ref.shape[0]
    for out, at in ((sent_ref, 1 - core_ref[0]), (kept_ref, core_ref[0])):
        rows = pl.ds(pl.multiple_of(at * half, half), half)
        out[...] = dotf(g_ref[rows, :], w_ref[...], NN).astype(LOW)


def feed_out(core, g, w):
    T, F = g.shape
    D = w.shape[1]
    part = jax.ShapeDtypeStruct((T // 2, D), LOW)
    return pl.pallas_call(
        feed_out_kernel,
        out_shape=(part, part),
        in_specs=[M, V, V],
        out_specs=(V, V),
        compiler_params=pltpu.CompilerParams(vmem_limit_bytes=24 * MIB),
        cost_estimate=cost(2 * T * F * D, 6 * MIB),
        name="feed_out",
    )(core, g, w)


def widen_kernel(low_ref, first_ref, second_ref):
    steps = pl.num_programs(0) // 2

    @pl.when(pl.program_id(0) < steps)
    def _():
        first_ref[...] = low_ref[...].astype(F32)

    @pl.when(pl.program_id(0) >= steps)
    def _():
        second_ref[...] = low_ref[...].astype(F32)


def widen(low, first):
    rows, D = low.shape
    steps = 4
    block = first // steps
    return pl.pallas_call(
        widen_kernel,
        grid=(2 * steps,),
        out_shape=(jax.ShapeDtypeStruct((first, D), F32), jax.ShapeDtypeStruct((rows - first, D), F32)),
        in_specs=[pl.BlockSpec((block, D), lambda i: (i, 0))],
        out_specs=(
            pl.BlockSpec((block, D), lambda i: (jnp.minimum(i, steps - 1), 0)),
            pl.BlockSpec((block, D), lambda i: (jnp.maximum(i - steps, 0), 0)),
        ),
        compiler_params=pltpu.CompilerParams(vmem_limit_bytes=16 * MIB),
        cost_estimate=cost(0, 12 * MIB),
        name="widen",
    )(low)


def pair_kernel(core_ref, own_ref, other_ref, out_ref):
    half = own_ref.shape[0]
    for ref, at in ((own_ref, core_ref[0]), (other_ref, 1 - core_ref[0])):
        out_ref[pl.ds(pl.multiple_of(at * half, half), half), :] = ref[...]


def lay_pair(core, own, other):
    half, D = own.shape
    return pl.pallas_call(
        pair_kernel,
        out_shape=jax.ShapeDtypeStruct((2 * half, D), own.dtype),
        in_specs=[M, V, V],
        out_specs=V,
        compiler_params=pltpu.CompilerParams(vmem_limit_bytes=16 * MIB),
        cost_estimate=cost(0, 8 * half * D),
        name="lay_pair",
    )(core, own, other)


def shift_dp(value, steps):
    count = lax.axis_size("dp")
    return lax.ppermute(value, "dp", [(i, (i + steps) % count) for i in range(count)])


def shift_group(value, steps, S):
    count = lax.axis_size("dp")
    return lax.ppermute(
        value, "dp", [(i, i // S * S + (i % S + steps) % S) for i in range(count)]
    )


def swap_core(value):
    return lax.ppermute(value, "tensor", [(i, i ^ 1) for i in range(lax.axis_size("tensor"))])


def swap_x(value):
    return lax.ppermute(value, "tensor", [(i, i ^ 2) for i in range(lax.axis_size("tensor"))])


def rows_at(value, start, count):
    return lax.dynamic_slice_in_dim(value, start, count, 0)


def pick(value, index):
    return lax.dynamic_index_in_dim(value, index, 0, keepdims=False)


def gate(value, *before):
    return lax.optimization_barrier((value, *before))[0]


def tied(*values):
    return lax.optimization_barrier(values)


def sum_group(parts, g, S):
    total = pick(parts, g).astype(F32)
    for e in range(1, S):
        total = total + shift_group(pick(parts, (g + e) % S).astype(LOW), e, S).astype(F32)
    return total


def spread_blocks(blocks, j, g, S):
    J = len(blocks)
    found = []
    for s, part in enumerate(blocks):
        found.append(((j - s) % J, g, part))
        for e in range(1, S):
            found.append(((j - s) % J, (g - e) % S, shift_group(part, e, S)))
    return found


def per_device(
    block_input,
    output_grad,
    seq_lengths,
    ln1_gain,
    ln1_bias,
    w_qkv,
    b_qv,
    w_out,
    b_out,
    ln2_gain,
    ln2_bias,
    w_fc,
    b_fc,
    w_proj,
    b_proj,
):
    T, D = block_input.shape
    local = w_qkv.shape[2]
    J = local // HEAD_DIM
    count = lax.axis_size("dp")
    S = count // J
    place = lax.axis_index("dp")
    j, g = place // S, place % S
    tensor = lax.axis_index("tensor")
    core, side = tensor % 2, tensor // 2
    half, share = T // 2, T // 4
    core_at = core[None].astype(jnp.int32)
    meta = g[None].astype(jnp.int32)
    groups = [[S * jj + gg for jj in range(J)] for gg in range(S)]

    def exchange(heads):
        return lax.all_to_all(heads, "dp", 0, 0, tiled=True, axis_index_groups=groups)

    def group(value):
        return [value] + [shift_group(value, e, S) for e in range(1, S)]

    first_low, queries, keys, values = qkv(block_input, ln1_gain, ln1_bias, w_qkv, b_qv)
    k_own, across = tied(exchange(keys), swap_x(w_out))
    ks = group(k_own)
    vs = group(gate(exchange(values), *ks[1:]))
    q_all = exchange(queries)

    pieces = jnp.stack([w_out, swap_core(w_out), across, swap_core(across)])
    order = jnp.stack([tensor ^ r for r in range(4)]).astype(jnp.int32)
    w_out_all = jnp.concatenate([pick(pieces, tensor ^ r) for r in range(4)], 0)

    q_all = gate(q_all, w_out_all)
    o_one, lse_one = attn_fwd(meta, seq_lengths, q_all, ks, vs, 0)
    o_two, lse_two = attn_fwd(meta, seq_lengths, gate(q_all, o_one), ks, vs, 1)
    home_one, o_two = tied(exchange(o_one), o_two)
    home_one = home_one.reshape(local, half)
    home_two, across = tied(exchange(o_two), swap_x(home_one))
    home_two = home_two.reshape(local, half)

    own_quarter = rows_at(first_low, core * half + side * share, share)
    own_quarter = rows_at(first_low, core * half + side * share, share)
    own_quarter = gate(own_quarter, home_two)
    norm_own = lax.all_gather(own_quarter, "dp", axis_index_groups=groups)

    def gather_tensor(value, across):
        return value, swap_core(value), across, swap_core(across)

    o_pieces = gather_tensor(home_one, across) + gather_tensor(home_two, swap_x(home_two))
    middle, second_low = out_stage(order, o_pieces, w_out_all, block_input, b_out, ln2_gain, ln2_bias)
    active_low, hidden_grad, sent, bias_one = mlp_stage(
        1 - core_at, second_low, output_grad, w_fc, w_proj, b_fc
    )
    arrived = swap_core(sent)
    active_low, hidden_grad, kept, bias_two = mlp_stage(
        core_at, second_low, output_grad, w_fc, w_proj, b_fc, (active_low, hidden_grad)
    )
    grad_b_fc = bias_one + bias_two
    second_half = add_low(kept, arrived)
    crossed = swap_x(second_half)
    grad_feed = feed_grads(active_low, output_grad, second_low, hidden_grad)
    feed_part = lax.psum_scatter(grad_feed, "dp", scatter_dimension=0, tiled=True)
    feed_kept, feed_sent = feed_out(core_at, active_low, w_proj)
    rolled = jnp.stack([pick(norm_own, (j + s) % J) for s in range(1, J)])
    crossed = gate(crossed, grad_feed, rolled, feed_kept)
    middle_grad, branch_half, sums_two = norm_back(
        core_at, second_half, crossed, middle, output_grad, ln2_gain
    )
    heads_grad, grad_w_out = do_stage(core_at, branch_half, swap_core(branch_half), w_out, home_one, home_two)
    do_all = exchange(heads_grad.reshape(J, HEAD_DIM, T))
    out_parts = lax.all_to_all(grad_w_out.reshape(count, local // count, D), "dp", 0, 0, tiled=True)

    norm_across = swap_x(gate(rolled, branch_half))

    o_all = jnp.concatenate([o_one, o_two], 2)
    lse = jnp.concatenate([lse_one, lse_two], 2)
    dq, dks, dvs = attn_bwd(meta, seq_lengths, q_all, ks, vs, o_all, lse, do_all)
    dq, dks, dvs, norm_across, out_parts = tied(dq, dks, dvs, norm_across, out_parts)

    norm_parts = [rolled, norm_across, swap_core(rolled), swap_core(norm_across)]

    def regroup(parts):
        return [shift_group(part, -e, S) for e, part in enumerate(parts) if e]

    def total(own, moved):
        for part in moved:
            own = add_low(own, part)
        return own

    q_home, dk_moved = tied(exchange(dq), regroup(dks))
    dk = total(dks[0], dk_moved)
    k_home, dv_moved = tied(exchange(gate(dk, q_home)), regroup(dvs))
    dv = total(dvs[0], dv_moved)
    v_home = exchange(gate(dv, k_home))
    feed_own = add_low(feed_kept, swap_core(gate(feed_sent, q_home)))
    feed_across = swap_x(feed_own)
    q_home, k_home, v_home = (x.reshape(local, T) for x in (q_home, k_home, v_home))

    spots = jnp.stack(
        [
            c * half + d * share
            for c, d in ((core, side), (core, 1 - side), (1 - core, side), (1 - core, 1 - side))
        ]
        + [(j + s) % J for s in range(J)]
    ).astype(jnp.int32)
    head_grad = grad_heads(spots, dq, dk, dv, first_low, norm_parts)
    v_home, head_grad, feed_across, feed_part = tied(v_home, head_grad, feed_across, feed_part)
    grad_feed = lax.all_gather(feed_part, "dp", axis=0, tiled=True)
    kept, sent = first_stage(core_at, q_home, k_home, v_home, w_qkv)
    first_half = add_low(kept, swap_core(sent))
    cut = head_grad.reshape(3 * HEAD_DIM, S, D // S).transpose(1, 0, 2)
    head_grad = sum_group(cut, g, S).astype(LOW)
    grad_w_out = jnp.sum(out_parts.astype(F32), axis=0).astype(LOW)
    block = jnp.concatenate([head_grad] + jnp.split(grad_w_out, S, axis=1), 0)
    blocks = [shift_dp(block, s * S) for s in range(1, J)]

    first_across = gate(swap_x(first_half), *blocks)
    _, input_half, sums_one = norm_back(
        core_at, first_half, first_across, block_input, middle_grad, ln1_gain
    )
    input_grad = lay_pair(core_at, input_half, swap_core(input_half))

    feed_across = gate(feed_across, input_half)
    feed_sum = feed_own.astype(F32) + feed_across.astype(F32)
    middle_half = rows_at(middle, core * half, half)
    output_half = (middle_half + (feed_sum + b_proj)).astype(LOW)
    block_output = lay_pair(core_at, output_half, swap_core(output_half))

    hidden_width = grad_b_fc.shape[1]
    wide_fc = lax.dynamic_update_slice_in_dim(
        jnp.zeros((1, hidden_width * lax.axis_size("tensor")), F32),
        grad_b_fc,
        tensor * hidden_width,
        1,
    ).reshape(-1, D)
    bias_qv = jnp.stack([jnp.sum(q_home.astype(F32), axis=1), jnp.sum(v_home.astype(F32), axis=1)])
    wide_qv = lax.dynamic_update_slice_in_dim(jnp.zeros((2, D), F32), bias_qv, tensor * local, 1)
    early = jnp.concatenate([wide_fc, wide_qv], 0)
    early = early + swap_x(early)
    small = jnp.concatenate([sums_two, sums_one[:2], early], 0)
    small = small + swap_core(small)
    step = 1
    while step < count:
        small = small + lax.ppermute(small, "dp", [(i, i ^ step) for i in range(count)])
        step *= 2
    found = spread_blocks([block, *blocks], j, g, S)
    grad_w_proj, grad_w_fc = widen(grad_feed, w_proj.shape[0])
    grad_w_qkv, grad_w_out = lay_blocks(found, J, S)
    tail = small.shape[0] - 2
    grad_b_qv = lax.dynamic_slice_in_dim(small[tail:], tensor * local, local, 1)
    grad_b_fc = rows_at(small[6:tail].reshape(-1), tensor * hidden_width, hidden_width)
    return (
        block_output,
        input_grad,
        small[4],
        small[5],
        grad_w_qkv,
        grad_b_qv,
        grad_w_out,
        small[2],
        small[0],
        small[1],
        grad_w_fc,
        grad_b_fc,
        grad_w_proj,
        small[3],
    )


def solution(mesh):
    placed = (
        P("dp", None),
        P("dp", None),
        P(),
        P(),
        P(),
        P(None, None, "tensor"),
        P(None, "tensor"),
        P("tensor", None),
        P(),
        P(),
        P(),
        P(None, "tensor"),
        P("tensor"),
        P("tensor", None),
        P(),
    )
    return jax.shard_map(
        per_device,
        mesh=mesh,
        in_specs=placed,
        out_specs=(
            P("dp", None),
            P("dp", None),
            P(),
            P(),
            P(None, None, "tensor"),
            P(None, "tensor"),
            P("tensor", None),
            P(),
            P(),
            P(),
            P(None, "tensor"),
            P("tensor"),
            P("tensor", None),
            P(),
        ),
        check_vma=False,
    )
```

```python
import functools
import math

import jax
import jax.numpy as jnp
from jax import lax
from jax.experimental import pallas as pl
from jax.experimental.pallas import tpu as pltpu
from jax.sharding import PartitionSpec as P

HEAD_DIM = 64
NEG = -1e30
EPS = 1e-05
NN = (((1,), (0,)), ((), ()))
NT = (((1,), (1,)), ((), ()))
TN = (((0,), (0,)), ((), ()))
LOW = jnp.bfloat16
F32 = jnp.float32
MIB = 2**20
LITTLE = 0
V = pl.BlockSpec(memory_space=pltpu.VMEM)
M = pl.BlockSpec(memory_space=pltpu.SMEM)


def dotf(a, b, dims):
    return lax.dot_general(a, b, dims, preferred_element_type=F32)


def norm_rows(values, weight_row, shift_row):
    centred = values - jnp.mean(values, axis=-1, keepdims=True)
    spread = jnp.mean(centred * centred, axis=-1, keepdims=True)
    return centred * lax.rsqrt(spread + EPS) * weight_row + shift_row


def far(value):
    return pltpu.with_memory_space_constraint(value, pltpu.HBM)


def cost(flops, moved):
    return pl.CostEstimate(flops=LITTLE * flops, bytes_accessed=LITTLE * moved, transcendentals=0)


def seq_start(place, ends):
    start = jnp.zeros_like(place)
    for end in ends:
        start = jnp.where(place >= end, end, start)
    return start


def read_ends(seq_ref):
    ends = []
    total = jnp.int32(0)
    for s in range(seq_ref.shape[0] - 1):
        total = total + seq_ref[s]
        ends.append(total)
    return ends


def key_spot(kstart, own, J, S, T):
    block = kstart // T
    distance = lax.rem(own - lax.rem(block, S) + S, S)
    return distance * J + block // S, lax.rem(kstart, T)


def tile_range(q0, bq, bk, ends):
    t0 = seq_start(q0, ends) // bk
    t3 = (q0 + bq + bk - 1) // bk
    t2 = jnp.maximum(q0 // bk, t0)
    t1 = jnp.minimum((seq_start(q0 + bq - 1, ends) + bk - 1) // bk, t2)
    return t0, jnp.maximum(t1, t0), t2, t3


def fill(refs, dst, flip):
    J = refs[0].shape[0]
    for e, ref in enumerate(refs):

        def one(i, _, e=e, ref=ref):
            dst[e * J + i] = ref[i].T if flip else ref[i]
            return 0

        lax.fori_loop(0, J, one, 0)


def fwd_kernel(bq, bk, S, part, meta_ref, seq_ref, q_ref, *refs):
    k_refs, v_refs = refs[:S], refs[S : 2 * S]
    o_ref, lse_ref, kt_ref, vf_ref = refs[2 * S :]
    J, _, T = q_ref.shape
    ends = read_ends(seq_ref)
    fill(k_refs, kt_ref, True)
    fill(v_refs, vf_ref, False)
    per = T // 2 // bq
    rows = lax.broadcasted_iota(jnp.int32, (bk, bq), 0)

    def q_tile(i, _):
        s = i // per
        to = pl.multiple_of(lax.rem(i, per) * bq, bq)
        qo = to + part * (T // 2)
        q0 = (s * S + meta_ref[0]) * T + qo
        q = q_ref[s, :, pl.ds(qo, bq)]
        place = q0 + lax.broadcasted_iota(jnp.int32, (1, bq), 1)
        start = seq_start(place, ends)

        def tile(masked, kt, carry):
            m, l, acc = carry
            kstart = kt * bk
            spot, ko = key_spot(kstart, meta_ref[0], J, S, T)
            ko = pl.multiple_of(ko, bk)
            k = kt_ref[spot, pl.ds(ko, bk), :]
            v = vf_ref[spot, :, pl.ds(ko, bk)]
            sc = dotf(k, q, NN)
            if masked:
                sc = jnp.where((rows >= start - kstart) & (rows <= place - kstart), sc, NEG)
            m2 = jnp.maximum(m, jnp.max(sc, axis=0, keepdims=True))
            p = jnp.exp(sc - m2)
            a = jnp.exp(m - m2)
            l = l * a + jnp.sum(p, axis=0, keepdims=True)
            acc = acc * a + dotf(v, p.astype(LOW), NN)
            return m2, l, acc

        t0, t1, t2, t3 = tile_range(q0, bq, bk, ends)
        c = (jnp.full((1, bq), NEG, F32), jnp.zeros((1, bq), F32), jnp.zeros((HEAD_DIM, bq), F32))
        c = lax.fori_loop(t2, t3, functools.partial(tile, True), c)
        c = lax.fori_loop(t0, t1, functools.partial(tile, True), c)
        m, l, acc = lax.fori_loop(t1, t2, functools.partial(tile, False), c)
        o_ref[s, :, pl.ds(to, bq)] = (acc / l).astype(LOW)
        lse_ref[s, :, pl.ds(to, bq)] = m + jnp.log(l)
        return 0

    lax.fori_loop(0, J * per, q_tile, 0)


def bwd_kernel(bq, bk, S, meta_ref, seq_ref, q_ref, *refs):
    k_refs, v_refs = refs[:S], refs[S : 2 * S]
    o_ref, lse_ref, do_ref, dq_ref = refs[2 * S : 2 * S + 4]
    dk_refs, dv_refs = refs[2 * S + 4 : 3 * S + 4], refs[3 * S + 4 : 4 * S + 4]
    kt_ref, kf_ref, vt_ref, dk_acc, dv_acc = refs[4 * S + 4 :]
    J, _, T = q_ref.shape
    ends = read_ends(seq_ref)
    fill(k_refs, kt_ref, True)
    fill(k_refs, kf_ref, False)
    fill(v_refs, vt_ref, True)
    dk_acc[...] = jnp.zeros_like(dk_acc)
    dv_acc[...] = jnp.zeros_like(dv_acc)
    per = T // bq
    rows = lax.broadcasted_iota(jnp.int32, (bk, bq), 0)

    def q_tile(i, _):
        s = i // per
        qo = pl.multiple_of(lax.rem(i, per) * bq, bq)
        q0 = (s * S + meta_ref[0]) * T + qo
        q = q_ref[s, :, pl.ds(qo, bq)]
        do = do_ref[s, :, pl.ds(qo, bq)]
        lse = lse_ref[s, :, pl.ds(qo, bq)]
        o = o_ref[s, :, pl.ds(qo, bq)].astype(F32)
        delta = jnp.sum(do.astype(F32) * o, axis=0, keepdims=True)
        place = q0 + lax.broadcasted_iota(jnp.int32, (1, bq), 1)
        start = seq_start(place, ends)

        def tile(masked, kt, dq):
            kstart = kt * bk
            spot, ko = key_spot(kstart, meta_ref[0], J, S, T)
            ko = pl.multiple_of(ko, bk)
            sc = dotf(kt_ref[spot, pl.ds(ko, bk), :], q, NN)
            p = jnp.exp(sc - lse)
            if masked:
                p = jnp.where((rows >= start - kstart) & (rows <= place - kstart), p, 0.0)
            dp = dotf(vt_ref[spot, pl.ds(ko, bk), :], do, NN)
            ds = (p * (dp - delta)).astype(LOW)
            dv_acc[spot, :, pl.ds(ko, bk)] += dotf(do, p.astype(LOW), NT)
            dk_acc[spot, :, pl.ds(ko, bk)] += dotf(q, ds, NT)
            return dq + dotf(kf_ref[spot, :, pl.ds(ko, bk)], ds, NN)

        t0, t1, t2, t3 = tile_range(q0, bq, bk, ends)
        dq = jnp.zeros((HEAD_DIM, bq), F32)
        dq = lax.fori_loop(t2, t3, functools.partial(tile, True), dq)
        dq = lax.fori_loop(t0, t1, functools.partial(tile, True), dq)
        dq = lax.fori_loop(t1, t2, functools.partial(tile, False), dq)
        dq_ref[s, :, pl.ds(qo, bq)] = (dq * 0.125).astype(LOW)
        return 0

    lax.fori_loop(0, J * per, q_tile, 0)
    for e in range(S):
        dk_refs[e][...] = dk_acc[e * J : (e + 1) * J].astype(LOW)
        dv_refs[e][...] = dv_acc[e * J : (e + 1) * J].astype(LOW)


def attn_params(keys):
    return pltpu.CompilerParams(vmem_limit_bytes=(58 if keys > 8192 else 24) * MIB)


def attn_fwd(meta, seq, q, ks, vs, part, bq=512, bk=512):
    J, _, T = q.shape
    S = len(ks)
    return pl.pallas_call(
        functools.partial(fwd_kernel, bq, bk, S, part),
        out_shape=(
            jax.ShapeDtypeStruct((J, HEAD_DIM, T // 2), LOW),
            jax.ShapeDtypeStruct((J, 1, T // 2), F32),
        ),
        in_specs=[M, M] + [V] * (1 + 2 * S),
        out_specs=(V, V),
        scratch_shapes=[
            pltpu.VMEM((S * J, T, HEAD_DIM), LOW),
            pltpu.VMEM((S * J, HEAD_DIM, T), LOW),
        ],
        compiler_params=attn_params(S * J * T),
        cost_estimate=cost(36 * 10**9, 4 * MIB),
        name="attn_fwd",
    )(meta, seq, q, *ks, *vs)


def attn_bwd(meta, seq, q, ks, vs, o, lse, do, bq=512, bk=512):
    J, _, T = q.shape
    S = len(ks)
    block = jax.ShapeDtypeStruct((J, HEAD_DIM, T), LOW)
    out = pl.pallas_call(
        functools.partial(bwd_kernel, bq, bk, S),
        out_shape=[block] * (1 + 2 * S),
        in_specs=[M, M] + [V] * (4 + 2 * S),
        out_specs=[V] * (1 + 2 * S),
        scratch_shapes=[
            pltpu.VMEM((S * J, T, HEAD_DIM), LOW),
            pltpu.VMEM((S * J, HEAD_DIM, T), LOW),
            pltpu.VMEM((S * J, T, HEAD_DIM), LOW),
            pltpu.VMEM((S * J, HEAD_DIM, T), F32),
            pltpu.VMEM((S * J, HEAD_DIM, T), F32),
        ],
        compiler_params=attn_params(S * J * T),
        cost_estimate=cost(10**6, 1000),
        name="attn_bwd",
    )(meta, seq, q, *ks, *vs, o, lse, do)
    return out[0], out[1 : 1 + S], out[1 + S :]


def qkv_kernel(x_ref, gain_ref, bias_ref, w_ref, b_ref, n_ref, q_ref, k_ref, v_ref):
    J = q_ref.shape[0]
    normed = norm_rows(x_ref[...].astype(F32), gain_ref[...], bias_ref[...]).astype(LOW)
    n_ref[...] = normed
    rows = normed.shape[0]
    for i, ref in ((1, k_ref), (2, v_ref), (0, q_ref)):
        made = dotf(normed, w_ref[i], NN)
        if i != 1:
            made = made + b_ref[i // 2][None]
        made = made.astype(LOW)
        if i == 0:
            made = (made * 0.125).astype(LOW)
        ref[...] = made.T.reshape(J, HEAD_DIM, rows)


def qkv(x, gain, bias, w, b):
    T, D = x.shape
    local = w.shape[2]
    J = local // HEAD_DIM
    rows = 256
    row_spec = pl.BlockSpec((rows, D), lambda i: (i, 0))
    head_spec = pl.BlockSpec((J, HEAD_DIM, rows), lambda i: (0, 0, i))
    heads = jax.ShapeDtypeStruct((J, HEAD_DIM, T), LOW)
    return pl.pallas_call(
        qkv_kernel,
        grid=(T // rows,),
        out_shape=(pltpu.HBM((T, D), LOW), heads, heads, heads),
        in_specs=[row_spec, V, V, V, V],
        out_specs=(row_spec, head_spec, head_spec, head_spec),
        compiler_params=pltpu.CompilerParams(vmem_limit_bytes=12 * MIB),
        cost_estimate=cost(6 * T * D * local, 8 * MIB),
        name="norm_qkv",
    )(far(x), far(gain[None]), far(bias[None]), far(w), far(b))


def out_kernel(pos_ref, *refs):
    pieces = refs[:8]
    w_ref, x_ref, b_ref, gain_ref, bias_ref, x1_ref, n2_ref, held = refs[8:]
    i = pl.program_id(0)
    rows = x1_ref.shape[0]

    @pl.when(i == 0)
    def _():
        for r, piece in enumerate(pieces):
            half = piece.shape[1]
            held[pos_ref[r % 4], :, r // 4 * half : (r // 4 + 1) * half] = piece[...]

    lanes = pl.ds(pl.multiple_of(i * rows, rows), rows)
    o = held[:, :, lanes].reshape(-1, rows)
    middle = x_ref[...].astype(F32) + dotf(o, w_ref[...], TN) + b_ref[...]
    x1_ref[...] = middle
    n2_ref[...] = norm_rows(middle, gain_ref[...], bias_ref[...]).astype(LOW)


def out_stage(pos, pieces, w, x, b, gain, bias):
    T, D = x.shape
    local = pieces[0].shape[0]
    rows = 256
    row_spec = pl.BlockSpec((rows, D), lambda i: (i, 0))
    return pl.pallas_call(
        out_kernel,
        grid=(T // rows,),
        out_shape=(pltpu.HBM((T, D), F32), jax.ShapeDtypeStruct((T, D), LOW)),
        in_specs=[M] + [V] * 9 + [row_spec, V, V, V],
        out_specs=(row_spec, row_spec),
        scratch_shapes=[pltpu.VMEM((4, local, T), LOW)],
        compiler_params=pltpu.CompilerParams(vmem_limit_bytes=16 * MIB),
        cost_estimate=cost(2 * T * D * 4 * local, 12 * MIB),
        name="out_norm",
    )(pos, *pieces, far(w), far(x), far(b[None]), far(gain[None]), far(bias[None]))


def mlp_kernel(at_ref, n2_ref, dm_ref, wf_ref, wp_ref, b_ref, *refs):
    g_ref, dh_ref, dn2_ref, db_ref = refs[-4:]
    hidden = dotf(n2_ref[...], wf_ref[...], NN) + b_ref[...]
    back = dotf(dm_ref[...], wp_ref[...], NT)
    root = math.sqrt(2.0 / math.pi)
    square = hidden * hidden
    bent = jnp.tanh(root * hidden * (1.0 + 0.044715 * square))
    half = 0.5 * (1.0 + bent)
    g_ref[...] = (hidden * half).astype(LOW)
    slope = half + 0.5 * hidden * (1.0 - bent * bent) * (root * (1.0 + 3 * 0.044715 * square))
    dh = (back * slope).astype(LOW)
    dh_ref[...] = dh
    dn2_ref[...] = dotf(dh, wf_ref[...], NT).astype(LOW)

    @pl.when(pl.program_id(0) == 0)
    def _():
        db_ref[...] = jnp.zeros_like(db_ref)

    db_ref[...] += jnp.sum(dh.astype(F32), axis=0, keepdims=True)


def mlp_stage(at, n2, dm, w_fc, w_proj, b_fc, before=()):
    T, D = n2.shape
    F = w_fc.shape[1]
    rows = 256
    steps = T // 2 // rows
    row_spec = pl.BlockSpec((rows, D), lambda i, at: (at[0] * steps + i, 0))
    hid_spec = pl.BlockSpec((rows, F), lambda i, at: (at[0] * steps + i, 0))
    own_spec = pl.BlockSpec((rows, D), lambda i, at: (i, 0))
    whole = pl.BlockSpec(memory_space=pltpu.VMEM)
    return pl.pallas_call(
        mlp_kernel,
        grid_spec=pltpu.PrefetchScalarGridSpec(
            num_scalar_prefetch=1,
            grid=(steps,),
            in_specs=[row_spec, row_spec, whole, whole, whole]
            + [pl.BlockSpec(memory_space=pl.ANY)] * len(before),
            out_specs=(hid_spec, hid_spec, own_spec, whole),
        ),
        out_shape=(
            jax.ShapeDtypeStruct((T, F), LOW),
            jax.ShapeDtypeStruct((T, F), LOW),
            pltpu.HBM((T // 2, D), LOW),
            jax.ShapeDtypeStruct((1, F), F32),
        ),
        input_output_aliases={6 + i: i for i in range(len(before))},
        compiler_params=pltpu.CompilerParams(vmem_limit_bytes=18 * MIB),
        cost_estimate=cost(3 * T * D * F, 9 * MIB),
        name="feed",
    )(at, n2, dm, w_fc, w_proj, b_fc[None], *before)


def back_kernel(at_ref, own_ref, crossed_ref, x_ref, kept_ref, gain_ref, wide_ref, low_ref, sums_ref):
    grad = own_ref[...].astype(F32) + crossed_ref[...].astype(F32)
    values = x_ref[...].astype(F32)
    centred = values - jnp.mean(values, axis=-1, keepdims=True)
    factor = lax.rsqrt(jnp.mean(centred * centred, axis=-1, keepdims=True) + EPS)
    z = centred * factor
    u = grad * gain_ref[...]
    mean_u = jnp.mean(u, axis=-1, keepdims=True)
    mean_uz = jnp.mean(u * z, axis=-1, keepdims=True)
    made = kept_ref[...].astype(F32) + factor * (u - mean_u - z * mean_uz)
    wide_ref[...] = made
    low = made.astype(LOW)
    low_ref[...] = low

    @pl.when(pl.program_id(0) == 0)
    def _():
        sums_ref[...] = jnp.zeros_like(sums_ref)

    for i, part in enumerate((grad * z, grad, low.astype(F32), kept_ref[...].astype(F32))):
        sums_ref[i : i + 1, :] += jnp.sum(part, axis=0, keepdims=True)


def norm_back(at, own, crossed, x, kept, gain):
    half, D = own.shape
    rows = 256
    steps = half // rows
    spec = pl.BlockSpec((rows, D), lambda i, at: (i, 0))
    from_whole = pl.BlockSpec((rows, D), lambda i, at: (at[0] * steps + i, 0))
    whole = pl.BlockSpec(memory_space=pltpu.VMEM)
    return pl.pallas_call(
        back_kernel,
        grid_spec=pltpu.PrefetchScalarGridSpec(
            num_scalar_prefetch=1,
            grid=(steps,),
            in_specs=[spec, spec, from_whole, spec if kept.shape[0] == half else from_whole, whole],
            out_specs=(spec, spec, whole),
        ),
        out_shape=(
            jax.ShapeDtypeStruct((half, D), F32),
            jax.ShapeDtypeStruct((half, D), LOW),
            jax.ShapeDtypeStruct((4, D), F32),
        ),
        compiler_params=pltpu.CompilerParams(vmem_limit_bytes=12 * MIB),
        cost_estimate=cost(0, 14 * half * D),
        name="norm_back",
    )(at, own, crossed, far(x), kept, gain[None])


def first_kernel(core_ref, q_ref, k_ref, v_ref, w_ref, keep_ref, send_ref):
    half = keep_ref.shape[0]
    for out, at in ((send_ref, 1 - core_ref[0]), (keep_ref, core_ref[0])):
        lanes = pl.ds(pl.multiple_of(at * half, half), half)
        total = jnp.zeros(out.shape, F32)
        for i, ref in enumerate((q_ref, k_ref, v_ref)):
            total += dotf(ref[:, lanes].T, w_ref[i], NT)
        out[...] = total.astype(LOW)


def first_stage(core, q, k, v, w):
    local, T = q.shape
    D = w.shape[1]
    part = jax.ShapeDtypeStruct((T // 2, D), LOW)
    return pl.pallas_call(
        first_kernel,
        out_shape=(part, part),
        in_specs=[M, V, V, V, V],
        out_specs=(V, V),
        compiler_params=pltpu.CompilerParams(vmem_limit_bytes=10 * MIB),
        cost_estimate=cost(10**6, 1000),
        name="first_grad",
    )(core, q, k, v, w)


def feed_grads_kernel(g_ref, dm_ref, n2_ref, dh_ref, out_ref):
    steps = pl.num_programs(0) // 2
    rows = out_ref.shape[0]
    i = pl.program_id(0)
    lanes = pl.ds(pl.multiple_of(i % steps * rows, rows), rows)

    @pl.when(i < steps)
    def _():
        out_ref[...] = dotf(g_ref[:, lanes], dm_ref[...], TN).astype(LOW)

    @pl.when(i >= steps)
    def _():
        out_ref[...] = dotf(n2_ref[:, lanes], dh_ref[...], TN).astype(LOW)


def feed_grads(g, dm, n2, dh):
    T, F = g.shape
    D = dm.shape[1]
    rows = 256
    return pl.pallas_call(
        feed_grads_kernel,
        grid=((F + D) // rows,),
        out_shape=pltpu.HBM((F + D, D), LOW),
        in_specs=[V] * 4,
        out_specs=pl.BlockSpec((rows, D), lambda i: (i, 0)),
        compiler_params=pltpu.CompilerParams(vmem_limit_bytes=10 * MIB),
        cost_estimate=cost(4 * T * D * F, 12 * MIB),
        name="feed_grads",
    )(g, dm, n2, dh)


def do_kernel(core_ref, own_ref, other_ref, w_ref, one_ref, two_ref, do_ref, grad_ref):
    half = own_ref.shape[0]
    grad = jnp.zeros(grad_ref.shape, F32)
    for ref, at in ((own_ref, core_ref[0]), (other_ref, 1 - core_ref[0])):
        lanes = pl.ds(pl.multiple_of(at * half, half), half)
        do_ref[:, lanes] = dotf(w_ref[...], ref[...], NT).astype(LOW)
        o = jnp.where(at == 0, one_ref[...], two_ref[...])
        grad += dotf(o, ref[...], NN)
    grad_ref[...] = grad.astype(LOW)


def do_stage(core, own, other, w_out, home_one, home_two):
    local, D = w_out.shape
    T = 2 * home_one.shape[1]
    return pl.pallas_call(
        do_kernel,
        out_shape=(jax.ShapeDtypeStruct((local, T), LOW), jax.ShapeDtypeStruct((local, D), LOW)),
        in_specs=[M, V, V, V, V, V],
        out_specs=(V, V),
        compiler_params=pltpu.CompilerParams(vmem_limit_bytes=8 * MIB),
        cost_estimate=cost(4 * T * D * local, 5 * MIB),
        name="heads_grad",
    )(core, own, other, w_out, home_one, home_two)


def grad_kernel(share, spot_ref, dq_ref, dk_ref, dv_ref, own_ref, *refs):
    parts, out_ref = refs[:-1], refs[-1]
    J = dq_ref.shape[0]
    for i, ref in enumerate((dq_ref, dk_ref, dv_ref)):
        total = dotf(ref[spot_ref[4]], own_ref[...], NN)
        for r, part in enumerate(parts):
            lanes = pl.ds(pl.multiple_of(spot_ref[r], share), share)
            for s in range(1, J):
                total += dotf(ref[spot_ref[4 + s], :, lanes], part[s - 1], NN)
        out_ref[i * HEAD_DIM : (i + 1) * HEAD_DIM] = total


def grad_heads(spots, dq, dk, dv, own, parts):
    J, _, T = dq.shape
    D = own.shape[1]
    return pl.pallas_call(
        functools.partial(grad_kernel, parts[0].shape[1]),
        out_shape=jax.ShapeDtypeStruct((3 * HEAD_DIM, D), F32),
        in_specs=[M] + [V] * (4 + len(parts)),
        out_specs=V,
        compiler_params=pltpu.CompilerParams(vmem_limit_bytes=12 * MIB),
        cost_estimate=cost(10**6, 1000),
        name="grad_heads",
    )(spots, dq, dk, dv, own, *parts)


def lay_kernel(S, spot_ref, *refs):
    parts, (qkv_ref, out_ref, held) = refs[:-3], refs[-3:]
    J, depth, _ = held.shape
    wide = parts[0].shape[1]
    few = (parts[0].shape[0] - depth) // S
    for i, part in enumerate(parts):
        jj, gg = spot_ref[2 * i], spot_ref[2 * i + 1]
        held[jj, :, pl.ds(pl.multiple_of(gg * wide, wide), wide)] = part[:depth]
        rest = part[depth:].astype(F32)
        rows = pl.ds(pl.multiple_of((jj * S + gg) * few, few), few)
        for e in range(S):
            out_ref[rows, e * wide : (e + 1) * wide] = rest[e * few : (e + 1) * few]
    for k in range(3):
        rows = [held[h, k * HEAD_DIM : (k + 1) * HEAD_DIM, :] for h in range(J)]
        qkv_ref[k] = jnp.concatenate(rows, 0).astype(F32).T


def lay_blocks(found, J, S):
    parts = [part for _, _, part in found]
    wide = parts[0].shape[1]
    spots = jnp.stack([x for jj, gg, _ in found for x in (jj, gg)]).astype(jnp.int32)
    return pl.pallas_call(
        functools.partial(lay_kernel, S),
        out_shape=(
            jax.ShapeDtypeStruct((3, S * wide, J * HEAD_DIM), F32),
            jax.ShapeDtypeStruct((J * HEAD_DIM, S * wide), F32),
        ),
        in_specs=[M] + [V] * len(parts),
        out_specs=(V, V),
        scratch_shapes=[pltpu.VMEM((J, 3 * HEAD_DIM, S * wide), LOW)],
        compiler_params=pltpu.CompilerParams(vmem_limit_bytes=12 * MIB),
        cost_estimate=cost(0, 6 * MIB),
        name="lay_blocks",
    )(spots, *parts)


def add_kernel(own_ref, other_ref, out_ref):
    out_ref[...] = (own_ref[...].astype(F32) + other_ref[...].astype(F32)).astype(LOW)


def add_low(own, other):
    return pl.pallas_call(
        add_kernel,
        out_shape=jax.ShapeDtypeStruct(own.shape, LOW),
        in_specs=[V, V],
        out_specs=V,
        compiler_params=pltpu.CompilerParams(vmem_limit_bytes=6 * MIB),
        cost_estimate=cost(0, 6 * own.size),
        name="add_low",
    )(own, other)


def feed_out_kernel(core_ref, g_ref, w_ref, kept_ref, sent_ref):
    half = kept_ref.shape[0]
    for out, at in ((sent_ref, 1 - core_ref[0]), (kept_ref, core_ref[0])):
        rows = pl.ds(pl.multiple_of(at * half, half), half)
        out[...] = dotf(g_ref[rows, :], w_ref[...], NN).astype(LOW)


def feed_out(core, g, w):
    T, F = g.shape
    D = w.shape[1]
    part = jax.ShapeDtypeStruct((T // 2, D), LOW)
    return pl.pallas_call(
        feed_out_kernel,
        out_shape=(part, part),
        in_specs=[M, V, V],
        out_specs=(V, V),
        compiler_params=pltpu.CompilerParams(vmem_limit_bytes=8 * MIB),
        cost_estimate=cost(2 * T * F * D, 6 * MIB),
        name="feed_out",
    )(core, g, w)


def widen_kernel(low_ref, first_ref, second_ref):
    steps = pl.num_programs(0) // 2

    @pl.when(pl.program_id(0) < steps)
    def _():
        first_ref[...] = low_ref[...].astype(F32)

    @pl.when(pl.program_id(0) >= steps)
    def _():
        second_ref[...] = low_ref[...].astype(F32)


def widen(low, first):
    rows, D = low.shape
    steps = 4
    block = first // steps
    return pl.pallas_call(
        widen_kernel,
        grid=(2 * steps,),
        out_shape=(jax.ShapeDtypeStruct((first, D), F32), jax.ShapeDtypeStruct((rows - first, D), F32)),
        in_specs=[pl.BlockSpec((block, D), lambda i: (i, 0))],
        out_specs=(
            pl.BlockSpec((block, D), lambda i: (jnp.minimum(i, steps - 1), 0)),
            pl.BlockSpec((block, D), lambda i: (jnp.maximum(i - steps, 0), 0)),
        ),
        compiler_params=pltpu.CompilerParams(vmem_limit_bytes=8 * MIB),
        cost_estimate=cost(0, 12 * MIB),
        name="widen",
    )(low)


def pair_kernel(core_ref, own_ref, other_ref, out_ref):
    half = own_ref.shape[0]
    for ref, at in ((own_ref, core_ref[0]), (other_ref, 1 - core_ref[0])):
        out_ref[pl.ds(pl.multiple_of(at * half, half), half), :] = ref[...]


def lay_pair(core, own, other):
    half, D = own.shape
    return pl.pallas_call(
        pair_kernel,
        out_shape=jax.ShapeDtypeStruct((2 * half, D), own.dtype),
        in_specs=[M, V, V],
        out_specs=V,
        compiler_params=pltpu.CompilerParams(vmem_limit_bytes=6 * MIB),
        cost_estimate=cost(0, 8 * half * D),
        name="lay_pair",
    )(core, own, other)


def shift_dp(value, steps):
    count = lax.axis_size("dp")
    return lax.ppermute(value, "dp", [(i, (i + steps) % count) for i in range(count)])


def shift_group(value, steps, S):
    count = lax.axis_size("dp")
    return lax.ppermute(
        value, "dp", [(i, i // S * S + (i % S + steps) % S) for i in range(count)]
    )


def swap_core(value):
    return lax.ppermute(value, "tensor", [(i, i ^ 1) for i in range(lax.axis_size("tensor"))])


def swap_x(value):
    return lax.ppermute(value, "tensor", [(i, i ^ 2) for i in range(lax.axis_size("tensor"))])


def rows_at(value, start, count):
    return lax.dynamic_slice_in_dim(value, start, count, 0)


def pick(value, index):
    return lax.dynamic_index_in_dim(value, index, 0, keepdims=False)


def gate(value, *before):
    return lax.optimization_barrier((value, *before))[0]


def tied(*values):
    return lax.optimization_barrier(values)


def sum_group(parts, g, S):
    total = pick(parts, g).astype(F32)
    for e in range(1, S):
        total = total + shift_group(pick(parts, (g + e) % S).astype(LOW), e, S).astype(F32)
    return total


def spread_blocks(blocks, j, g, S):
    J = len(blocks)
    found = []
    for s, part in enumerate(blocks):
        found.append(((j - s) % J, g, part))
        for e in range(1, S):
            found.append(((j - s) % J, (g - e) % S, shift_group(part, e, S)))
    return found


def per_device(
    block_input,
    output_grad,
    seq_lengths,
    ln1_gain,
    ln1_bias,
    w_qkv,
    b_qv,
    w_out,
    b_out,
    ln2_gain,
    ln2_bias,
    w_fc,
    b_fc,
    w_proj,
    b_proj,
):
    T, D = block_input.shape
    local = w_qkv.shape[2]
    J = local // HEAD_DIM
    count = lax.axis_size("dp")
    S = count // J
    place = lax.axis_index("dp")
    j, g = place // S, place % S
    tensor = lax.axis_index("tensor")
    core, side = tensor % 2, tensor // 2
    half, share = T // 2, T // 4
    core_at = core[None].astype(jnp.int32)
    meta = g[None].astype(jnp.int32)
    groups = [[S * jj + gg for jj in range(J)] for gg in range(S)]

    def exchange(heads):
        return lax.all_to_all(heads, "dp", 0, 0, tiled=True, axis_index_groups=groups)

    def group(value):
        return [value] + [shift_group(value, e, S) for e in range(1, S)]

    first_low, queries, keys, values = qkv(block_input, ln1_gain, ln1_bias, w_qkv, b_qv)
    k_own, across = tied(exchange(keys), swap_x(w_out))
    ks = group(k_own)
    vs = group(gate(exchange(values), *ks[1:]))
    q_all = exchange(queries)

    pieces = jnp.stack([w_out, swap_core(w_out), across, swap_core(across)])
    order = jnp.stack([tensor ^ r for r in range(4)]).astype(jnp.int32)
    w_out_all = jnp.concatenate([pick(pieces, tensor ^ r) for r in range(4)], 0)

    q_all = gate(q_all, w_out_all)
    o_one, lse_one = attn_fwd(meta, seq_lengths, q_all, ks, vs, 0)
    o_two, lse_two = attn_fwd(meta, seq_lengths, gate(q_all, o_one), ks, vs, 1)
    home_one, o_two = tied(exchange(o_one), o_two)
    home_one = home_one.reshape(local, half)
    home_two, across = tied(exchange(o_two), swap_x(home_one))
    home_two = home_two.reshape(local, half)

    own_quarter = rows_at(first_low, core * half + side * share, share)
    own_quarter = rows_at(first_low, core * half + side * share, share)
    own_quarter = gate(own_quarter, home_two)
    norm_own = lax.all_gather(own_quarter, "dp", axis_index_groups=groups)

    def gather_tensor(value, across):
        return value, swap_core(value), across, swap_core(across)

    o_pieces = gather_tensor(home_one, across) + gather_tensor(home_two, swap_x(home_two))
    middle, second_low = out_stage(order, o_pieces, w_out_all, block_input, b_out, ln2_gain, ln2_bias)
    active_low, hidden_grad, sent, bias_one = mlp_stage(
        1 - core_at, second_low, output_grad, w_fc, w_proj, b_fc
    )
    arrived = swap_core(sent)
    active_low, hidden_grad, kept, bias_two = mlp_stage(
        core_at, second_low, output_grad, w_fc, w_proj, b_fc, (active_low, hidden_grad)
    )
    grad_b_fc = bias_one + bias_two
    second_half = add_low(kept, arrived)
    crossed = swap_x(second_half)
    grad_feed = feed_grads(active_low, output_grad, second_low, hidden_grad)
    feed_part = lax.psum_scatter(grad_feed, "dp", scatter_dimension=0, tiled=True)
    feed_kept, feed_sent = feed_out(core_at, active_low, w_proj)
    rolled = jnp.stack([pick(norm_own, (j + s) % J) for s in range(1, J)])
    crossed = gate(crossed, grad_feed, rolled, feed_kept)
    middle_grad, branch_half, sums_two = norm_back(
        core_at, second_half, crossed, middle, output_grad, ln2_gain
    )
    heads_grad, grad_w_out = do_stage(core_at, branch_half, swap_core(branch_half), w_out, home_one, home_two)
    do_all = exchange(heads_grad.reshape(J, HEAD_DIM, T))
    out_parts = lax.all_to_all(grad_w_out.reshape(count, local // count, D), "dp", 0, 0, tiled=True)

    norm_across = swap_x(gate(rolled, branch_half))

    o_all = jnp.concatenate([o_one, o_two], 2)
    lse = jnp.concatenate([lse_one, lse_two], 2)
    dq, dks, dvs = attn_bwd(meta, seq_lengths, q_all, ks, vs, o_all, lse, do_all)
    dq, dks, dvs, norm_across, out_parts = tied(dq, dks, dvs, norm_across, out_parts)

    norm_parts = [rolled, norm_across, swap_core(rolled), swap_core(norm_across)]

    def regroup(parts):
        return [shift_group(part, -e, S) for e, part in enumerate(parts) if e]

    def total(own, moved):
        for part in moved:
            own = add_low(own, part)
        return own

    q_home, dk_moved = tied(exchange(dq), regroup(dks))
    dk = total(dks[0], dk_moved)
    k_home, dv_moved = tied(exchange(gate(dk, q_home)), regroup(dvs))
    dv = total(dvs[0], dv_moved)
    v_home = exchange(gate(dv, k_home))
    feed_own = add_low(feed_kept, swap_core(gate(feed_sent, q_home)))
    feed_across = swap_x(feed_own)
    q_home, k_home, v_home = (x.reshape(local, T) for x in (q_home, k_home, v_home))

    spots = jnp.stack(
        [
            c * half + d * share
            for c, d in ((core, side), (core, 1 - side), (1 - core, side), (1 - core, 1 - side))
        ]
        + [(j + s) % J for s in range(J)]
    ).astype(jnp.int32)
    head_grad = grad_heads(spots, dq, dk, dv, first_low, norm_parts)
    v_home, head_grad, feed_across, feed_part = tied(v_home, head_grad, feed_across, feed_part)
    grad_feed = lax.all_gather(feed_part, "dp", axis=0, tiled=True)
    kept, sent = first_stage(core_at, q_home, k_home, v_home, w_qkv)
    first_half = add_low(kept, swap_core(sent))
    cut = head_grad.reshape(3 * HEAD_DIM, S, D // S).transpose(1, 0, 2)
    head_grad = sum_group(cut, g, S).astype(LOW)
    grad_w_out = jnp.sum(out_parts.astype(F32), axis=0).astype(LOW)
    block = jnp.concatenate([head_grad] + jnp.split(grad_w_out, S, axis=1), 0)
    blocks = [shift_dp(block, s * S) for s in range(1, J)]

    first_across = gate(swap_x(first_half), *blocks)
    _, input_half, sums_one = norm_back(
        core_at, first_half, first_across, block_input, middle_grad, ln1_gain
    )
    input_grad = lay_pair(core_at, input_half, swap_core(input_half))

    feed_across = gate(feed_across, block)
    feed_sum = feed_own.astype(F32) + feed_across.astype(F32)
    middle_half = rows_at(middle, core * half, half)
    output_half = (middle_half + (feed_sum + b_proj)).astype(LOW)
    block_output = lay_pair(core_at, output_half, swap_core(output_half))

    hidden_width = grad_b_fc.shape[1]
    wide_fc = lax.dynamic_update_slice_in_dim(
        jnp.zeros((1, hidden_width * lax.axis_size("tensor")), F32),
        grad_b_fc,
        tensor * hidden_width,
        1,
    ).reshape(-1, D)
    bias_qv = jnp.stack([jnp.sum(q_home.astype(F32), axis=1), jnp.sum(v_home.astype(F32), axis=1)])
    wide_qv = lax.dynamic_update_slice_in_dim(jnp.zeros((2, D), F32), bias_qv, tensor * local, 1)
    early = jnp.concatenate([wide_fc, wide_qv], 0)
    early = early + swap_x(early)
    small = jnp.concatenate([sums_two, sums_one[:2], early], 0)
    small = small + swap_core(small)
    step = 1
    while step < count:
        small = small + lax.ppermute(small, "dp", [(i, i ^ step) for i in range(count)])
        if step == 2:
            small, input_grad, block_output = tied(small, input_grad, block_output)
        step *= 2
    found = spread_blocks([block, *blocks], j, g, S)
    grad_w_proj, grad_w_fc = widen(grad_feed, w_proj.shape[0])
    grad_w_qkv, grad_w_out = lay_blocks(found, J, S)
    tail = small.shape[0] - 2
    grad_b_qv = lax.dynamic_slice_in_dim(small[tail:], tensor * local, local, 1)
    grad_b_fc = rows_at(small[6:tail].reshape(-1), tensor * hidden_width, hidden_width)
    return (
        block_output,
        input_grad,
        small[4],
        small[5],
        grad_w_qkv,
        grad_b_qv,
        grad_w_out,
        small[2],
        small[0],
        small[1],
        grad_w_fc,
        grad_b_fc,
        grad_w_proj,
        small[3],
    )


def solution(mesh):
    placed = (
        P("dp", None),
        P("dp", None),
        P(),
        P(),
        P(),
        P(None, None, "tensor"),
        P(None, "tensor"),
        P("tensor", None),
        P(),
        P(),
        P(),
        P(None, "tensor"),
        P("tensor"),
        P("tensor", None),
        P(),
    )
    return jax.shard_map(
        per_device,
        mesh=mesh,
        in_specs=placed,
        out_specs=(
            P("dp", None),
            P("dp", None),
            P(),
            P(),
            P(None, None, "tensor"),
            P(None, "tensor"),
            P("tensor", None),
            P(),
            P(),
            P(),
            P(None, "tensor"),
            P("tensor"),
            P("tensor", None),
            P(),
        ),
        check_vma=False,
    )
```

```python
import functools
import math

import jax
import jax.numpy as jnp
from jax import lax
from jax.experimental import pallas as pl
from jax.experimental.pallas import tpu as pltpu
from jax.sharding import PartitionSpec as P

HEAD_DIM = 64
NEG = -1e30
EPS = 1e-05
NN = (((1,), (0,)), ((), ()))
NT = (((1,), (1,)), ((), ()))
TN = (((0,), (0,)), ((), ()))
LOW = jnp.bfloat16
F32 = jnp.float32
MIB = 2**20
LITTLE = 0
V = pl.BlockSpec(memory_space=pltpu.VMEM)
M = pl.BlockSpec(memory_space=pltpu.SMEM)


def dotf(a, b, dims):
    return lax.dot_general(a, b, dims, preferred_element_type=F32)


def norm_rows(values, weight_row, shift_row):
    centred = values - jnp.mean(values, axis=-1, keepdims=True)
    spread = jnp.mean(centred * centred, axis=-1, keepdims=True)
    return centred * lax.rsqrt(spread + EPS) * weight_row + shift_row


def far(value):
    return pltpu.with_memory_space_constraint(value, pltpu.HBM)


def cost(flops, moved):
    return pl.CostEstimate(flops=LITTLE * flops, bytes_accessed=LITTLE * moved, transcendentals=0)


def seq_start(place, ends):
    start = jnp.zeros_like(place)
    for end in ends:
        start = jnp.where(place >= end, end, start)
    return start


def read_ends(seq_ref):
    ends = []
    total = jnp.int32(0)
    for s in range(seq_ref.shape[0] - 1):
        total = total + seq_ref[s]
        ends.append(total)
    return ends


def key_spot(kstart, own, J, S, T):
    block = kstart // T
    distance = lax.rem(own - lax.rem(block, S) + S, S)
    return distance * J + block // S, lax.rem(kstart, T)


def tile_range(q0, bq, bk, ends):
    t0 = seq_start(q0, ends) // bk
    t3 = (q0 + bq + bk - 1) // bk
    t2 = jnp.maximum(q0 // bk, t0)
    t1 = jnp.minimum((seq_start(q0 + bq - 1, ends) + bk - 1) // bk, t2)
    return t0, jnp.maximum(t1, t0), t2, t3


def fill(refs, dst, flip):
    J = refs[0].shape[0]
    for e, ref in enumerate(refs):

        def one(i, _, e=e, ref=ref):
            dst[e * J + i] = ref[i].T if flip else ref[i]
            return 0

        lax.fori_loop(0, J, one, 0)


def fwd_kernel(bq, bk, S, part, meta_ref, seq_ref, q_ref, *refs):
    k_refs, v_refs = refs[:S], refs[S : 2 * S]
    o_ref, lse_ref, kt_ref, vf_ref = refs[2 * S :]
    J, _, T = q_ref.shape
    ends = read_ends(seq_ref)
    fill(k_refs, kt_ref, True)
    fill(v_refs, vf_ref, False)
    per = T // 2 // bq
    rows = lax.broadcasted_iota(jnp.int32, (bk, bq), 0)

    def q_tile(i, _):
        s = i // per
        to = pl.multiple_of(lax.rem(i, per) * bq, bq)
        qo = to + part * (T // 2)
        q0 = (s * S + meta_ref[0]) * T + qo
        q = q_ref[s, :, pl.ds(qo, bq)]
        place = q0 + lax.broadcasted_iota(jnp.int32, (1, bq), 1)
        start = seq_start(place, ends)

        def tile(masked, kt, carry):
            m, l, acc = carry
            kstart = kt * bk
            spot, ko = key_spot(kstart, meta_ref[0], J, S, T)
            ko = pl.multiple_of(ko, bk)
            k = kt_ref[spot, pl.ds(ko, bk), :]
            v = vf_ref[spot, :, pl.ds(ko, bk)]
            sc = dotf(k, q, NN)
            if masked:
                sc = jnp.where((rows >= start - kstart) & (rows <= place - kstart), sc, NEG)
            m2 = jnp.maximum(m, jnp.max(sc, axis=0, keepdims=True))
            p = jnp.exp(sc - m2)
            a = jnp.exp(m - m2)
            l = l * a + jnp.sum(p, axis=0, keepdims=True)
            acc = acc * a + dotf(v, p.astype(LOW), NN)
            return m2, l, acc

        t0, t1, t2, t3 = tile_range(q0, bq, bk, ends)
        c = (jnp.full((1, bq), NEG, F32), jnp.zeros((1, bq), F32), jnp.zeros((HEAD_DIM, bq), F32))
        c = lax.fori_loop(t2, t3, functools.partial(tile, True), c)
        c = lax.fori_loop(t0, t1, functools.partial(tile, True), c)
        m, l, acc = lax.fori_loop(t1, t2, functools.partial(tile, False), c)
        o_ref[s, :, pl.ds(to, bq)] = (acc / l).astype(LOW)
        lse_ref[s, :, pl.ds(to, bq)] = m + jnp.log(l)
        return 0

    lax.fori_loop(0, J * per, q_tile, 0)


def bwd_kernel(bq, bk, S, meta_ref, seq_ref, q_ref, *refs):
    k_refs, v_refs = refs[:S], refs[S : 2 * S]
    o_ref, lse_ref, do_ref, dq_ref = refs[2 * S : 2 * S + 4]
    dk_refs, dv_refs = refs[2 * S + 4 : 3 * S + 4], refs[3 * S + 4 : 4 * S + 4]
    kt_ref, kf_ref, vt_ref, dk_acc, dv_acc = refs[4 * S + 4 :]
    J, _, T = q_ref.shape
    ends = read_ends(seq_ref)
    fill(k_refs, kt_ref, True)
    fill(k_refs, kf_ref, False)
    fill(v_refs, vt_ref, True)
    dk_acc[...] = jnp.zeros_like(dk_acc)
    dv_acc[...] = jnp.zeros_like(dv_acc)
    per = T // bq
    rows = lax.broadcasted_iota(jnp.int32, (bk, bq), 0)

    def q_tile(i, _):
        s = i // per
        qo = pl.multiple_of(lax.rem(i, per) * bq, bq)
        q0 = (s * S + meta_ref[0]) * T + qo
        q = q_ref[s, :, pl.ds(qo, bq)]
        do = do_ref[s, :, pl.ds(qo, bq)]
        lse = lse_ref[s, :, pl.ds(qo, bq)]
        o = o_ref[s, :, pl.ds(qo, bq)].astype(F32)
        delta = jnp.sum(do.astype(F32) * o, axis=0, keepdims=True)
        place = q0 + lax.broadcasted_iota(jnp.int32, (1, bq), 1)
        start = seq_start(place, ends)

        def tile(masked, kt, dq):
            kstart = kt * bk
            spot, ko = key_spot(kstart, meta_ref[0], J, S, T)
            ko = pl.multiple_of(ko, bk)
            sc = dotf(kt_ref[spot, pl.ds(ko, bk), :], q, NN)
            p = jnp.exp(sc - lse)
            if masked:
                p = jnp.where((rows >= start - kstart) & (rows <= place - kstart), p, 0.0)
            dp = dotf(vt_ref[spot, pl.ds(ko, bk), :], do, NN)
            ds = (p * (dp - delta)).astype(LOW)
            dv_acc[spot, :, pl.ds(ko, bk)] += dotf(do, p.astype(LOW), NT)
            dk_acc[spot, :, pl.ds(ko, bk)] += dotf(q, ds, NT)
            return dq + dotf(kf_ref[spot, :, pl.ds(ko, bk)], ds, NN)

        t0, t1, t2, t3 = tile_range(q0, bq, bk, ends)
        dq = jnp.zeros((HEAD_DIM, bq), F32)
        dq = lax.fori_loop(t2, t3, functools.partial(tile, True), dq)
        dq = lax.fori_loop(t0, t1, functools.partial(tile, True), dq)
        dq = lax.fori_loop(t1, t2, functools.partial(tile, False), dq)
        dq_ref[s, :, pl.ds(qo, bq)] = (dq * 0.125).astype(LOW)
        return 0

    lax.fori_loop(0, J * per, q_tile, 0)
    for e in range(S):
        dk_refs[e][...] = dk_acc[e * J : (e + 1) * J].astype(LOW)
        dv_refs[e][...] = dv_acc[e * J : (e + 1) * J].astype(LOW)


def attn_params(keys):
    return pltpu.CompilerParams(vmem_limit_bytes=(58 if keys > 8192 else 24) * MIB)


def attn_fwd(meta, seq, q, ks, vs, part, bq=512, bk=512):
    J, _, T = q.shape
    S = len(ks)
    return pl.pallas_call(
        functools.partial(fwd_kernel, bq, bk, S, part),
        out_shape=(
            jax.ShapeDtypeStruct((J, HEAD_DIM, T // 2), LOW),
            jax.ShapeDtypeStruct((J, 1, T // 2), F32),
        ),
        in_specs=[M, M] + [V] * (1 + 2 * S),
        out_specs=(V, V),
        scratch_shapes=[
            pltpu.VMEM((S * J, T, HEAD_DIM), LOW),
            pltpu.VMEM((S * J, HEAD_DIM, T), LOW),
        ],
        compiler_params=attn_params(S * J * T),
        cost_estimate=cost(36 * 10**9, 4 * MIB),
        name="attn_fwd",
    )(meta, seq, q, *ks, *vs)


def attn_bwd(meta, seq, q, ks, vs, o, lse, do, bq=512, bk=512):
    J, _, T = q.shape
    S = len(ks)
    block = pltpu.HBM((J, HEAD_DIM, T), LOW)
    out = pl.pallas_call(
        functools.partial(bwd_kernel, bq, bk, S),
        out_shape=[block] * (1 + 2 * S),
        in_specs=[M, M] + [V] * (4 + 2 * S),
        out_specs=[pl.BlockSpec()] * (1 + 2 * S),
        scratch_shapes=[
            pltpu.VMEM((S * J, T, HEAD_DIM), LOW),
            pltpu.VMEM((S * J, HEAD_DIM, T), LOW),
            pltpu.VMEM((S * J, T, HEAD_DIM), LOW),
            pltpu.VMEM((S * J, HEAD_DIM, T), F32),
            pltpu.VMEM((S * J, HEAD_DIM, T), F32),
        ],
        compiler_params=attn_params(S * J * T),
        cost_estimate=cost(10**6, 1000),
        name="attn_bwd",
    )(meta, seq, q, *ks, *vs, o, lse, do)
    return out[0], out[1 : 1 + S], out[1 + S :]


def qkv_kernel(x_ref, gain_ref, bias_ref, w_ref, b_ref, n_ref, q_ref, k_ref, v_ref):
    J = q_ref.shape[0]
    normed = norm_rows(x_ref[...].astype(F32), gain_ref[...], bias_ref[...]).astype(LOW)
    n_ref[...] = normed
    rows = normed.shape[0]
    for i, ref in ((1, k_ref), (2, v_ref), (0, q_ref)):
        made = dotf(normed, w_ref[i], NN)
        if i != 1:
            made = made + b_ref[i // 2][None]
        made = made.astype(LOW)
        if i == 0:
            made = (made * 0.125).astype(LOW)
        ref[...] = made.T.reshape(J, HEAD_DIM, rows)


def qkv(x, gain, bias, w, b):
    T, D = x.shape
    local = w.shape[2]
    J = local // HEAD_DIM
    rows = 256
    row_spec = pl.BlockSpec((rows, D), lambda i: (i, 0))
    head_spec = pl.BlockSpec((J, HEAD_DIM, rows), lambda i: (0, 0, i))
    heads = jax.ShapeDtypeStruct((J, HEAD_DIM, T), LOW)
    return pl.pallas_call(
        qkv_kernel,
        grid=(T // rows,),
        out_shape=(pltpu.HBM((T, D), LOW), heads, heads, heads),
        in_specs=[row_spec, V, V, V, V],
        out_specs=(row_spec, head_spec, head_spec, head_spec),
        compiler_params=pltpu.CompilerParams(vmem_limit_bytes=12 * MIB),
        cost_estimate=cost(6 * T * D * local, 8 * MIB),
        name="norm_qkv",
    )(far(x), far(gain[None]), far(bias[None]), far(w), far(b))


def out_kernel(pos_ref, *refs):
    pieces = refs[:8]
    w_ref, x_ref, b_ref, gain_ref, bias_ref, x1_ref, n2_ref, held = refs[8:]
    i = pl.program_id(0)
    rows = x1_ref.shape[0]

    @pl.when(i == 0)
    def _():
        for r, piece in enumerate(pieces):
            half = piece.shape[1]
            held[pos_ref[r % 4], :, r // 4 * half : (r // 4 + 1) * half] = piece[...]

    lanes = pl.ds(pl.multiple_of(i * rows, rows), rows)
    o = held[:, :, lanes].reshape(-1, rows)
    middle = x_ref[...].astype(F32) + dotf(o, w_ref[...], TN) + b_ref[...]
    x1_ref[...] = middle
    n2_ref[...] = norm_rows(middle, gain_ref[...], bias_ref[...]).astype(LOW)


def out_stage(pos, pieces, w, x, b, gain, bias):
    T, D = x.shape
    local = pieces[0].shape[0]
    rows = 256
    row_spec = pl.BlockSpec((rows, D), lambda i: (i, 0))
    return pl.pallas_call(
        out_kernel,
        grid=(T // rows,),
        out_shape=(pltpu.HBM((T, D), F32), jax.ShapeDtypeStruct((T, D), LOW)),
        in_specs=[M] + [V] * 9 + [row_spec, V, V, V],
        out_specs=(row_spec, row_spec),
        scratch_shapes=[pltpu.VMEM((4, local, T), LOW)],
        compiler_params=pltpu.CompilerParams(vmem_limit_bytes=16 * MIB),
        cost_estimate=cost(2 * T * D * 4 * local, 12 * MIB),
        name="out_norm",
    )(pos, *pieces, far(w), far(x), far(b[None]), far(gain[None]), far(bias[None]))


def mlp_kernel(at_ref, n2_ref, dm_ref, wf_ref, wp_ref, b_ref, *refs):
    g_ref, dh_ref, dn2_ref, db_ref = refs[-4:]
    hidden = dotf(n2_ref[...], wf_ref[...], NN) + b_ref[...]
    back = dotf(dm_ref[...], wp_ref[...], NT)
    root = math.sqrt(2.0 / math.pi)
    square = hidden * hidden
    bent = jnp.tanh(root * hidden * (1.0 + 0.044715 * square))
    half = 0.5 * (1.0 + bent)
    g_ref[...] = (hidden * half).astype(LOW)
    slope = half + 0.5 * hidden * (1.0 - bent * bent) * (root * (1.0 + 3 * 0.044715 * square))
    dh = (back * slope).astype(LOW)
    dh_ref[...] = dh
    dn2_ref[...] = dotf(dh, wf_ref[...], NT).astype(LOW)

    @pl.when(pl.program_id(0) == 0)
    def _():
        db_ref[...] = jnp.zeros_like(db_ref)

    db_ref[...] += jnp.sum(dh.astype(F32), axis=0, keepdims=True)


def mlp_stage(at, n2, dm, w_fc, w_proj, b_fc, before=()):
    T, D = n2.shape
    F = w_fc.shape[1]
    rows = 256
    steps = T // 2 // rows
    row_spec = pl.BlockSpec((rows, D), lambda i, at: (at[0] * steps + i, 0))
    hid_spec = pl.BlockSpec((rows, F), lambda i, at: (at[0] * steps + i, 0))
    own_spec = pl.BlockSpec((rows, D), lambda i, at: (i, 0))
    whole = pl.BlockSpec(memory_space=pltpu.VMEM)
    return pl.pallas_call(
        mlp_kernel,
        grid_spec=pltpu.PrefetchScalarGridSpec(
            num_scalar_prefetch=1,
            grid=(steps,),
            in_specs=[row_spec, row_spec, whole, whole, whole]
            + [pl.BlockSpec(memory_space=pl.ANY)] * len(before),
            out_specs=(hid_spec, hid_spec, own_spec, whole),
        ),
        out_shape=(
            jax.ShapeDtypeStruct((T, F), LOW),
            jax.ShapeDtypeStruct((T, F), LOW),
            pltpu.HBM((T // 2, D), LOW),
            jax.ShapeDtypeStruct((1, F), F32),
        ),
        input_output_aliases={6 + i: i for i in range(len(before))},
        compiler_params=pltpu.CompilerParams(vmem_limit_bytes=18 * MIB),
        cost_estimate=cost(3 * T * D * F, 9 * MIB),
        name="feed",
    )(at, n2, dm, w_fc, w_proj, b_fc[None], *before)


def back_kernel(at_ref, own_ref, crossed_ref, x_ref, kept_ref, gain_ref, wide_ref, low_ref, sums_ref):
    grad = own_ref[...].astype(F32) + crossed_ref[...].astype(F32)
    values = x_ref[...].astype(F32)
    centred = values - jnp.mean(values, axis=-1, keepdims=True)
    factor = lax.rsqrt(jnp.mean(centred * centred, axis=-1, keepdims=True) + EPS)
    z = centred * factor
    u = grad * gain_ref[...]
    mean_u = jnp.mean(u, axis=-1, keepdims=True)
    mean_uz = jnp.mean(u * z, axis=-1, keepdims=True)
    made = kept_ref[...].astype(F32) + factor * (u - mean_u - z * mean_uz)
    wide_ref[...] = made
    low = made.astype(LOW)
    low_ref[...] = low

    @pl.when(pl.program_id(0) == 0)
    def _():
        sums_ref[...] = jnp.zeros_like(sums_ref)

    for i, part in enumerate((grad * z, grad, low.astype(F32), kept_ref[...].astype(F32))):
        sums_ref[i : i + 1, :] += jnp.sum(part, axis=0, keepdims=True)


def norm_back(at, own, crossed, x, kept, gain):
    half, D = own.shape
    rows = 256
    steps = half // rows
    spec = pl.BlockSpec((rows, D), lambda i, at: (i, 0))
    from_whole = pl.BlockSpec((rows, D), lambda i, at: (at[0] * steps + i, 0))
    whole = pl.BlockSpec(memory_space=pltpu.VMEM)
    return pl.pallas_call(
        back_kernel,
        grid_spec=pltpu.PrefetchScalarGridSpec(
            num_scalar_prefetch=1,
            grid=(steps,),
            in_specs=[spec, spec, from_whole, spec if kept.shape[0] == half else from_whole, whole],
            out_specs=(spec, spec, whole),
        ),
        out_shape=(
            pltpu.HBM((half, D), F32),
            jax.ShapeDtypeStruct((half, D), LOW),
            jax.ShapeDtypeStruct((4, D), F32),
        ),
        compiler_params=pltpu.CompilerParams(vmem_limit_bytes=12 * MIB),
        cost_estimate=cost(0, 14 * half * D),
        name="norm_back",
    )(at, own, crossed, far(x), kept, gain[None])


def first_kernel(core_ref, q_ref, k_ref, v_ref, w_ref, keep_ref, send_ref):
    half = keep_ref.shape[0]
    for out, at in ((send_ref, 1 - core_ref[0]), (keep_ref, core_ref[0])):
        lanes = pl.ds(pl.multiple_of(at * half, half), half)
        total = jnp.zeros(out.shape, F32)
        for i, ref in enumerate((q_ref, k_ref, v_ref)):
            total += dotf(ref[:, lanes].T, w_ref[i], NT)
        out[...] = total.astype(LOW)


def first_stage(core, q, k, v, w):
    local, T = q.shape
    D = w.shape[1]
    part = jax.ShapeDtypeStruct((T // 2, D), LOW)
    return pl.pallas_call(
        first_kernel,
        out_shape=(part, part),
        in_specs=[M, V, V, V, V],
        out_specs=(V, V),
        compiler_params=pltpu.CompilerParams(vmem_limit_bytes=10 * MIB),
        cost_estimate=cost(10**6, 1000),
        name="first_grad",
    )(core, q, k, v, w)


def feed_grads_kernel(g_ref, dm_ref, n2_ref, dh_ref, out_ref):
    steps = pl.num_programs(0) // 2
    rows = out_ref.shape[0]
    i = pl.program_id(0)
    lanes = pl.ds(pl.multiple_of(i % steps * rows, rows), rows)

    @pl.when(i < steps)
    def _():
        out_ref[...] = dotf(g_ref[:, lanes], dm_ref[...], TN).astype(LOW)

    @pl.when(i >= steps)
    def _():
        out_ref[...] = dotf(n2_ref[:, lanes], dh_ref[...], TN).astype(LOW)


def feed_grads(g, dm, n2, dh):
    T, F = g.shape
    D = dm.shape[1]
    rows = 256
    return pl.pallas_call(
        feed_grads_kernel,
        grid=((F + D) // rows,),
        out_shape=pltpu.HBM((F + D, D), LOW),
        in_specs=[V] * 4,
        out_specs=pl.BlockSpec((rows, D), lambda i: (i, 0)),
        compiler_params=pltpu.CompilerParams(vmem_limit_bytes=10 * MIB),
        cost_estimate=cost(4 * T * D * F, 12 * MIB),
        name="feed_grads",
    )(g, dm, n2, dh)


def do_kernel(core_ref, own_ref, other_ref, w_ref, one_ref, two_ref, do_ref, grad_ref):
    half = own_ref.shape[0]
    grad = jnp.zeros(grad_ref.shape, F32)
    for ref, at in ((own_ref, core_ref[0]), (other_ref, 1 - core_ref[0])):
        lanes = pl.ds(pl.multiple_of(at * half, half), half)
        do_ref[:, lanes] = dotf(w_ref[...], ref[...], NT).astype(LOW)
        o = jnp.where(at == 0, one_ref[...], two_ref[...])
        grad += dotf(o, ref[...], NN)
    grad_ref[...] = grad.astype(LOW)


def do_stage(core, own, other, w_out, home_one, home_two):
    local, D = w_out.shape
    T = 2 * home_one.shape[1]
    return pl.pallas_call(
        do_kernel,
        out_shape=(pltpu.HBM((local, T), LOW), pltpu.HBM((local, D), LOW)),
        in_specs=[M, V, V, V, V, V],
        out_specs=(pl.BlockSpec(), pl.BlockSpec()),
        compiler_params=pltpu.CompilerParams(vmem_limit_bytes=8 * MIB),
        cost_estimate=cost(4 * T * D * local, 5 * MIB),
        name="heads_grad",
    )(core, own, other, w_out, home_one, home_two)


def grad_kernel(share, spot_ref, dq_ref, dk_ref, dv_ref, own_ref, *refs):
    parts, out_ref = refs[:-1], refs[-1]
    J = dq_ref.shape[0]
    for i, ref in enumerate((dq_ref, dk_ref, dv_ref)):
        total = dotf(ref[spot_ref[4]], own_ref[...], NN)
        for r, part in enumerate(parts):
            lanes = pl.ds(pl.multiple_of(spot_ref[r], share), share)
            for s in range(1, J):
                total += dotf(ref[spot_ref[4 + s], :, lanes], part[s - 1], NN)
        out_ref[i * HEAD_DIM : (i + 1) * HEAD_DIM] = total


def grad_heads(spots, dq, dk, dv, own, parts):
    J, _, T = dq.shape
    D = own.shape[1]
    return pl.pallas_call(
        functools.partial(grad_kernel, parts[0].shape[1]),
        out_shape=jax.ShapeDtypeStruct((3 * HEAD_DIM, D), F32),
        in_specs=[M] + [V] * (4 + len(parts)),
        out_specs=V,
        compiler_params=pltpu.CompilerParams(vmem_limit_bytes=12 * MIB),
        cost_estimate=cost(10**6, 1000),
        name="grad_heads",
    )(spots, dq, dk, dv, own, *parts)


def lay_kernel(S, spot_ref, *refs):
    parts, (qkv_ref, out_ref, held) = refs[:-3], refs[-3:]
    J, depth, _ = held.shape
    wide = parts[0].shape[1]
    few = (parts[0].shape[0] - depth) // S
    for i, part in enumerate(parts):
        jj, gg = spot_ref[2 * i], spot_ref[2 * i + 1]
        held[jj, :, pl.ds(pl.multiple_of(gg * wide, wide), wide)] = part[:depth]
        rest = part[depth:].astype(F32)
        rows = pl.ds(pl.multiple_of((jj * S + gg) * few, few), few)
        for e in range(S):
            out_ref[rows, e * wide : (e + 1) * wide] = rest[e * few : (e + 1) * few]
    for k in range(3):
        rows = [held[h, k * HEAD_DIM : (k + 1) * HEAD_DIM, :] for h in range(J)]
        qkv_ref[k] = jnp.concatenate(rows, 0).astype(F32).T


def lay_blocks(found, J, S):
    parts = [part for _, _, part in found]
    wide = parts[0].shape[1]
    spots = jnp.stack([x for jj, gg, _ in found for x in (jj, gg)]).astype(jnp.int32)
    return pl.pallas_call(
        functools.partial(lay_kernel, S),
        out_shape=(
            jax.ShapeDtypeStruct((3, S * wide, J * HEAD_DIM), F32),
            jax.ShapeDtypeStruct((J * HEAD_DIM, S * wide), F32),
        ),
        in_specs=[M] + [V] * len(parts),
        out_specs=(V, V),
        scratch_shapes=[pltpu.VMEM((J, 3 * HEAD_DIM, S * wide), LOW)],
        compiler_params=pltpu.CompilerParams(vmem_limit_bytes=12 * MIB),
        cost_estimate=cost(0, 6 * MIB),
        name="lay_blocks",
    )(spots, *parts)


def add_kernel(own_ref, other_ref, out_ref):
    out_ref[...] = (own_ref[...].astype(F32) + other_ref[...].astype(F32)).astype(LOW)


def add_low(own, other):
    return pl.pallas_call(
        add_kernel,
        out_shape=jax.ShapeDtypeStruct(own.shape, LOW),
        in_specs=[V, V],
        out_specs=V,
        compiler_params=pltpu.CompilerParams(vmem_limit_bytes=6 * MIB),
        cost_estimate=cost(0, 6 * own.size),
        name="add_low",
    )(own, other)


def feed_out_kernel(core_ref, g_ref, w_ref, kept_ref, sent_ref):
    half = kept_ref.shape[0]
    for out, at in ((sent_ref, 1 - core_ref[0]), (kept_ref, core_ref[0])):
        rows = pl.ds(pl.multiple_of(at * half, half), half)
        out[...] = dotf(g_ref[rows, :], w_ref[...], NN).astype(LOW)


def feed_out(core, g, w):
    T, F = g.shape
    D = w.shape[1]
    part = jax.ShapeDtypeStruct((T // 2, D), LOW)
    return pl.pallas_call(
        feed_out_kernel,
        out_shape=(part, part),
        in_specs=[M, V, V],
        out_specs=(V, V),
        compiler_params=pltpu.CompilerParams(vmem_limit_bytes=8 * MIB),
        cost_estimate=cost(2 * T * F * D, 6 * MIB),
        name="feed_out",
    )(core, g, w)


def widen_kernel(low_ref, first_ref, second_ref):
    steps = pl.num_programs(0) // 2

    @pl.when(pl.program_id(0) < steps)
    def _():
        first_ref[...] = low_ref[...].astype(F32)

    @pl.when(pl.program_id(0) >= steps)
    def _():
        second_ref[...] = low_ref[...].astype(F32)


def widen(low, first):
    rows, D = low.shape
    steps = 4
    block = first // steps
    return pl.pallas_call(
        widen_kernel,
        grid=(2 * steps,),
        out_shape=(jax.ShapeDtypeStruct((first, D), F32), jax.ShapeDtypeStruct((rows - first, D), F32)),
        in_specs=[pl.BlockSpec((block, D), lambda i: (i, 0))],
        out_specs=(
            pl.BlockSpec((block, D), lambda i: (jnp.minimum(i, steps - 1), 0)),
            pl.BlockSpec((block, D), lambda i: (jnp.maximum(i - steps, 0), 0)),
        ),
        compiler_params=pltpu.CompilerParams(vmem_limit_bytes=8 * MIB),
        cost_estimate=cost(0, 12 * MIB),
        name="widen",
    )(low)


def pair_kernel(core_ref, own_ref, other_ref, out_ref):
    half = own_ref.shape[0]
    for ref, at in ((own_ref, core_ref[0]), (other_ref, 1 - core_ref[0])):
        out_ref[pl.ds(pl.multiple_of(at * half, half), half), :] = ref[...]


def lay_pair(core, own, other):
    half, D = own.shape
    return pl.pallas_call(
        pair_kernel,
        out_shape=jax.ShapeDtypeStruct((2 * half, D), own.dtype),
        in_specs=[M, V, V],
        out_specs=V,
        compiler_params=pltpu.CompilerParams(vmem_limit_bytes=6 * MIB),
        cost_estimate=cost(0, 8 * half * D),
        name="lay_pair",
    )(core, own, other)


def shift_dp(value, steps):
    count = lax.axis_size("dp")
    return lax.ppermute(value, "dp", [(i, (i + steps) % count) for i in range(count)])


def shift_group(value, steps, S):
    count = lax.axis_size("dp")
    return lax.ppermute(
        value, "dp", [(i, i // S * S + (i % S + steps) % S) for i in range(count)]
    )


def swap_core(value):
    return lax.ppermute(value, "tensor", [(i, i ^ 1) for i in range(lax.axis_size("tensor"))])


def swap_x(value):
    return lax.ppermute(value, "tensor", [(i, i ^ 2) for i in range(lax.axis_size("tensor"))])


def rows_at(value, start, count):
    return lax.dynamic_slice_in_dim(value, start, count, 0)


def pick(value, index):
    return lax.dynamic_index_in_dim(value, index, 0, keepdims=False)


def gate(value, *before):
    return lax.optimization_barrier((value, *before))[0]


def tied(*values):
    return lax.optimization_barrier(values)


def sum_group(parts, g, S):
    total = pick(parts, g).astype(F32)
    for e in range(1, S):
        total = total + shift_group(pick(parts, (g + e) % S).astype(LOW), e, S).astype(F32)
    return total


def spread_blocks(blocks, j, g, S):
    J = len(blocks)
    found = []
    for s, part in enumerate(blocks):
        found.append(((j - s) % J, g, part))
        for e in range(1, S):
            found.append(((j - s) % J, (g - e) % S, shift_group(part, e, S)))
    return found


def per_device(
    block_input,
    output_grad,
    seq_lengths,
    ln1_gain,
    ln1_bias,
    w_qkv,
    b_qv,
    w_out,
    b_out,
    ln2_gain,
    ln2_bias,
    w_fc,
    b_fc,
    w_proj,
    b_proj,
):
    T, D = block_input.shape
    local = w_qkv.shape[2]
    J = local // HEAD_DIM
    count = lax.axis_size("dp")
    S = count // J
    place = lax.axis_index("dp")
    j, g = place // S, place % S
    tensor = lax.axis_index("tensor")
    core, side = tensor % 2, tensor // 2
    half, share = T // 2, T // 4
    core_at = core[None].astype(jnp.int32)
    meta = g[None].astype(jnp.int32)
    groups = [[S * jj + gg for jj in range(J)] for gg in range(S)]

    def exchange(heads):
        return lax.all_to_all(heads, "dp", 0, 0, tiled=True, axis_index_groups=groups)

    def group(value):
        return [value] + [shift_group(value, e, S) for e in range(1, S)]

    first_low, queries, keys, values = qkv(block_input, ln1_gain, ln1_bias, w_qkv, b_qv)
    k_own, across = tied(exchange(keys), swap_x(w_out))
    ks = group(k_own)
    vs = group(gate(exchange(values), *ks[1:]))
    q_all = exchange(queries)

    pieces = jnp.stack([w_out, swap_core(w_out), across, swap_core(across)])
    order = jnp.stack([tensor ^ r for r in range(4)]).astype(jnp.int32)
    w_out_all = jnp.concatenate([pick(pieces, tensor ^ r) for r in range(4)], 0)

    q_all = gate(q_all, w_out_all)
    o_one, lse_one = attn_fwd(meta, seq_lengths, q_all, ks, vs, 0)
    o_two, lse_two = attn_fwd(meta, seq_lengths, gate(q_all, o_one), ks, vs, 1)
    home_one, o_two = tied(exchange(o_one), o_two)
    home_one = home_one.reshape(local, half)
    home_two, across = tied(exchange(o_two), swap_x(home_one))
    home_two = home_two.reshape(local, half)

    own_quarter = rows_at(first_low, core * half + side * share, share)
    own_quarter = rows_at(first_low, core * half + side * share, share)
    own_quarter = gate(own_quarter, home_two)
    norm_own = lax.all_gather(own_quarter, "dp", axis_index_groups=groups)

    def gather_tensor(value, across):
        return value, swap_core(value), across, swap_core(across)

    o_pieces = gather_tensor(home_one, across) + gather_tensor(home_two, swap_x(home_two))
    middle, second_low = out_stage(order, o_pieces, w_out_all, block_input, b_out, ln2_gain, ln2_bias)
    active_low, hidden_grad, sent, bias_one = mlp_stage(
        1 - core_at, second_low, output_grad, w_fc, w_proj, b_fc
    )
    arrived = swap_core(sent)
    active_low, hidden_grad, kept, bias_two = mlp_stage(
        core_at, second_low, output_grad, w_fc, w_proj, b_fc, (active_low, hidden_grad)
    )
    grad_b_fc = bias_one + bias_two
    second_half = add_low(kept, arrived)
    crossed = swap_x(second_half)
    grad_feed = feed_grads(active_low, output_grad, second_low, hidden_grad)
    feed_part = lax.psum_scatter(grad_feed, "dp", scatter_dimension=0, tiled=True)
    feed_kept, feed_sent = feed_out(core_at, active_low, w_proj)
    rolled = jnp.stack([pick(norm_own, (j + s) % J) for s in range(1, J)])
    crossed = gate(crossed, grad_feed, rolled, feed_kept)
    middle_grad, branch_half, sums_two = norm_back(
        core_at, second_half, crossed, middle, output_grad, ln2_gain
    )
    heads_grad, grad_w_out = do_stage(core_at, branch_half, swap_core(branch_half), w_out, home_one, home_two)
    do_all = exchange(heads_grad.reshape(J, HEAD_DIM, T))
    out_parts = lax.all_to_all(grad_w_out.reshape(count, local // count, D), "dp", 0, 0, tiled=True)

    norm_across = swap_x(gate(rolled, branch_half))

    o_all = jnp.concatenate([o_one, o_two], 2)
    lse = jnp.concatenate([lse_one, lse_two], 2)
    dq, dks, dvs = attn_bwd(meta, seq_lengths, q_all, ks, vs, o_all, lse, do_all)
    dq, dks, dvs, norm_across, out_parts = tied(dq, dks, dvs, norm_across, out_parts)

    norm_parts = [rolled, norm_across, swap_core(rolled), swap_core(norm_across)]

    def regroup(parts):
        return [shift_group(part, -e, S) for e, part in enumerate(parts) if e]

    def total(own, moved):
        for part in moved:
            own = add_low(own, part)
        return own

    q_home, dk_moved = tied(exchange(dq), regroup(dks))
    dk = total(dks[0], dk_moved)
    k_home, dv_moved = tied(exchange(gate(dk, q_home)), regroup(dvs))
    dv = total(dvs[0], dv_moved)
    v_home = exchange(gate(dv, k_home))
    feed_own = add_low(feed_kept, swap_core(gate(feed_sent, q_home)))
    feed_across = swap_x(feed_own)
    q_home, k_home, v_home = (x.reshape(local, T) for x in (q_home, k_home, v_home))

    spots = jnp.stack(
        [
            c * half + d * share
            for c, d in ((core, side), (core, 1 - side), (1 - core, side), (1 - core, 1 - side))
        ]
        + [(j + s) % J for s in range(J)]
    ).astype(jnp.int32)
    head_grad = grad_heads(spots, dq, dk, dv, first_low, norm_parts)
    v_home, head_grad, feed_across, feed_part = tied(v_home, head_grad, feed_across, feed_part)
    grad_feed = lax.all_gather(feed_part, "dp", axis=0, tiled=True)
    kept, sent = first_stage(core_at, q_home, k_home, v_home, w_qkv)
    first_half = add_low(kept, swap_core(sent))
    cut = head_grad.reshape(3 * HEAD_DIM, S, D // S).transpose(1, 0, 2)
    head_grad = sum_group(cut, g, S).astype(LOW)
    grad_w_out = jnp.sum(out_parts.astype(F32), axis=0).astype(LOW)
    block = jnp.concatenate([head_grad] + jnp.split(grad_w_out, S, axis=1), 0)
    blocks = [shift_dp(block, s * S) for s in range(1, J)]

    first_across = gate(swap_x(first_half), *blocks)
    _, input_half, sums_one = norm_back(
        core_at, first_half, first_across, block_input, middle_grad, ln1_gain
    )
    input_grad = lay_pair(core_at, input_half, swap_core(input_half))

    feed_across = gate(feed_across, block)
    feed_sum = feed_own.astype(F32) + feed_across.astype(F32)
    middle_half = rows_at(middle, core * half, half)
    output_half = (middle_half + (feed_sum + b_proj)).astype(LOW)
    block_output = lay_pair(core_at, output_half, swap_core(output_half))

    hidden_width = grad_b_fc.shape[1]
    wide_fc = lax.dynamic_update_slice_in_dim(
        jnp.zeros((1, hidden_width * lax.axis_size("tensor")), F32),
        grad_b_fc,
        tensor * hidden_width,
        1,
    ).reshape(-1, D)
    bias_qv = jnp.stack([jnp.sum(q_home.astype(F32), axis=1), jnp.sum(v_home.astype(F32), axis=1)])
    wide_qv = lax.dynamic_update_slice_in_dim(jnp.zeros((2, D), F32), bias_qv, tensor * local, 1)
    early = jnp.concatenate([wide_fc, wide_qv], 0)
    early = early + swap_x(early)
    small = jnp.concatenate([sums_two, sums_one[:2], early], 0)
    small = small + swap_core(small)
    step = 1
    while step < count:
        small = small + lax.ppermute(small, "dp", [(i, i ^ step) for i in range(count)])
        if step == 2:
            small, input_grad, block_output = tied(small, input_grad, block_output)
        step *= 2
    found = spread_blocks([block, *blocks], j, g, S)
    grad_w_proj, grad_w_fc = widen(grad_feed, w_proj.shape[0])
    grad_w_qkv, grad_w_out = lay_blocks(found, J, S)
    tail = small.shape[0] - 2
    grad_b_qv = lax.dynamic_slice_in_dim(small[tail:], tensor * local, local, 1)
    grad_b_fc = rows_at(small[6:tail].reshape(-1), tensor * hidden_width, hidden_width)
    return (
        block_output,
        input_grad,
        small[4],
        small[5],
        grad_w_qkv,
        grad_b_qv,
        grad_w_out,
        small[2],
        small[0],
        small[1],
        grad_w_fc,
        grad_b_fc,
        grad_w_proj,
        small[3],
    )


def solution(mesh):
    placed = (
        P("dp", None),
        P("dp", None),
        P(),
        P(),
        P(),
        P(None, None, "tensor"),
        P(None, "tensor"),
        P("tensor", None),
        P(),
        P(),
        P(),
        P(None, "tensor"),
        P("tensor"),
        P("tensor", None),
        P(),
    )
    return jax.shard_map(
        per_device,
        mesh=mesh,
        in_specs=placed,
        out_specs=(
            P("dp", None),
            P("dp", None),
            P(),
            P(),
            P(None, None, "tensor"),
            P(None, "tensor"),
            P("tensor", None),
            P(),
            P(),
            P(),
            P(None, "tensor"),
            P("tensor"),
            P("tensor", None),
            P(),
        ),
        check_vma=False,
    )
```

```python
import functools
import math

import jax
import jax.numpy as jnp
from jax import lax
from jax.experimental import pallas as pl
from jax.experimental.pallas import tpu as pltpu
from jax.sharding import PartitionSpec as P

HEAD_DIM = 64
NEG = -1e30
EPS = 1e-05
NN = (((1,), (0,)), ((), ()))
NT = (((1,), (1,)), ((), ()))
TN = (((0,), (0,)), ((), ()))
LOW = jnp.bfloat16
F32 = jnp.float32
MIB = 2**20
LITTLE = 0
V = pl.BlockSpec(memory_space=pltpu.VMEM)
M = pl.BlockSpec(memory_space=pltpu.SMEM)


def dotf(a, b, dims):
    return lax.dot_general(a, b, dims, preferred_element_type=F32)


def norm_rows(values, weight_row, shift_row):
    centred = values - jnp.mean(values, axis=-1, keepdims=True)
    spread = jnp.mean(centred * centred, axis=-1, keepdims=True)
    return centred * lax.rsqrt(spread + EPS) * weight_row + shift_row


def far(value):
    return pltpu.with_memory_space_constraint(value, pltpu.HBM)


def cost(flops, moved):
    return pl.CostEstimate(flops=LITTLE * flops, bytes_accessed=LITTLE * moved, transcendentals=0)


def seq_start(place, ends):
    start = jnp.zeros_like(place)
    for end in ends:
        start = jnp.where(place >= end, end, start)
    return start


def read_ends(seq_ref):
    ends = []
    total = jnp.int32(0)
    for s in range(seq_ref.shape[0] - 1):
        total = total + seq_ref[s]
        ends.append(total)
    return ends


def key_spot(kstart, own, J, S, T):
    block = kstart // T
    distance = lax.rem(own - lax.rem(block, S) + S, S)
    return distance * J + block // S, lax.rem(kstart, T)


def tile_range(q0, bq, bk, ends):
    t0 = seq_start(q0, ends) // bk
    t3 = (q0 + bq + bk - 1) // bk
    t2 = jnp.maximum(q0 // bk, t0)
    t1 = jnp.minimum((seq_start(q0 + bq - 1, ends) + bk - 1) // bk, t2)
    return t0, jnp.maximum(t1, t0), t2, t3


def fill(refs, dst, flip):
    J = refs[0].shape[0]
    for e, ref in enumerate(refs):

        def one(i, _, e=e, ref=ref):
            dst[e * J + i] = ref[i].T if flip else ref[i]
            return 0

        lax.fori_loop(0, J, one, 0)


def fwd_kernel(bq, bk, S, part, meta_ref, seq_ref, q_ref, *refs):
    k_refs, v_refs = refs[:S], refs[S : 2 * S]
    o_ref, lse_ref, kt_ref, vf_ref = refs[2 * S :]
    J, _, T = q_ref.shape
    ends = read_ends(seq_ref)
    fill(k_refs, kt_ref, True)
    fill(v_refs, vf_ref, False)
    per = T // 2 // bq
    rows = lax.broadcasted_iota(jnp.int32, (bk, bq), 0)

    def q_tile(i, _):
        s = i // per
        to = pl.multiple_of(lax.rem(i, per) * bq, bq)
        qo = to + part * (T // 2)
        q0 = (s * S + meta_ref[0]) * T + qo
        q = q_ref[s, :, pl.ds(qo, bq)]
        place = q0 + lax.broadcasted_iota(jnp.int32, (1, bq), 1)
        start = seq_start(place, ends)

        def tile(masked, kt, carry):
            m, l, acc = carry
            kstart = kt * bk
            spot, ko = key_spot(kstart, meta_ref[0], J, S, T)
            ko = pl.multiple_of(ko, bk)
            k = kt_ref[spot, pl.ds(ko, bk), :]
            v = vf_ref[spot, :, pl.ds(ko, bk)]
            sc = dotf(k, q, NN)
            if masked:
                sc = jnp.where((rows >= start - kstart) & (rows <= place - kstart), sc, NEG)
            m2 = jnp.maximum(m, jnp.max(sc, axis=0, keepdims=True))
            p = jnp.exp(sc - m2)
            a = jnp.exp(m - m2)
            l = l * a + jnp.sum(p, axis=0, keepdims=True)
            acc = acc * a + dotf(v, p.astype(LOW), NN)
            return m2, l, acc

        t0, t1, t2, t3 = tile_range(q0, bq, bk, ends)
        c = (jnp.full((1, bq), NEG, F32), jnp.zeros((1, bq), F32), jnp.zeros((HEAD_DIM, bq), F32))
        c = lax.fori_loop(t2, t3, functools.partial(tile, True), c)
        c = lax.fori_loop(t0, t1, functools.partial(tile, True), c)
        m, l, acc = lax.fori_loop(t1, t2, functools.partial(tile, False), c)
        o_ref[s, :, pl.ds(to, bq)] = (acc / l).astype(LOW)
        lse_ref[s, :, pl.ds(to, bq)] = m + jnp.log(l)
        return 0

    lax.fori_loop(0, J * per, q_tile, 0)


def bwd_kernel(bq, bk, S, meta_ref, seq_ref, q_ref, *refs):
    k_refs, v_refs = refs[:S], refs[S : 2 * S]
    o_ref, lse_ref, do_ref, dq_ref = refs[2 * S : 2 * S + 4]
    dk_refs, dv_refs = refs[2 * S + 4 : 3 * S + 4], refs[3 * S + 4 : 4 * S + 4]
    kt_ref, kf_ref, vt_ref, dk_acc, dv_acc = refs[4 * S + 4 :]
    J, _, T = q_ref.shape
    ends = read_ends(seq_ref)
    fill(k_refs, kt_ref, True)
    fill(k_refs, kf_ref, False)
    fill(v_refs, vt_ref, True)
    dk_acc[...] = jnp.zeros_like(dk_acc)
    dv_acc[...] = jnp.zeros_like(dv_acc)
    per = T // bq
    rows = lax.broadcasted_iota(jnp.int32, (bk, bq), 0)

    def q_tile(i, _):
        s = i // per
        qo = pl.multiple_of(lax.rem(i, per) * bq, bq)
        q0 = (s * S + meta_ref[0]) * T + qo
        q = q_ref[s, :, pl.ds(qo, bq)]
        do = do_ref[s, :, pl.ds(qo, bq)]
        lse = lse_ref[s, :, pl.ds(qo, bq)]
        o = o_ref[s, :, pl.ds(qo, bq)].astype(F32)
        delta = jnp.sum(do.astype(F32) * o, axis=0, keepdims=True)
        place = q0 + lax.broadcasted_iota(jnp.int32, (1, bq), 1)
        start = seq_start(place, ends)

        def tile(masked, kt, dq):
            kstart = kt * bk
            spot, ko = key_spot(kstart, meta_ref[0], J, S, T)
            ko = pl.multiple_of(ko, bk)
            sc = dotf(kt_ref[spot, pl.ds(ko, bk), :], q, NN)
            p = jnp.exp(sc - lse)
            if masked:
                p = jnp.where((rows >= start - kstart) & (rows <= place - kstart), p, 0.0)
            dp = dotf(vt_ref[spot, pl.ds(ko, bk), :], do, NN)
            ds = (p * (dp - delta)).astype(LOW)
            dv_acc[spot, :, pl.ds(ko, bk)] += dotf(do, p.astype(LOW), NT)
            dk_acc[spot, :, pl.ds(ko, bk)] += dotf(q, ds, NT)
            return dq + dotf(kf_ref[spot, :, pl.ds(ko, bk)], ds, NN)

        t0, t1, t2, t3 = tile_range(q0, bq, bk, ends)
        dq = jnp.zeros((HEAD_DIM, bq), F32)
        dq = lax.fori_loop(t2, t3, functools.partial(tile, True), dq)
        dq = lax.fori_loop(t0, t1, functools.partial(tile, True), dq)
        dq = lax.fori_loop(t1, t2, functools.partial(tile, False), dq)
        dq_ref[s, :, pl.ds(qo, bq)] = (dq * 0.125).astype(LOW)
        return 0

    lax.fori_loop(0, J * per, q_tile, 0)
    for e in range(S):
        dk_refs[e][...] = dk_acc[e * J : (e + 1) * J].astype(LOW)
        dv_refs[e][...] = dv_acc[e * J : (e + 1) * J].astype(LOW)


def attn_params(keys):
    return pltpu.CompilerParams(vmem_limit_bytes=(58 if keys > 8192 else 24) * MIB)


def attn_fwd(meta, seq, q, ks, vs, part, bq=512, bk=512):
    J, _, T = q.shape
    S = len(ks)
    return pl.pallas_call(
        functools.partial(fwd_kernel, bq, bk, S, part),
        out_shape=(
            pltpu.HBM((J, HEAD_DIM, T // 2), LOW),
            jax.ShapeDtypeStruct((J, 1, T // 2), F32),
        ),
        in_specs=[M, M] + [V] * (1 + 2 * S),
        out_specs=(pl.BlockSpec(), V),
        scratch_shapes=[
            pltpu.VMEM((S * J, T, HEAD_DIM), LOW),
            pltpu.VMEM((S * J, HEAD_DIM, T), LOW),
        ],
        compiler_params=attn_params(S * J * T),
        cost_estimate=cost(36 * 10**9, 4 * MIB),
        name="attn_fwd",
    )(meta, seq, q, *ks, *vs)


def attn_bwd(meta, seq, q, ks, vs, o, lse, do, bq=512, bk=512):
    J, _, T = q.shape
    S = len(ks)
    block = pltpu.HBM((J, HEAD_DIM, T), LOW)
    out = pl.pallas_call(
        functools.partial(bwd_kernel, bq, bk, S),
        out_shape=[block] * (1 + 2 * S),
        in_specs=[M, M] + [V] * (4 + 2 * S),
        out_specs=[pl.BlockSpec()] * (1 + 2 * S),
        scratch_shapes=[
            pltpu.VMEM((S * J, T, HEAD_DIM), LOW),
            pltpu.VMEM((S * J, HEAD_DIM, T), LOW),
            pltpu.VMEM((S * J, T, HEAD_DIM), LOW),
            pltpu.VMEM((S * J, HEAD_DIM, T), F32),
            pltpu.VMEM((S * J, HEAD_DIM, T), F32),
        ],
        compiler_params=attn_params(S * J * T),
        cost_estimate=cost(10**6, 1000),
        name="attn_bwd",
    )(meta, seq, q, *ks, *vs, o, lse, do)
    return out[0], out[1 : 1 + S], out[1 + S :]


def qkv_kernel(x_ref, gain_ref, bias_ref, w_ref, b_ref, n_ref, q_ref, k_ref, v_ref):
    J = q_ref.shape[0]
    normed = norm_rows(x_ref[...].astype(F32), gain_ref[...], bias_ref[...]).astype(LOW)
    n_ref[...] = normed
    rows = normed.shape[0]
    for i, ref in ((1, k_ref), (2, v_ref), (0, q_ref)):
        made = dotf(normed, w_ref[i], NN)
        if i != 1:
            made = made + b_ref[i // 2][None]
        made = made.astype(LOW)
        if i == 0:
            made = (made * 0.125).astype(LOW)
        ref[...] = made.T.reshape(J, HEAD_DIM, rows)


def qkv(x, gain, bias, w, b):
    T, D = x.shape
    local = w.shape[2]
    J = local // HEAD_DIM
    rows = 256
    row_spec = pl.BlockSpec((rows, D), lambda i: (i, 0))
    head_spec = pl.BlockSpec((J, HEAD_DIM, rows), lambda i: (0, 0, i))
    heads = jax.ShapeDtypeStruct((J, HEAD_DIM, T), LOW)
    return pl.pallas_call(
        qkv_kernel,
        grid=(T // rows,),
        out_shape=(pltpu.HBM((T, D), LOW), heads, heads, heads),
        in_specs=[row_spec, V, V, V, V],
        out_specs=(row_spec, head_spec, head_spec, head_spec),
        compiler_params=pltpu.CompilerParams(vmem_limit_bytes=12 * MIB),
        cost_estimate=cost(6 * T * D * local, 8 * MIB),
        name="norm_qkv",
    )(far(x), far(gain[None]), far(bias[None]), far(w), far(b))


def out_kernel(pos_ref, *refs):
    pieces = refs[:8]
    w_ref, x_ref, b_ref, gain_ref, bias_ref, x1_ref, n2_ref, held = refs[8:]
    i = pl.program_id(0)
    rows = x1_ref.shape[0]

    @pl.when(i == 0)
    def _():
        for r, piece in enumerate(pieces):
            half = piece.shape[1]
            held[pos_ref[r % 4], :, r // 4 * half : (r // 4 + 1) * half] = piece[...]

    lanes = pl.ds(pl.multiple_of(i * rows, rows), rows)
    o = held[:, :, lanes].reshape(-1, rows)
    middle = x_ref[...].astype(F32) + dotf(o, w_ref[...], TN) + b_ref[...]
    x1_ref[...] = middle
    n2_ref[...] = norm_rows(middle, gain_ref[...], bias_ref[...]).astype(LOW)


def out_stage(pos, pieces, w, x, b, gain, bias):
    T, D = x.shape
    local = pieces[0].shape[0]
    rows = 256
    row_spec = pl.BlockSpec((rows, D), lambda i: (i, 0))
    return pl.pallas_call(
        out_kernel,
        grid=(T // rows,),
        out_shape=(pltpu.HBM((T, D), F32), jax.ShapeDtypeStruct((T, D), LOW)),
        in_specs=[M] + [V] * 9 + [row_spec, V, V, V],
        out_specs=(row_spec, row_spec),
        scratch_shapes=[pltpu.VMEM((4, local, T), LOW)],
        compiler_params=pltpu.CompilerParams(vmem_limit_bytes=16 * MIB),
        cost_estimate=cost(2 * T * D * 4 * local, 12 * MIB),
        name="out_norm",
    )(pos, *pieces, far(w), far(x), far(b[None]), far(gain[None]), far(bias[None]))


def mlp_kernel(at_ref, n2_ref, dm_ref, wf_ref, wp_ref, b_ref, *refs):
    g_ref, dh_ref, dn2_ref, db_ref = refs[-4:]
    hidden = dotf(n2_ref[...], wf_ref[...], NN) + b_ref[...]
    back = dotf(dm_ref[...], wp_ref[...], NT)
    root = math.sqrt(2.0 / math.pi)
    square = hidden * hidden
    bent = jnp.tanh(root * hidden * (1.0 + 0.044715 * square))
    half = 0.5 * (1.0 + bent)
    g_ref[...] = (hidden * half).astype(LOW)
    slope = half + 0.5 * hidden * (1.0 - bent * bent) * (root * (1.0 + 3 * 0.044715 * square))
    dh = (back * slope).astype(LOW)
    dh_ref[...] = dh
    dn2_ref[...] = dotf(dh, wf_ref[...], NT).astype(LOW)

    @pl.when(pl.program_id(0) == 0)
    def _():
        db_ref[...] = jnp.zeros_like(db_ref)

    db_ref[...] += jnp.sum(dh.astype(F32), axis=0, keepdims=True)


def mlp_stage(at, n2, dm, w_fc, w_proj, b_fc, before=()):
    T, D = n2.shape
    F = w_fc.shape[1]
    rows = 256
    steps = T // 2 // rows
    row_spec = pl.BlockSpec((rows, D), lambda i, at: (at[0] * steps + i, 0))
    hid_spec = pl.BlockSpec((rows, F), lambda i, at: (at[0] * steps + i, 0))
    own_spec = pl.BlockSpec((rows, D), lambda i, at: (i, 0))
    whole = pl.BlockSpec(memory_space=pltpu.VMEM)
    return pl.pallas_call(
        mlp_kernel,
        grid_spec=pltpu.PrefetchScalarGridSpec(
            num_scalar_prefetch=1,
            grid=(steps,),
            in_specs=[row_spec, row_spec, whole, whole, whole]
            + [pl.BlockSpec(memory_space=pl.ANY)] * len(before),
            out_specs=(hid_spec, hid_spec, own_spec, whole),
        ),
        out_shape=(
            jax.ShapeDtypeStruct((T, F), LOW),
            jax.ShapeDtypeStruct((T, F), LOW),
            pltpu.HBM((T // 2, D), LOW),
            jax.ShapeDtypeStruct((1, F), F32),
        ),
        input_output_aliases={6 + i: i for i in range(len(before))},
        compiler_params=pltpu.CompilerParams(vmem_limit_bytes=18 * MIB),
        cost_estimate=cost(3 * T * D * F, 9 * MIB),
        name="feed",
    )(at, n2, dm, w_fc, w_proj, b_fc[None], *before)


def back_kernel(at_ref, own_ref, crossed_ref, x_ref, kept_ref, gain_ref, wide_ref, low_ref, sums_ref):
    grad = own_ref[...].astype(F32) + crossed_ref[...].astype(F32)
    values = x_ref[...].astype(F32)
    centred = values - jnp.mean(values, axis=-1, keepdims=True)
    factor = lax.rsqrt(jnp.mean(centred * centred, axis=-1, keepdims=True) + EPS)
    z = centred * factor
    u = grad * gain_ref[...]
    mean_u = jnp.mean(u, axis=-1, keepdims=True)
    mean_uz = jnp.mean(u * z, axis=-1, keepdims=True)
    made = kept_ref[...].astype(F32) + factor * (u - mean_u - z * mean_uz)
    wide_ref[...] = made
    low = made.astype(LOW)
    low_ref[...] = low

    @pl.when(pl.program_id(0) == 0)
    def _():
        sums_ref[...] = jnp.zeros_like(sums_ref)

    for i, part in enumerate((grad * z, grad, low.astype(F32), kept_ref[...].astype(F32))):
        sums_ref[i : i + 1, :] += jnp.sum(part, axis=0, keepdims=True)


def norm_back(at, own, crossed, x, kept, gain):
    half, D = own.shape
    rows = 256
    steps = half // rows
    spec = pl.BlockSpec((rows, D), lambda i, at: (i, 0))
    from_whole = pl.BlockSpec((rows, D), lambda i, at: (at[0] * steps + i, 0))
    whole = pl.BlockSpec(memory_space=pltpu.VMEM)
    return pl.pallas_call(
        back_kernel,
        grid_spec=pltpu.PrefetchScalarGridSpec(
            num_scalar_prefetch=1,
            grid=(steps,),
            in_specs=[spec, spec, from_whole, spec if kept.shape[0] == half else from_whole, whole],
            out_specs=(spec, spec, whole),
        ),
        out_shape=(
            pltpu.HBM((half, D), F32),
            jax.ShapeDtypeStruct((half, D), LOW),
            jax.ShapeDtypeStruct((4, D), F32),
        ),
        compiler_params=pltpu.CompilerParams(vmem_limit_bytes=12 * MIB),
        cost_estimate=cost(0, 14 * half * D),
        name="norm_back",
    )(at, own, crossed, far(x), kept, gain[None])


def first_kernel(core_ref, q_ref, k_ref, v_ref, w_ref, keep_ref, send_ref):
    half = keep_ref.shape[0]
    for out, at in ((send_ref, 1 - core_ref[0]), (keep_ref, core_ref[0])):
        lanes = pl.ds(pl.multiple_of(at * half, half), half)
        total = jnp.zeros(out.shape, F32)
        for i, ref in enumerate((q_ref, k_ref, v_ref)):
            total += dotf(ref[:, lanes].T, w_ref[i], NT)
        out[...] = total.astype(LOW)


def first_stage(core, q, k, v, w):
    local, T = q.shape
    D = w.shape[1]
    part = pltpu.HBM((T // 2, D), LOW)
    return pl.pallas_call(
        first_kernel,
        out_shape=(part, part),
        in_specs=[M, V, V, V, V],
        out_specs=(pl.BlockSpec(), pl.BlockSpec()),
        compiler_params=pltpu.CompilerParams(vmem_limit_bytes=10 * MIB),
        cost_estimate=cost(10**6, 1000),
        name="first_grad",
    )(core, q, k, v, w)


def feed_grads_kernel(g_ref, dm_ref, n2_ref, dh_ref, out_ref):
    steps = pl.num_programs(0) // 2
    rows = out_ref.shape[0]
    i = pl.program_id(0)
    lanes = pl.ds(pl.multiple_of(i % steps * rows, rows), rows)

    @pl.when(i < steps)
    def _():
        out_ref[...] = dotf(g_ref[:, lanes], dm_ref[...], TN).astype(LOW)

    @pl.when(i >= steps)
    def _():
        out_ref[...] = dotf(n2_ref[:, lanes], dh_ref[...], TN).astype(LOW)


def feed_grads(g, dm, n2, dh):
    T, F = g.shape
    D = dm.shape[1]
    rows = 256
    return pl.pallas_call(
        feed_grads_kernel,
        grid=((F + D) // rows,),
        out_shape=pltpu.HBM((F + D, D), LOW),
        in_specs=[V] * 4,
        out_specs=pl.BlockSpec((rows, D), lambda i: (i, 0)),
        compiler_params=pltpu.CompilerParams(vmem_limit_bytes=10 * MIB),
        cost_estimate=cost(4 * T * D * F, 12 * MIB),
        name="feed_grads",
    )(g, dm, n2, dh)


def do_kernel(core_ref, own_ref, other_ref, w_ref, one_ref, two_ref, do_ref, grad_ref):
    half = own_ref.shape[0]
    grad = jnp.zeros(grad_ref.shape, F32)
    for ref, at in ((own_ref, core_ref[0]), (other_ref, 1 - core_ref[0])):
        lanes = pl.ds(pl.multiple_of(at * half, half), half)
        do_ref[:, lanes] = dotf(w_ref[...], ref[...], NT).astype(LOW)
        o = jnp.where(at == 0, one_ref[...], two_ref[...])
        grad += dotf(o, ref[...], NN)
    grad_ref[...] = grad.astype(LOW)


def do_stage(core, own, other, w_out, home_one, home_two):
    local, D = w_out.shape
    T = 2 * home_one.shape[1]
    return pl.pallas_call(
        do_kernel,
        out_shape=(pltpu.HBM((local, T), LOW), pltpu.HBM((local, D), LOW)),
        in_specs=[M, V, V, V, V, V],
        out_specs=(pl.BlockSpec(), pl.BlockSpec()),
        compiler_params=pltpu.CompilerParams(vmem_limit_bytes=8 * MIB),
        cost_estimate=cost(4 * T * D * local, 5 * MIB),
        name="heads_grad",
    )(core, own, other, w_out, home_one, home_two)


def grad_kernel(share, spot_ref, dq_ref, dk_ref, dv_ref, own_ref, *refs):
    parts, out_ref = refs[:-1], refs[-1]
    J = dq_ref.shape[0]
    for i, ref in enumerate((dq_ref, dk_ref, dv_ref)):
        total = dotf(ref[spot_ref[4]], own_ref[...], NN)
        for r, part in enumerate(parts):
            lanes = pl.ds(pl.multiple_of(spot_ref[r], share), share)
            for s in range(1, J):
                total += dotf(ref[spot_ref[4 + s], :, lanes], part[s - 1], NN)
        out_ref[i * HEAD_DIM : (i + 1) * HEAD_DIM] = total


def grad_heads(spots, dq, dk, dv, own, parts):
    J, _, T = dq.shape
    D = own.shape[1]
    return pl.pallas_call(
        functools.partial(grad_kernel, parts[0].shape[1]),
        out_shape=jax.ShapeDtypeStruct((3 * HEAD_DIM, D), F32),
        in_specs=[M] + [V] * (4 + len(parts)),
        out_specs=V,
        compiler_params=pltpu.CompilerParams(vmem_limit_bytes=12 * MIB),
        cost_estimate=cost(10**6, 1000),
        name="grad_heads",
    )(spots, dq, dk, dv, own, *parts)


def lay_kernel(S, spot_ref, *refs):
    parts, (qkv_ref, out_ref, held) = refs[:-3], refs[-3:]
    J, depth, _ = held.shape
    wide = parts[0].shape[1]
    few = (parts[0].shape[0] - depth) // S
    for i, part in enumerate(parts):
        jj, gg = spot_ref[2 * i], spot_ref[2 * i + 1]
        held[jj, :, pl.ds(pl.multiple_of(gg * wide, wide), wide)] = part[:depth]
        rest = part[depth:].astype(F32)
        rows = pl.ds(pl.multiple_of((jj * S + gg) * few, few), few)
        for e in range(S):
            out_ref[rows, e * wide : (e + 1) * wide] = rest[e * few : (e + 1) * few]
    for k in range(3):
        rows = [held[h, k * HEAD_DIM : (k + 1) * HEAD_DIM, :] for h in range(J)]
        qkv_ref[k] = jnp.concatenate(rows, 0).astype(F32).T


def lay_blocks(found, J, S):
    parts = [part for _, _, part in found]
    wide = parts[0].shape[1]
    spots = jnp.stack([x for jj, gg, _ in found for x in (jj, gg)]).astype(jnp.int32)
    return pl.pallas_call(
        functools.partial(lay_kernel, S),
        out_shape=(
            jax.ShapeDtypeStruct((3, S * wide, J * HEAD_DIM), F32),
            jax.ShapeDtypeStruct((J * HEAD_DIM, S * wide), F32),
        ),
        in_specs=[M] + [V] * len(parts),
        out_specs=(V, V),
        scratch_shapes=[pltpu.VMEM((J, 3 * HEAD_DIM, S * wide), LOW)],
        compiler_params=pltpu.CompilerParams(vmem_limit_bytes=12 * MIB),
        cost_estimate=cost(0, 6 * MIB),
        name="lay_blocks",
    )(spots, *parts)


def add_kernel(own_ref, other_ref, out_ref):
    out_ref[...] = (own_ref[...].astype(F32) + other_ref[...].astype(F32)).astype(LOW)


def add_low(own, other):
    return pl.pallas_call(
        add_kernel,
        out_shape=jax.ShapeDtypeStruct(own.shape, LOW),
        in_specs=[V, V],
        out_specs=V,
        compiler_params=pltpu.CompilerParams(vmem_limit_bytes=6 * MIB),
        cost_estimate=cost(0, 6 * own.size),
        name="add_low",
    )(own, other)


def feed_out_kernel(core_ref, g_ref, w_ref, kept_ref, sent_ref):
    half = kept_ref.shape[0]
    for out, at in ((sent_ref, 1 - core_ref[0]), (kept_ref, core_ref[0])):
        rows = pl.ds(pl.multiple_of(at * half, half), half)
        out[...] = dotf(g_ref[rows, :], w_ref[...], NN).astype(LOW)


def feed_out(core, g, w):
    T, F = g.shape
    D = w.shape[1]
    part = jax.ShapeDtypeStruct((T // 2, D), LOW)
    return pl.pallas_call(
        feed_out_kernel,
        out_shape=(part, part),
        in_specs=[M, V, V],
        out_specs=(V, V),
        compiler_params=pltpu.CompilerParams(vmem_limit_bytes=8 * MIB),
        cost_estimate=cost(2 * T * F * D, 6 * MIB),
        name="feed_out",
    )(core, g, w)


def widen_kernel(low_ref, first_ref, second_ref):
    steps = pl.num_programs(0) // 2

    @pl.when(pl.program_id(0) < steps)
    def _():
        first_ref[...] = low_ref[...].astype(F32)

    @pl.when(pl.program_id(0) >= steps)
    def _():
        second_ref[...] = low_ref[...].astype(F32)


def widen(low, first):
    rows, D = low.shape
    steps = 4
    block = first // steps
    return pl.pallas_call(
        widen_kernel,
        grid=(2 * steps,),
        out_shape=(jax.ShapeDtypeStruct((first, D), F32), jax.ShapeDtypeStruct((rows - first, D), F32)),
        in_specs=[pl.BlockSpec((block, D), lambda i: (i, 0))],
        out_specs=(
            pl.BlockSpec((block, D), lambda i: (jnp.minimum(i, steps - 1), 0)),
            pl.BlockSpec((block, D), lambda i: (jnp.maximum(i - steps, 0), 0)),
        ),
        compiler_params=pltpu.CompilerParams(vmem_limit_bytes=8 * MIB),
        cost_estimate=cost(0, 12 * MIB),
        name="widen",
    )(low)


def pair_kernel(core_ref, own_ref, other_ref, out_ref):
    half = own_ref.shape[0]
    for ref, at in ((own_ref, core_ref[0]), (other_ref, 1 - core_ref[0])):
        out_ref[pl.ds(pl.multiple_of(at * half, half), half), :] = ref[...]


def lay_pair(core, own, other):
    half, D = own.shape
    return pl.pallas_call(
        pair_kernel,
        out_shape=jax.ShapeDtypeStruct((2 * half, D), own.dtype),
        in_specs=[M, V, V],
        out_specs=V,
        compiler_params=pltpu.CompilerParams(vmem_limit_bytes=6 * MIB),
        cost_estimate=cost(0, 8 * half * D),
        name="lay_pair",
    )(core, own, other)


def shift_dp(value, steps):
    count = lax.axis_size("dp")
    return lax.ppermute(value, "dp", [(i, (i + steps) % count) for i in range(count)])


def shift_group(value, steps, S):
    count = lax.axis_size("dp")
    return lax.ppermute(
        value, "dp", [(i, i // S * S + (i % S + steps) % S) for i in range(count)]
    )


def swap_core(value):
    return lax.ppermute(value, "tensor", [(i, i ^ 1) for i in range(lax.axis_size("tensor"))])


def swap_x(value):
    return lax.ppermute(value, "tensor", [(i, i ^ 2) for i in range(lax.axis_size("tensor"))])


def rows_at(value, start, count):
    return lax.dynamic_slice_in_dim(value, start, count, 0)


def pick(value, index):
    return lax.dynamic_index_in_dim(value, index, 0, keepdims=False)


def gate(value, *before):
    return lax.optimization_barrier((value, *before))[0]


def tied(*values):
    return lax.optimization_barrier(values)


def sum_group(parts, g, S):
    total = pick(parts, g).astype(F32)
    for e in range(1, S):
        total = total + shift_group(pick(parts, (g + e) % S).astype(LOW), e, S).astype(F32)
    return total


def spread_blocks(blocks, j, g, S):
    J = len(blocks)
    found = []
    for s, part in enumerate(blocks):
        found.append(((j - s) % J, g, part))
        for e in range(1, S):
            found.append(((j - s) % J, (g - e) % S, shift_group(part, e, S)))
    return found


def per_device(
    block_input,
    output_grad,
    seq_lengths,
    ln1_gain,
    ln1_bias,
    w_qkv,
    b_qv,
    w_out,
    b_out,
    ln2_gain,
    ln2_bias,
    w_fc,
    b_fc,
    w_proj,
    b_proj,
):
    T, D = block_input.shape
    local = w_qkv.shape[2]
    J = local // HEAD_DIM
    count = lax.axis_size("dp")
    S = count // J
    place = lax.axis_index("dp")
    j, g = place // S, place % S
    tensor = lax.axis_index("tensor")
    core, side = tensor % 2, tensor // 2
    half, share = T // 2, T // 4
    core_at = core[None].astype(jnp.int32)
    meta = g[None].astype(jnp.int32)
    groups = [[S * jj + gg for jj in range(J)] for gg in range(S)]

    def exchange(heads):
        return lax.all_to_all(heads, "dp", 0, 0, tiled=True, axis_index_groups=groups)

    def group(value):
        return [value] + [shift_group(value, e, S) for e in range(1, S)]

    first_low, queries, keys, values = qkv(block_input, ln1_gain, ln1_bias, w_qkv, b_qv)
    k_own, across = tied(exchange(keys), swap_x(w_out))
    ks = group(k_own)
    vs = group(gate(exchange(values), *ks[1:]))
    q_all = exchange(queries)

    pieces = jnp.stack([w_out, swap_core(w_out), across, swap_core(across)])
    order = jnp.stack([tensor ^ r for r in range(4)]).astype(jnp.int32)
    w_out_all = jnp.concatenate([pick(pieces, tensor ^ r) for r in range(4)], 0)

    q_all = gate(q_all, w_out_all)
    o_one, lse_one = attn_fwd(meta, seq_lengths, q_all, ks, vs, 0)
    o_two, lse_two = attn_fwd(meta, seq_lengths, gate(q_all, o_one), ks, vs, 1)
    home_one, o_two = tied(exchange(o_one), o_two)
    home_one = home_one.reshape(local, half)
    home_two, across = tied(exchange(o_two), swap_x(home_one))
    home_two = home_two.reshape(local, half)

    own_quarter = rows_at(first_low, core * half + side * share, share)
    own_quarter = rows_at(first_low, core * half + side * share, share)
    own_quarter = gate(own_quarter, home_two)
    norm_own = lax.all_gather(own_quarter, "dp", axis_index_groups=groups)

    def gather_tensor(value, across):
        return value, swap_core(value), across, swap_core(across)

    o_pieces = gather_tensor(home_one, across) + gather_tensor(home_two, swap_x(home_two))
    middle, second_low = out_stage(order, o_pieces, w_out_all, block_input, b_out, ln2_gain, ln2_bias)
    active_low, hidden_grad, sent, bias_one = mlp_stage(
        1 - core_at, second_low, output_grad, w_fc, w_proj, b_fc
    )
    arrived = swap_core(sent)
    active_low, hidden_grad, kept, bias_two = mlp_stage(
        core_at, second_low, output_grad, w_fc, w_proj, b_fc, (active_low, hidden_grad)
    )
    grad_b_fc = bias_one + bias_two
    second_half = add_low(kept, arrived)
    crossed = swap_x(second_half)
    grad_feed = feed_grads(active_low, output_grad, second_low, hidden_grad)
    feed_part = lax.psum_scatter(grad_feed, "dp", scatter_dimension=0, tiled=True)
    feed_kept, feed_sent = feed_out(core_at, active_low, w_proj)
    rolled = jnp.stack([pick(norm_own, (j + s) % J) for s in range(1, J)])
    crossed = gate(crossed, grad_feed, rolled, feed_kept)
    middle_grad, branch_half, sums_two = norm_back(
        core_at, second_half, crossed, middle, output_grad, ln2_gain
    )
    heads_grad, grad_w_out = do_stage(core_at, branch_half, swap_core(branch_half), w_out, home_one, home_two)
    do_all = exchange(heads_grad.reshape(J, HEAD_DIM, T))
    out_parts = lax.all_to_all(grad_w_out.reshape(count, local // count, D), "dp", 0, 0, tiled=True)

    norm_across = swap_x(gate(rolled, branch_half))

    o_all = jnp.concatenate([o_one, o_two], 2)
    lse = jnp.concatenate([lse_one, lse_two], 2)
    dq, dks, dvs = attn_bwd(meta, seq_lengths, q_all, ks, vs, o_all, lse, do_all)
    dq, dks, dvs, norm_across, out_parts = tied(dq, dks, dvs, norm_across, out_parts)

    norm_parts = [rolled, norm_across, swap_core(rolled), swap_core(norm_across)]

    def regroup(parts):
        return [shift_group(part, -e, S) for e, part in enumerate(parts) if e]

    def total(own, moved):
        for part in moved:
            own = add_low(own, part)
        return own

    q_home, dk_moved = tied(exchange(dq), regroup(dks))
    dk = total(dks[0], dk_moved)
    k_home, dv_moved = tied(exchange(gate(dk, q_home)), regroup(dvs))
    dv = total(dvs[0], dv_moved)
    v_home = exchange(gate(dv, k_home))
    feed_own = add_low(feed_kept, swap_core(gate(feed_sent, q_home)))
    feed_across = swap_x(feed_own)
    q_home, k_home, v_home = (x.reshape(local, T) for x in (q_home, k_home, v_home))

    spots = jnp.stack(
        [
            c * half + d * share
            for c, d in ((core, side), (core, 1 - side), (1 - core, side), (1 - core, 1 - side))
        ]
        + [(j + s) % J for s in range(J)]
    ).astype(jnp.int32)
    head_grad = grad_heads(spots, dq, dk, dv, first_low, norm_parts)
    v_home, head_grad, feed_across, feed_part = tied(v_home, head_grad, feed_across, feed_part)
    grad_feed = lax.all_gather(feed_part, "dp", axis=0, tiled=True)
    kept, sent = first_stage(core_at, q_home, k_home, v_home, w_qkv)
    first_half = add_low(kept, swap_core(sent))
    cut = head_grad.reshape(3 * HEAD_DIM, S, D // S).transpose(1, 0, 2)
    head_grad = sum_group(cut, g, S).astype(LOW)
    grad_w_out = jnp.sum(out_parts.astype(F32), axis=0).astype(LOW)
    block = jnp.concatenate([head_grad] + jnp.split(grad_w_out, S, axis=1), 0)
    blocks = [shift_dp(block, s * S) for s in range(1, J)]

    first_across = gate(swap_x(first_half), *blocks)
    _, input_half, sums_one = norm_back(
        core_at, first_half, first_across, block_input, middle_grad, ln1_gain
    )
    input_grad = lay_pair(core_at, input_half, swap_core(input_half))

    feed_across = gate(feed_across, block)
    feed_sum = feed_own.astype(F32) + feed_across.astype(F32)
    middle_half = rows_at(middle, core * half, half)
    output_half = (middle_half + (feed_sum + b_proj)).astype(LOW)
    block_output = lay_pair(core_at, output_half, swap_core(output_half))

    hidden_width = grad_b_fc.shape[1]
    wide_fc = lax.dynamic_update_slice_in_dim(
        jnp.zeros((1, hidden_width * lax.axis_size("tensor")), F32),
        grad_b_fc,
        tensor * hidden_width,
        1,
    ).reshape(-1, D)
    bias_qv = jnp.stack([jnp.sum(q_home.astype(F32), axis=1), jnp.sum(v_home.astype(F32), axis=1)])
    wide_qv = lax.dynamic_update_slice_in_dim(jnp.zeros((2, D), F32), bias_qv, tensor * local, 1)
    early = jnp.concatenate([wide_fc, wide_qv], 0)
    early = early + swap_x(early)
    small = jnp.concatenate([sums_two, sums_one[:2], early], 0)
    small = small + swap_core(small)
    step = 1
    while step < count:
        small = small + lax.ppermute(small, "dp", [(i, i ^ step) for i in range(count)])
        if step == 2:
            small, input_grad, block_output = tied(small, input_grad, block_output)
        step *= 2
    found = spread_blocks([block, *blocks], j, g, S)
    grad_w_proj, grad_w_fc = widen(grad_feed, w_proj.shape[0])
    grad_w_qkv, grad_w_out = lay_blocks(found, J, S)
    tail = small.shape[0] - 2
    grad_b_qv = lax.dynamic_slice_in_dim(small[tail:], tensor * local, local, 1)
    grad_b_fc = rows_at(small[6:tail].reshape(-1), tensor * hidden_width, hidden_width)
    return (
        block_output,
        input_grad,
        small[4],
        small[5],
        grad_w_qkv,
        grad_b_qv,
        grad_w_out,
        small[2],
        small[0],
        small[1],
        grad_w_fc,
        grad_b_fc,
        grad_w_proj,
        small[3],
    )


def solution(mesh):
    placed = (
        P("dp", None),
        P("dp", None),
        P(),
        P(),
        P(),
        P(None, None, "tensor"),
        P(None, "tensor"),
        P("tensor", None),
        P(),
        P(),
        P(),
        P(None, "tensor"),
        P("tensor"),
        P("tensor", None),
        P(),
    )
    return jax.shard_map(
        per_device,
        mesh=mesh,
        in_specs=placed,
        out_specs=(
            P("dp", None),
            P("dp", None),
            P(),
            P(),
            P(None, None, "tensor"),
            P(None, "tensor"),
            P("tensor", None),
            P(),
            P(),
            P(),
            P(None, "tensor"),
            P("tensor"),
            P("tensor", None),
            P(),
        ),
        check_vma=False,
    )
```
